32 devices in a mesh: dp: 16 (over z, y, x), cent: 2 (over core).
Axes of the slice: x: 2, y: 2, z: 4, core: 2. Of those that a mesh axis runs over, the one named last changes fastest.
Arguments:
- points: bfloat16 [16384, 256], P('dp'), may hold values from -8 to 8
- centroids: bfloat16 [8192, 256], P('cent'), may hold values from -0.5 to 0.5
Outputs:
- new_centroids: float32 [8192, 256], P('cent')
- counts: float32 [8192], P('cent')
- log_evidence: float32 [16384], P('dp')
The draws below stay inside these ranges and needn't reach their ends.
All inputs are finite; a program needn't handle non-finite values.
Results may differ from the reference program's by a relative error of at most 0.0016.
Values sent between devices are 32-bit elements; how exact they have to be, the bound alone decides.
No kernel may reach another device: no remote copies, remote signals or barrier semaphores. Data moves between devices by JAX's collectives and lax.ppermute only.
A program may use at most 64 MiB of HBM per device.

```python
import math
import jax
import jax.numpy as jnp
from jax import lax

D = 256
CENTROIDS = 8192
TOTAL_ROWS = 16384


def aligned_signs(key):
    signs = jax.random.bernoulli(jax.random.fold_in(key, 7001), 0.5, (D,))
    return jnp.where(signs, 1.0, -1.0).astype(jnp.float32)


def draw_points(key, part):
    first = jax.random.fold_in(key, 11)
    base = jax.random.truncated_normal(first, -6.0, 6.0, (TOTAL_ROWS, D))
    index = jnp.arange(TOTAL_ROWS)
    strength = jnp.array([5.0, 6.0, 8.0], jnp.float32)[index // 251 % 3]
    chosen = index % 251 == 7
    signs = aligned_signs(key)
    base = jnp.where(chosen[:, None], strength[:, None] * signs[None, :], base)
    return base.astype(jnp.float32).astype(jnp.bfloat16)


def draw_centroids(key, part):
    first = jax.random.fold_in(key, 21)
    base = jax.random.truncated_normal(first, -6.0, 6.0, (CENTROIDS, D)) / 16.0
    index = jnp.arange(CENTROIDS)
    signs = aligned_signs(key)
    leading = jnp.arange(D) == 0
    second = jnp.where(leading, 0.375, 0.5) * signs
    base = jnp.where((index % 509 == 5)[:, None], 0.5 * signs[None, :], base)
    base = jnp.where((index % 509 == 6)[:, None], second[None, :], base)
    return base.astype(jnp.float32).astype(jnp.bfloat16)


def setup_inputs(seed: int = 0) -> dict:
    key_of = jax.random.split(jax.random.key(seed), 3)
    points = draw_points(jax.random.fold_in(key_of[2], 71), 0)
    centroids = draw_centroids(jax.random.fold_in(key_of[2], 71), 0)
    return dict(points=points, centroids=centroids)


prior_mass = 0.5


def reference(points, centroids):
    cnorm = jnp.einsum("kd,kd->k", centroids, centroids, preferred_element_type=jnp.float32)
    block = min(512, TOTAL_ROWS)
    pieces = points.reshape(TOTAL_ROWS // block, block, D)

    def visit(carry, piece):
        sums, counts = carry
        score = 2.0 * jnp.dot(piece, centroids.T, preferred_element_type=jnp.float32) - cnorm[None, :]
        top = jnp.max(score, axis=1)
        weights = jnp.exp(score - top[:, None])
        total = jnp.sum(weights, axis=1)
        resp = (weights / total[:, None]).astype(jnp.bfloat16)
        sums = sums + jnp.dot(resp.T, piece, preferred_element_type=jnp.float32)
        counts = counts + jnp.sum(resp.astype(jnp.float32), axis=0)
        return (sums, counts), top + jnp.log(total) - math.log(CENTROIDS)

    start = (jnp.zeros((CENTROIDS, D), jnp.float32), jnp.zeros((CENTROIDS,), jnp.float32))
    (sums, counts), evidence = lax.scan(visit, start, pieces)
    new_centroids = (sums + prior_mass * centroids.astype(jnp.float32)) / (counts + prior_mass)[:, None]
    return new_centroids, counts, evidence.reshape(TOTAL_ROWS)
```

```python
import functools
import math

import jax
import jax.numpy as jnp
from jax import lax
from jax.experimental import pallas as pl
from jax.experimental.pallas import tpu as pltpu
from jax.sharding import PartitionSpec as P

prior_mass = 0.5
VMEM_LIMIT = 48 * 1024 * 1024
NT = (((1,), (1,)), ((), ()))
NN = (((1,), (0,)), ((), ()))


def call(kernel, out_shape, *args, name, scratch=(), flops=0):
    vmem = pl.BlockSpec(memory_space=pltpu.VMEM)
    return pl.pallas_call(
        kernel,
        out_shape=out_shape,
        in_specs=[vmem] * len(args),
        out_specs=jax.tree.map(lambda _: vmem, out_shape),
        scratch_shapes=list(scratch),
        compiler_params=pltpu.CompilerParams(vmem_limit_bytes=VMEM_LIMIT),
        cost_estimate=pl.CostEstimate(
            flops=flops,
            bytes_accessed=sum(a.size * a.dtype.itemsize for a in args),
            transcendentals=0,
        ),
        name=name,
    )(*args)


def f32(*shape):
    return jax.ShapeDtypeStruct(shape, jnp.float32)


def prepare_kernel(c_ref, twice_ref, norm_ref):
    c = c_ref[...].astype(jnp.float32)
    twice_ref[...] = (2.0 * c).astype(jnp.bfloat16)
    norm_ref[...] = jnp.broadcast_to(jnp.sum(c * c, axis=1, keepdims=True), norm_ref.shape)


def shifted(norm, width):
    return jnp.concatenate([norm] * (width // norm.shape[1]), axis=1) if width > norm.shape[1] else norm[:, :width]


def stats_kernel(count, twice_ref, norm_ref, *refs):
    x_refs, out_ref = refs[:count], refs[count]
    twice = twice_ref[...]
    for i, x_ref in enumerate(x_refs):
        rows = x_ref.shape[0]
        tile = min(256, rows)
        for start in range(0, rows, tile):
            x = x_ref[start : start + tile, :].astype(jnp.bfloat16)
            dots = lax.dot_general(twice, x, NT, preferred_element_type=jnp.float32)
            score = dots - shifted(norm_ref[...], tile)
            top = jnp.max(score, axis=0, keepdims=True)
            total = jnp.sum(jnp.exp(score - top), axis=0, keepdims=True)
            out_ref[0, i : i + 1, start : start + tile] = top
            out_ref[1, i : i + 1, start : start + tile] = total


def stats(twice, norm, blocks):
    rows = blocks[0].shape[0]
    flops = 2 * twice.shape[0] * twice.shape[1] * rows * len(blocks)
    return call(
        functools.partial(stats_kernel, len(blocks)),
        f32(2, len(blocks), rows),
        twice,
        norm,
        *blocks,
        name="stats",
        flops=flops,
    )


def sums_kernel(count, lines, twice_ref, norm_ref, *refs):
    x_refs = refs[:count]
    st_refs = refs[count : 2 * count]
    out_ref, lse_ref, acc_ref, cnt_ref = refs[2 * count :]
    local, width = twice_ref.shape
    for b in range(count):
        tops = [st_refs[s][0, b ^ s : (b ^ s) + 1, :] for s in range(count)]
        totals = [st_refs[s][1, b ^ s : (b ^ s) + 1, :] for s in range(count)]
        top = functools.reduce(jnp.maximum, tops)
        total = functools.reduce(jnp.add, [t * jnp.exp(m - top) for m, t in zip(tops, totals)])
        lse_ref[b : b + 1, :] = top + jnp.log(total)
    twice = twice_ref[...]
    first = True
    for b in range(count):
        rows = x_refs[b].shape[0]
        tile = min(256, rows)
        for start in range(0, rows, tile):
            x = x_refs[b][start : start + tile, :].astype(jnp.bfloat16)
            dots = lax.dot_general(twice, x, NT, preferred_element_type=jnp.float32)
            score = dots - shifted(norm_ref[...], tile)
            resp = jnp.exp(score - lse_ref[b : b + 1, start : start + tile]).astype(jnp.bfloat16)
            part = lax.dot_general(resp, x, NN, preferred_element_type=jnp.float32)
            wide = resp.astype(jnp.float32)
            lanes = min(128, tile)
            counted = functools.reduce(
                jnp.add, [wide[:, k : k + lanes] for k in range(0, tile, lanes)]
            )
            if first:
                acc_ref[...] = part
                cnt_ref[...] = counted
                first = False
            else:
                acc_ref[...] += part
                cnt_ref[...] += counted
    size = local // lines
    for l in range(lines):
        out_ref[l, 0:size, :] = acc_ref[l * size : (l + 1) * size, :]
        turned = jnp.sum(cnt_ref[l * size : (l + 1) * size, :].T, axis=0, keepdims=True)
        if size < width:
            turned = jnp.concatenate([turned, jnp.zeros((1, width - size), jnp.float32)], axis=1)
        out_ref[l, size : size + 8, :] = jnp.broadcast_to(turned, (8, width))


def finish_kernel(mine_ref, left_ref, right_ref, c_ref, out_ref):
    size, width = c_ref.shape
    total = mine_ref[...] + left_ref[...] + right_ref[...]
    counts = total[size:, :]
    column = counts.T[:size, 0:1]
    new = (total[:size, :] + prior_mass * c_ref[...].astype(jnp.float32)) / (column + prior_mass)
    out_ref[0:size, :] = new
    out_ref[size:, :] = counts


def body(n, cores, points, centroids):
    rows, width = points.shape
    local_cent = centroids.shape[0]
    lines = n // 4
    me = lax.axis_index("dp")
    core = lax.axis_index("cent")
    plane = lax.rem(me, 4)
    line = lax.div(me, 4)
    block = rows // cores
    share = local_cent // 4
    size = share // lines

    def flip_dp(x, bits):
        return lax.ppermute(x, "dp", [(i, i ^ bits) for i in range(n)])

    def flip_core(x, bits):
        return lax.ppermute(x, "cent", [(i, i ^ bits) for i in range(cores)])

    def up(x, last):
        return lax.ppermute(x, "dp", [(i, i + 4) for i in range(4 * min(last, lines - 1))])

    def down(x, last):
        return lax.ppermute(
            x, "dp", [(i, i - 4) for i in range(n - 4 * min(last, lines - 1), n)]
        )

    blocks = [None] * (4 * cores)
    for rc in range(cores):
        blocks[rc] = lax.dynamic_slice_in_dim(points, (core ^ rc) * block, block, axis=0)
    own = blocks[0].astype(jnp.float32)
    near = [flip_dp(own, 1), flip_dp(own, 2)]
    half = block // 2
    far = [flip_dp(near[0][:half], 2), flip_dp(near[1][half:], 1)]
    blocks[cores] = near[0]
    blocks[2 * cores] = near[1]
    blocks[3 * cores] = jnp.concatenate(far, axis=0)
    for k in (1, 2, 3):
        for rc in range(1, cores):
            blocks[k * cores + rc] = flip_core(blocks[k * cores], rc)

    mine = lax.dynamic_slice_in_dim(centroids, plane * share, share, axis=0)
    twice, norm = call(
        prepare_kernel,
        (jax.ShapeDtypeStruct((share, width), jnp.bfloat16), f32(share, 128)),
        mine,
        name="prepare",
    )
    parts = [stats(twice, norm, blocks[k * cores : (k + 1) * cores]) for k in range(4)]
    own_stats = jnp.concatenate(parts, axis=1)
    all_stats = [own_stats]
    for s in range(1, 4 * cores):
        perm = [(i, i ^ s) if cores == 1 else (i, (((i // cores) ^ (s // cores)) * cores) + ((i % cores) ^ (s % cores))) for i in range(n * cores)]
        all_stats.append(lax.ppermute(own_stats, ("dp", "cent"), perm))

    payload, lse = call(
        functools.partial(sums_kernel, 4 * cores, lines),
        (f32(lines, size + 8, width), f32(4 * cores, block)),
        twice,
        norm,
        *blocks,
        *all_stats,
        name="sums",
        scratch=[
            pltpu.VMEM((share, width), jnp.float32),
            pltpu.VMEM((share, min(128, block)), jnp.float32),
        ],
        flops=4 * share * width * 4 * rows,
    )
    own_lse = [lax.dynamic_index_in_dim(lse, core ^ rc, axis=0, keepdims=False) for rc in range(cores)]
    log_evidence = jnp.concatenate(own_lse, axis=0) - math.log(local_cent * cores)

    def pick(place):
        return lax.dynamic_index_in_dim(payload, jnp.clip(place, 0, lines - 1), axis=0, keepdims=False)

    from_left = from_right = None
    for t in range(1, lines):
        send_up = pick(line + lines - t)
        send_down = pick(line - lines + t)
        if t > 1:
            send_up = send_up + from_left
            send_down = send_down + from_right
        from_left, from_right = up(send_up, t), down(send_down, t)
    own_cent = lax.dynamic_slice_in_dim(mine, line * size, size, axis=0)
    done = call(
        finish_kernel,
        f32(size + 8, width),
        pick(line),
        from_left,
        from_right,
        own_cent,
        name="finish",
    )

    lefts, rights = [done], [done]
    for t in range(1, lines):
        lefts.append(lax.ppermute(lefts[-1], "dp", [(i, i + 4) for i in range(4 * (t - 1), n - 4)]))
        rights.append(lax.ppermute(rights[-1], "dp", [(i, i - 4) for i in range(4, n - 4 * (t - 1))]))
    order = [sorted(range(lines), key=lambda l: (abs(l - z), (l - z) % 2 if z % 2 else l, l)) for z in range(lines)]
    order = [[z] + sorted([l for l in range(lines) if l != z], key=lambda l: (abs(l - z), l != z ^ 1)) for z in range(lines)]
    table = jnp.array(order, jnp.int32)
    column = [done]
    for k in range(1, lines):
        column.append(
            lax.select_n(
                line,
                *[
                    lefts[z - order[z][k]] if order[z][k] < z else rights[order[z][k] - z]
                    for z in range(lines)
                ],
            )
        )
    over_x = [flip_dp(b, 1) for b in column]
    over_y = [flip_dp(b, 2) for b in column]
    cut = lines // 2
    over_xy = [flip_dp(b, 2) for b in over_x[:cut]] + [flip_dp(b, 1) for b in over_y[cut:]]

    new = jnp.zeros((4 * lines * size, width), jnp.float32)
    counts = jnp.zeros((4 * lines, size), jnp.float32)
    for k in range(lines):
        at = lax.dynamic_index_in_dim(lax.dynamic_index_in_dim(table, line, 0, False), k, 0, False)
        for bits, group in enumerate((column, over_x, over_y, over_xy)):
            place = (plane ^ bits) * lines + at
            new = lax.dynamic_update_slice_in_dim(new, group[k][:size], place * size, axis=0)
            counts = lax.dynamic_update_slice_in_dim(counts, group[k][size : size + 1, :size], place, axis=0)
    return new, counts.reshape(-1), log_evidence


def solution(mesh):
    n, cores = mesh.shape["dp"], mesh.shape["cent"]
    return jax.shard_map(
        functools.partial(body, n, cores),
        mesh=mesh,
        in_specs=(P("dp", None), P("cent", None)),
        out_specs=(P("cent", None), P("cent"), P("dp")),
        check_vma=False,
    )
```

```python
import functools
import math

import jax
import jax.numpy as jnp
from jax import lax
from jax.experimental import pallas as pl
from jax.experimental.pallas import tpu as pltpu
from jax.sharding import PartitionSpec as P

prior_mass = 0.5
VMEM_LIMIT = 48 * 1024 * 1024
LANES = 128
NT = (((1,), (1,)), ((), ()))
NN = (((1,), (0,)), ((), ()))
VMEM = pl.BlockSpec(memory_space=pltpu.VMEM)
SMEM = pl.BlockSpec(memory_space=pltpu.SMEM)
ANY = pl.BlockSpec(memory_space=pl.ANY)


def f32(*shape):
    return jax.ShapeDtypeStruct(shape, jnp.float32)


def call(kernel, out_shape, in_specs, args, name, out_specs=None, scratch=(), flops=0, aliases={}):
    return pl.pallas_call(
        kernel,
        out_shape=out_shape,
        in_specs=in_specs,
        out_specs=jax.tree.map(lambda _: VMEM, out_shape) if out_specs is None else out_specs,
        scratch_shapes=list(scratch),
        input_output_aliases=aliases,
        compiler_params=pltpu.CompilerParams(vmem_limit_bytes=VMEM_LIMIT),
        cost_estimate=pl.CostEstimate(
            flops=flops,
            bytes_accessed=sum(a.size * a.dtype.itemsize for a in args),
            transcendentals=0,
        ),
        name=name,
    )(*args)


def open_kernel(where_ref, points_ref, first_ref, second_ref):
    half = first_ref.shape[0]
    start = pl.multiple_of(where_ref[1] * (2 * half), 2 * half)
    first_ref[...] = points_ref[pl.ds(start, half), :].astype(jnp.float32)
    second_ref[...] = points_ref[pl.ds(pl.multiple_of(start + half, half), half), :].astype(jnp.float32)


def widen(norm, width):
    if width <= norm.shape[1]:
        return norm[:, :width]
    return jnp.concatenate([norm] * (width // norm.shape[1]), axis=1)


def norms(c):
    c = c.astype(jnp.float32)
    return jnp.broadcast_to(jnp.sum(c * c, axis=1, keepdims=True), (c.shape[0], LANES))


def stats_kernel(points_ref, c_ref, out_ref, norm_ref):
    rows, local = points_ref.shape[0], c_ref.shape[0]
    tile, chunk = min(256, rows), min(1024, local)
    for part in range(0, local, chunk):
        c = c_ref[part : part + chunk, :]
        norm_ref[...] = norms(c)
        twice = c + c
        for start in range(0, rows, tile):
            at = slice(start, start + tile)
            dots = lax.dot_general(twice, points_ref[at, :], NT, preferred_element_type=jnp.float32)
            score = dots - widen(norm_ref[...], tile)
            top = jnp.max(score, axis=0, keepdims=True)
            total = jnp.sum(jnp.exp(score - top), axis=0, keepdims=True)
            if part:
                old_top, old_total = out_ref[0:1, at], out_ref[1:2, at]
                new_top = jnp.maximum(old_top, top)
                total = old_total * jnp.exp(old_top - new_top) + total * jnp.exp(top - new_top)
                top = new_top
            out_ref[0:1, at] = top
            out_ref[1:2, at] = total


def add_block(twice, norm, x, lse, acc_ref, cnt_ref, first):
    dots = lax.dot_general(twice, x, NT, preferred_element_type=jnp.float32)
    score = dots - widen(norm, x.shape[0])
    resp = jnp.exp(score - lse).astype(jnp.bfloat16)
    part = lax.dot_general(resp, x, NN, preferred_element_type=jnp.float32)
    wide = resp.astype(jnp.float32)
    lanes = cnt_ref.shape[1]
    counted = functools.reduce(
        jnp.add, [wide[:, k : k + lanes] for k in range(0, x.shape[0], lanes)]
    )
    if first:
        acc_ref[...] = part
        cnt_ref[...] = counted
    else:
        acc_ref[...] += part
        cnt_ref[...] += counted


def near_kernel(cores, where_ref, points_ref, c_ref, lse_ref, *refs):
    x_refs, lse_refs = refs[: 4 * cores], refs[4 * cores : 4 * cores + 2]
    acc_ref, cnt_ref, twice_ref, norm_ref, own_ref = refs[4 * cores + 2 :]
    share, size = twice_ref.shape[0], own_ref.shape[0]
    plane, line = lax.rem(where_ref[0], 4), lax.div(where_ref[0], 4)
    start = pl.multiple_of(plane * share, share)
    c = c_ref[pl.ds(start, share), :]
    twice_ref[...] = c + c
    norm_ref[...] = norms(c)
    own_ref[...] = c_ref[pl.ds(pl.multiple_of(start + line * size, size), size), :]
    half = points_ref.shape[0] // (2 * cores)
    for i in range(2 * cores):
        x = points_ref[i * half : (i + 1) * half, :]
        add_block(twice_ref[...], norm_ref[...], x, lse_ref[i : i + 1, :], acc_ref, cnt_ref, i == 0)
    for k in range(2):
        add_chip(cores, where_ref, twice_ref, norm_ref, x_refs[2 * cores * k : 2 * cores * (k + 1)], lse_refs[k], acc_ref, cnt_ref)


def add_chip(cores, where_ref, twice_ref, norm_ref, x_refs, lse_ref, acc_ref, cnt_ref):
    for rc in range(cores):
        for part in range(2):
            x = x_refs[2 * rc + part][...].astype(jnp.bfloat16)
            at = 2 * (where_ref[1] ^ rc) + part
            lse = lse_ref[pl.ds(at, 1), :]
            add_block(twice_ref[...], norm_ref[...], x, lse, acc_ref, cnt_ref, False)


def far_kernel(cores, lines, where_ref, twice_ref, norm_ref, acc_in_ref, cnt_in_ref, lse_ref, *refs):
    x_refs, out_refs = refs[: 2 * cores], refs[2 * cores : 2 * cores + lines]
    acc_ref, cnt_ref = refs[2 * cores + lines :]
    acc_ref[...] = acc_in_ref[...]
    cnt_ref[...] = cnt_in_ref[...]
    add_chip(cores, where_ref, twice_ref, norm_ref, x_refs, lse_ref, acc_ref, cnt_ref)
    line = lax.div(where_ref[0], 4)
    width = acc_ref.shape[1]
    size = acc_ref.shape[0] // lines
    for r in range(lines):
        start = pl.multiple_of((line ^ r) * size, size)
        out_refs[r][0:size, :] = acc_ref[pl.ds(start, size), :]
        turned = jnp.sum(cnt_ref[pl.ds(start, size), :].T, axis=0, keepdims=True)
        if size < width:
            turned = jnp.concatenate([turned, jnp.zeros((1, width - size), jnp.float32)], axis=1)
        out_refs[r][size : size + 8, :] = jnp.broadcast_to(turned, (8, width))


def finish_kernel(c_ref, *refs):
    out_ref = refs[-1]
    size, width = c_ref.shape
    total = functools.reduce(jnp.add, [ref[...] for ref in refs[:-1]])
    counts = total[size:, :]
    column = counts.T[:size, 0:1]
    out_ref[0:size, :] = (total[:size, :] + prior_mass * c_ref[...].astype(jnp.float32)) / (
        column + prior_mass
    )
    row = lax.broadcasted_iota(jnp.int32, (8, LANES), 0)
    spread = jnp.zeros((8, LANES), jnp.float32)
    for k in range(size // LANES):
        spread = jnp.where(row == k, counts[:, k * LANES : (k + 1) * LANES], spread)
    out_ref[size:, :] = jnp.concatenate([spread] * (width // LANES), axis=1)


def place_kernel(count, lines, late, where_ref, *refs):
    block_refs = refs[:count]
    if late is None:
        new_ref, sems = refs[count:]
        chosen = range(count)
    else:
        _, new_ref, counts_ref, tiles_ref, sems = refs[count:]
        chosen = late
    width = new_ref.shape[1]
    size = block_refs[0].shape[0] - 8
    plane, line = lax.rem(where_ref[0], 4), lax.div(where_ref[0], 4)

    def place(i, names):
        bits, r = names
        return (plane ^ bits) * lines + (line ^ r)

    names = NAMES(lines)
    copies = []
    for i in chosen:
        at = pl.multiple_of(place(i, names[i]) * size, size)
        copies.append(
            pltpu.make_async_copy(block_refs[i].at[0:size, :], new_ref.at[pl.ds(at, size), :], sems.at[i])
        )
    if late is not None:
        for i in range(count):
            copies.append(
                pltpu.make_async_copy(block_refs[i].at[size:, :], tiles_ref.at[i], sems.at[count + i])
            )
    for copy in copies:
        copy.start()
    for copy in copies:
        copy.wait()
    if late is not None:
        each = size // LANES
        for i in range(count):
            for k in range(each):
                counts_ref[pl.ds(place(i, names[i]) * each + k, 1), :] = tiles_ref[i, k : k + 1, 0:LANES]


def NAMES(lines):
    cut = lines // 2
    names = [(0, r) for r in range(lines)]
    names += [(b, r) for r in range(lines) for b in (1, 2)]
    names += [(3, r) for r in range(lines)]
    return names


def body(n, cores, points, centroids):
    rows, width = points.shape
    local_cent = centroids.shape[0]
    lines = n // 4
    half = rows // (2 * cores)
    share = local_cent // 4
    size = share // lines
    where = jnp.stack([lax.axis_index("dp"), lax.axis_index("cent")]).astype(jnp.int32)

    def flip(x, bits):
        return lax.ppermute(x, "dp", [(i, i ^ bits) for i in range(n)])

    def flip_core(x, bits):
        return lax.ppermute(x, "cent", [(i, i ^ bits) for i in range(cores)])

    first, second = call(
        open_kernel, (f32(half, width), f32(half, width)), [SMEM, VMEM], (where, points), "open"
    )
    x0, y1 = flip(first, 1), flip(second, 2)
    x1, y0 = flip(second, 1), flip(first, 2)

    pair = call(
        stats_kernel,
        f32(2, rows),
        [VMEM, VMEM],
        (points, centroids),
        "stats",
        scratch=[pltpu.VMEM((min(1024, local_cent), LANES), jnp.float32)],
        flops=2 * rows * local_cent * width,
    )
    pair, x0, y1 = lax.optimization_barrier((pair, x0, y1))
    d0, d1 = flip(x0, 2), flip(y1, 1)
    pairs = [pair] + [flip_core(pair, rc) for rc in range(1, cores)]
    top = functools.reduce(jnp.maximum, [p[0] for p in pairs])
    total = functools.reduce(jnp.add, [p[1] * jnp.exp(p[0] - top) for p in pairs])
    lse = top + jnp.log(total)
    log_evidence = lse - math.log(local_cent * cores)
    lse = lse.reshape(2 * cores, half)
    lse_x, lse_y, lse_d = flip(lse, 1), flip(lse, 2), flip(lse, 3)

    def with_siblings(a, b):
        out = [a, b]
        for rc in range(1, cores):
            out += [flip_core(a, rc), flip_core(b, rc)]
        return out

    acc, cnt, twice, norm, own = call(
        functools.partial(near_kernel, cores),
        (
            f32(share, width),
            f32(share, min(LANES, half)),
            jax.ShapeDtypeStruct((share, width), jnp.bfloat16),
            f32(share, LANES),
            jax.ShapeDtypeStruct((size, width), jnp.bfloat16),
        ),
        [SMEM] + [VMEM] * (5 + 4 * cores),
        (where, points, centroids, lse, *with_siblings(x0, x1), *with_siblings(y0, y1), lse_x, lse_y),
        "near",
        flops=4 * share * width * 3 * rows,
    )
    sums = call(
        functools.partial(far_kernel, cores, lines),
        [f32(size + 8, width)] * lines,
        [SMEM] + [VMEM] * (5 + 2 * cores),
        (where, twice, norm, acc, cnt, lse_d, *with_siblings(d0, d1)),
        "far",
        scratch=[
            pltpu.VMEM((share, width), jnp.float32),
            pltpu.VMEM((share, min(LANES, half)), jnp.float32),
        ],
        flops=4 * share * width * rows,
    )
    summed = [sums[0]] + [flip(sums[r], 4 * r) for r in range(1, lines)]
    done = call(finish_kernel, f32(size + 8, width), [VMEM] * (1 + lines), (own, *summed), "finish")

    column = [done] + [flip(done, 4 * r) for r in range(1, lines)]
    over_x = [flip(b, 1) for b in column]
    over_y = [flip(b, 2) for b in column]
    cut = lines // 2
    over_xy = [flip(b, 2) for b in over_x[:cut]] + [flip(b, 1) for b in over_y[cut:]]
    blocks = column + [b for pair in zip(over_x, over_y) for b in pair] + over_xy
    count = 4 * lines
    early = count - lines
    new = call(
        functools.partial(place_kernel, early, lines, None),
        f32(local_cent, width),
        [SMEM] + [ANY] * early,
        (where, *blocks[:early]),
        "place_early",
        out_specs=ANY,
        scratch=[pltpu.SemaphoreType.DMA((early,))],
    )
    new, counts = call(
        functools.partial(place_kernel, count, lines, tuple(range(early, count))),
        (f32(local_cent, width), f32(local_cent // LANES, LANES)),
        [SMEM] + [ANY] * (count + 1),
        (where, *blocks, new),
        "place_late",
        out_specs=(ANY, VMEM),
        scratch=[pltpu.VMEM((count, 8, width), jnp.float32), pltpu.SemaphoreType.DMA((2 * count,))],
        aliases={count + 1: 0},
    )
    return new, counts.reshape(-1), log_evidence


def solution(mesh):
    n, cores = mesh.shape["dp"], mesh.shape["cent"]
    return jax.shard_map(
        functools.partial(body, n, cores),
        mesh=mesh,
        in_specs=(P("dp", None), P("cent", None)),
        out_specs=(P("cent", None), P("cent"), P("dp")),
        check_vma=False,
    )
```

```python
import functools
import math

import jax
import jax.numpy as jnp
from jax import lax
from jax.experimental import pallas as pl
from jax.experimental.pallas import tpu as pltpu
from jax.sharding import PartitionSpec as P

prior_mass = 0.5
VMEM_LIMIT = 48 * 1024 * 1024
LANES = 128
NT = (((1,), (1,)), ((), ()))
NN = (((1,), (0,)), ((), ()))
VMEM = pl.BlockSpec(memory_space=pltpu.VMEM)
SMEM = pl.BlockSpec(memory_space=pltpu.SMEM)
ANY = pl.BlockSpec(memory_space=pl.ANY)


def f32(*shape):
    return jax.ShapeDtypeStruct(shape, jnp.float32)


def call(kernel, out_shape, in_specs, args, name, out_specs=None, scratch=(), flops=0, aliases={}):
    return pl.pallas_call(
        kernel,
        out_shape=out_shape,
        in_specs=in_specs,
        out_specs=jax.tree.map(lambda _: VMEM, out_shape) if out_specs is None else out_specs,
        scratch_shapes=list(scratch),
        input_output_aliases=aliases,
        compiler_params=pltpu.CompilerParams(vmem_limit_bytes=VMEM_LIMIT),
        cost_estimate=pl.CostEstimate(
            flops=flops,
            bytes_accessed=sum(a.size * a.dtype.itemsize for a in args),
            transcendentals=0,
        ),
        name=name,
    )(*args)


def open_kernel(where_ref, points_ref, first_ref, second_ref):
    half = first_ref.shape[0]
    start = pl.multiple_of(where_ref[1] * (2 * half), 2 * half)
    first_ref[...] = points_ref[pl.ds(start, half), :].astype(jnp.float32)
    second_ref[...] = points_ref[pl.ds(pl.multiple_of(start + half, half), half), :].astype(jnp.float32)


def widen(norm, width):
    if width <= norm.shape[1]:
        return norm[:, :width]
    return jnp.concatenate([norm] * (width // norm.shape[1]), axis=1)


def norms(c):
    c = c.astype(jnp.float32)
    return jnp.broadcast_to(jnp.sum(c * c, axis=1, keepdims=True), (c.shape[0], LANES))


def stats_kernel(points_ref, c_ref, out_ref, norm_ref):
    rows, local = points_ref.shape[0], c_ref.shape[0]
    tile, chunk = min(256, rows), min(1024, local)
    for part in range(0, local, chunk):
        c = c_ref[part : part + chunk, :]
        norm_ref[...] = norms(c)
        twice = c + c
        for start in range(0, rows, tile):
            at = slice(start, start + tile)
            dots = lax.dot_general(twice, points_ref[at, :], NT, preferred_element_type=jnp.float32)
            score = dots - widen(norm_ref[...], tile)
            top = jnp.max(score, axis=0, keepdims=True)
            total = jnp.sum(jnp.exp(score - top), axis=0, keepdims=True)
            if part:
                old_top, old_total = out_ref[0:1, at], out_ref[1:2, at]
                new_top = jnp.maximum(old_top, top)
                total = old_total * jnp.exp(old_top - new_top) + total * jnp.exp(top - new_top)
                top = new_top
            out_ref[0:1, at] = top
            out_ref[1:2, at] = total


def add_block(twice, norm, x, lse, acc_ref, cnt_ref, first):
    dots = lax.dot_general(twice, x, NT, preferred_element_type=jnp.float32)
    score = dots - widen(norm, x.shape[0])
    resp = jnp.exp(score - lse).astype(jnp.bfloat16)
    part = lax.dot_general(resp, x, NN, preferred_element_type=jnp.float32)
    wide = resp.astype(jnp.float32)
    lanes = cnt_ref.shape[1]
    counted = functools.reduce(
        jnp.add, [wide[:, k : k + lanes] for k in range(0, x.shape[0], lanes)]
    )
    if first:
        acc_ref[...] = part
        cnt_ref[...] = counted
    else:
        acc_ref[...] += part
        cnt_ref[...] += counted


def add_pieces(where_ref, twice_ref, norm_ref, pieces, acc_ref, cnt_ref):
    for x_ref, lse_ref, rc, part in pieces:
        at = 2 * (where_ref[1] ^ rc) + part
        x = x_ref[...].astype(jnp.bfloat16)
        add_block(twice_ref[...], norm_ref[...], x, lse_ref[pl.ds(at, 1), :], acc_ref, cnt_ref, False)


def near_kernel(cores, order, where_ref, points_ref, c_ref, lse_ref, lse_x_ref, lse_y_ref, *refs):
    x_refs = refs[: 2 * cores]
    acc_ref, cnt_ref, twice_ref, norm_ref, own_ref = refs[2 * cores :]
    share, size = twice_ref.shape[0], own_ref.shape[0]
    plane, line = lax.rem(where_ref[0], 4), lax.div(where_ref[0], 4)
    start = pl.multiple_of(plane * share, share)
    c = c_ref[pl.ds(start, share), :]
    twice_ref[...] = c + c
    norm_ref[...] = norms(c)
    own_ref[...] = c_ref[pl.ds(pl.multiple_of(start + line * size, size), size), :]
    half = points_ref.shape[0] // (2 * cores)
    for i in range(2 * cores):
        x = points_ref[i * half : (i + 1) * half, :]
        add_block(twice_ref[...], norm_ref[...], x, lse_ref[i : i + 1, :], acc_ref, cnt_ref, i == 0)
    pieces = [(x_refs[rc], lse_x_ref, rc, 0) for rc in range(cores)]
    pieces += [(x_refs[cores + rc], lse_y_ref, rc, 1) for rc in range(cores)]
    add_pieces(where_ref, twice_ref, norm_ref, pieces, acc_ref, cnt_ref)


def far_kernel(cores, order, where_ref, twice_ref, norm_ref, acc_in_ref, cnt_in_ref, lse_x_ref, lse_y_ref, lse_d_ref, *refs):
    lines = len(order)
    x_refs, out_refs = refs[: 4 * cores], refs[4 * cores : 4 * cores + lines]
    acc_ref, cnt_ref = refs[4 * cores + lines :]
    acc_ref[...] = acc_in_ref[...]
    cnt_ref[...] = cnt_in_ref[...]
    whose = ((lse_x_ref, 1), (lse_y_ref, 0), (lse_d_ref, 0), (lse_d_ref, 1))
    pieces = [
        (x_refs[k * cores + rc], lse, rc, part)
        for k, (lse, part) in enumerate(whose)
        for rc in range(cores)
    ]
    add_pieces(where_ref, twice_ref, norm_ref, pieces, acc_ref, cnt_ref)
    line = lax.div(where_ref[0], 4)
    width = acc_ref.shape[1]
    size = acc_ref.shape[0] // lines
    for s in range(lines):
        start = pl.multiple_of(behind(order, line, s) * size, size)
        out_refs[s][0:size, :] = acc_ref[pl.ds(start, size), :]
        turned = jnp.sum(cnt_ref[pl.ds(start, size), :].T, axis=0, keepdims=True)
        if size < width:
            turned = jnp.concatenate([turned, jnp.zeros((1, width - size), jnp.float32)], axis=1)
        out_refs[s][size : size + 8, :] = jnp.broadcast_to(turned, (8, width))


def behind(order, line, steps):
    n = len(order)
    return functools.reduce(
        jnp.add,
        [jnp.where(line == order[p], order[(p - steps) % n], 0) for p in range(n)],
    )


def add_kernel(a_ref, b_ref, out_ref):
    out_ref[...] = a_ref[...] + b_ref[...]


def finish_kernel(c_ref, *refs):
    out_ref = refs[-1]
    size, width = c_ref.shape
    total = functools.reduce(jnp.add, [ref[...] for ref in refs[:-1]])
    counts = total[size:, :]
    column = counts.T[:size, 0:1]
    out_ref[0:size, :] = (total[:size, :] + prior_mass * c_ref[...].astype(jnp.float32)) / (
        column + prior_mass
    )
    row = lax.broadcasted_iota(jnp.int32, (8, LANES), 0)
    spread = jnp.zeros((8, LANES), jnp.float32)
    for k in range(size // LANES):
        spread = jnp.where(row == k, counts[:, k * LANES : (k + 1) * LANES], spread)
    out_ref[size:, :] = jnp.concatenate([spread] * (width // LANES), axis=1)


def place_kernel(names, order, late, where_ref, *refs):
    count, lines = len(names), len(order)
    block_refs = refs[:count]
    if late is None:
        new_ref, sems = refs[count:]
        chosen = range(count)
    else:
        _, new_ref, counts_ref, tiles_ref, sems = refs[count:]
        chosen = late
    width = new_ref.shape[1]
    size = block_refs[0].shape[0] - 8
    plane, line = lax.rem(where_ref[0], 4), lax.div(where_ref[0], 4)

    def place(i):
        bits, steps = names[i]
        return (plane ^ bits) * lines + behind(order, line, steps)

    copies = []
    for i in chosen:
        at = pl.multiple_of(place(i) * size, size)
        copies.append(
            pltpu.make_async_copy(block_refs[i].at[0:size, :], new_ref.at[pl.ds(at, size), :], sems.at[i])
        )
    if late is not None:
        for i in range(count):
            copies.append(
                pltpu.make_async_copy(block_refs[i].at[size:, :], tiles_ref.at[i], sems.at[count + i])
            )
    for copy in copies:
        copy.start()
    for copy in copies:
        copy.wait()
    if late is not None:
        each = size // LANES
        for i in range(count):
            for k in range(each):
                counts_ref[pl.ds(place(i) * each + k, 1), :] = tiles_ref[i, k : k + 1, 0:LANES]


def body(n, cores, points, centroids):
    rows, width = points.shape
    local_cent = centroids.shape[0]
    lines = n // 4
    half = rows // (2 * cores)
    share = local_cent // 4
    size = share // lines
    order = tuple(range(0, lines, 2)) + tuple(range(1, lines, 2))[::-1]
    where = jnp.stack([lax.axis_index("dp"), lax.axis_index("cent")]).astype(jnp.int32)

    def flip(x, bits):
        return lax.ppermute(x, "dp", [(i, i ^ bits) for i in range(n)])

    def flip_core(x, bits):
        return lax.ppermute(x, "cent", [(i, i ^ bits) for i in range(cores)])

    def ring(x):
        pairs = [(order[p], order[(p + 1) % lines]) for p in range(lines)]
        return lax.ppermute(x, "dp", [(4 * a + i, 4 * b + i) for a, b in pairs for i in range(4)])

    first, second = call(
        open_kernel, (f32(half, width), f32(half, width)), [SMEM, VMEM], (where, points), "open"
    )
    x0, y1 = flip(first, 1), flip(second, 2)
    x1, y0 = flip(second, 1), flip(first, 2)

    pair = call(
        stats_kernel,
        f32(2, rows),
        [VMEM, VMEM],
        (points, centroids),
        "stats",
        scratch=[pltpu.VMEM((min(1024, local_cent), LANES), jnp.float32)],
        flops=2 * rows * local_cent * width,
    )
    pair, x0, y1 = lax.optimization_barrier((pair, x0, y1))
    d0, d1 = flip(x0, 2), flip(y1, 1)
    pairs = [pair] + [flip_core(pair, rc) for rc in range(1, cores)]
    top = functools.reduce(jnp.maximum, [p[0] for p in pairs])
    total = functools.reduce(jnp.add, [p[1] * jnp.exp(p[0] - top) for p in pairs])
    lse = top + jnp.log(total)
    log_evidence = lse - math.log(local_cent * cores)
    lse = lse.reshape(2 * cores, half)
    lse_x, lse_y, lse_d = flip(lse, 1), flip(lse, 2), flip(lse, 3)

    def with_siblings(pieces):
        return [a if rc == 0 else flip_core(a, rc) for a in pieces for rc in range(cores)]

    acc, cnt, twice, norm, own = call(
        functools.partial(near_kernel, cores, order),
        (
            f32(share, width),
            f32(share, min(LANES, half)),
            jax.ShapeDtypeStruct((share, width), jnp.bfloat16),
            f32(share, LANES),
            jax.ShapeDtypeStruct((size, width), jnp.bfloat16),
        ),
        [SMEM] + [VMEM] * (5 + 2 * cores),
        (where, points, centroids, lse, lse_x, lse_y, *with_siblings((x0, y1))),
        "near",
        flops=4 * share * width * 2 * rows,
    )
    late = lax.optimization_barrier((x1, y0, d0, d1))
    sums = call(
        functools.partial(far_kernel, cores, order),
        [f32(size + 8, width)] * lines,
        [SMEM] + [VMEM] * (7 + 4 * cores),
        (where, twice, norm, acc, cnt, lse_x, lse_y, lse_d, *with_siblings(late)),
        "far",
        scratch=[
            pltpu.VMEM((share, width), jnp.float32),
            pltpu.VMEM((share, min(LANES, half)), jnp.float32),
        ],
        flops=4 * share * width * 2 * rows,
    )
    moving = ring(sums[1])
    for s in range(2, lines):
        moving = ring(call(add_kernel, f32(size + 8, width), [VMEM] * 2, (sums[s], moving), "add"))
    done = call(finish_kernel, f32(size + 8, width), [VMEM] * 3, (own, sums[0], moving), "finish")

    column = [done]
    for s in range(1, lines):
        column.append(ring(column[-1]))
    over_x = [flip(b, 1) for b in column]
    over_y = [flip(b, 2) for b in column]
    cut = lines // 2
    over_xy = [flip(b, 2) for b in over_x[:cut]] + [flip(b, 1) for b in over_y[cut:]]
    blocks = column + [b for pair in zip(over_x, over_y) for b in pair] + over_xy
    names = [(0, s) for s in range(lines)] + [(b, s) for s in range(lines) for b in (1, 2)]
    names += [(3, s) for s in range(lines)]
    count = 4 * lines
    early = count - lines
    new = call(
        functools.partial(place_kernel, names[:early], order, None),
        f32(local_cent, width),
        [SMEM] + [ANY] * early,
        (where, *blocks[:early]),
        "place_early",
        out_specs=ANY,
        scratch=[pltpu.SemaphoreType.DMA((early,))],
    )
    new, counts = call(
        functools.partial(place_kernel, names, order, tuple(range(early, count))),
        (f32(local_cent, width), f32(local_cent // LANES, LANES)),
        [SMEM] + [ANY] * (count + 1),
        (where, *blocks, new),
        "place_late",
        out_specs=(ANY, VMEM),
        scratch=[pltpu.VMEM((count, 8, width), jnp.float32), pltpu.SemaphoreType.DMA((2 * count,))],
        aliases={count + 1: 0},
    )
    return new, counts.reshape(-1), log_evidence


def solution(mesh):
    n, cores = mesh.shape["dp"], mesh.shape["cent"]
    return jax.shard_map(
        functools.partial(body, n, cores),
        mesh=mesh,
        in_specs=(P("dp", None), P("cent", None)),
        out_specs=(P("cent", None), P("cent"), P("dp")),
        check_vma=False,
    )
```

```python
import functools
import math

import jax
import jax.numpy as jnp
from jax import lax
from jax.experimental import pallas as pl
from jax.experimental.pallas import tpu as pltpu
from jax.sharding import PartitionSpec as P

prior_mass = 0.5
VMEM_LIMIT = 48 * 1024 * 1024
LANES = 128
NT = (((1,), (1,)), ((), ()))
NN = (((1,), (0,)), ((), ()))
VMEM = pl.BlockSpec(memory_space=pltpu.VMEM)
SMEM = pl.BlockSpec(memory_space=pltpu.SMEM)
ANY = pl.BlockSpec(memory_space=pl.ANY)


def f32(*shape):
    return jax.ShapeDtypeStruct(shape, jnp.float32)


def call(kernel, out_shape, in_specs, args, name, out_specs=None, scratch=(), flops=0, aliases={}):
    return pl.pallas_call(
        kernel,
        out_shape=out_shape,
        in_specs=in_specs,
        out_specs=jax.tree.map(lambda _: VMEM, out_shape) if out_specs is None else out_specs,
        scratch_shapes=list(scratch),
        input_output_aliases=aliases,
        compiler_params=pltpu.CompilerParams(vmem_limit_bytes=VMEM_LIMIT),
        cost_estimate=pl.CostEstimate(
            flops=flops,
            bytes_accessed=sum(a.size * a.dtype.itemsize for a in args),
            transcendentals=0,
        ),
        name=name,
    )(*args)


def open_kernel(where_ref, points_ref, first_ref, second_ref):
    half = first_ref.shape[0]
    start = pl.multiple_of(where_ref[1] * (2 * half), 2 * half)
    first_ref[...] = points_ref[pl.ds(start, half), :].astype(jnp.float32)
    second_ref[...] = points_ref[pl.ds(pl.multiple_of(start + half, half), half), :].astype(jnp.float32)


def widen(norm, width):
    if width <= norm.shape[1]:
        return norm[:, :width]
    return jnp.concatenate([norm] * (width // norm.shape[1]), axis=1)


def norms(c):
    c = c.astype(jnp.float32)
    return jnp.broadcast_to(jnp.sum(c * c, axis=1, keepdims=True), (c.shape[0], LANES))


def stats_kernel(points_ref, c_ref, out_ref, norm_ref):
    rows, local = points_ref.shape[0], c_ref.shape[0]
    tile, chunk = min(256, rows), min(1024, local)
    for part in range(0, local, chunk):
        c = c_ref[part : part + chunk, :]
        norm_ref[...] = norms(c)
        twice = c + c
        for start in range(0, rows, tile):
            at = slice(start, start + tile)
            dots = lax.dot_general(twice, points_ref[at, :], NT, preferred_element_type=jnp.float32)
            score = dots - widen(norm_ref[...], tile)
            top = jnp.max(score, axis=0, keepdims=True)
            total = jnp.sum(jnp.exp(score - top), axis=0, keepdims=True)
            if part:
                old_top, old_total = out_ref[0:1, at], out_ref[1:2, at]
                new_top = jnp.maximum(old_top, top)
                total = old_total * jnp.exp(old_top - new_top) + total * jnp.exp(top - new_top)
                top = new_top
            out_ref[0:1, at] = top
            out_ref[1:2, at] = total


def add_block(twice, norm, x, lse, acc_ref, cnt_ref, first):
    dots = lax.dot_general(twice, x, NT, preferred_element_type=jnp.float32)
    score = dots - widen(norm, x.shape[0])
    resp = jnp.exp(score - lse).astype(jnp.bfloat16)
    part = lax.dot_general(resp, x, NN, preferred_element_type=jnp.float32)
    wide = resp.astype(jnp.float32)
    lanes = cnt_ref.shape[1]
    counted = functools.reduce(
        jnp.add, [wide[:, k : k + lanes] for k in range(0, x.shape[0], lanes)]
    )
    if first:
        acc_ref[...] = part
        cnt_ref[...] = counted
    else:
        acc_ref[...] += part
        cnt_ref[...] += counted


def add_pieces(where_ref, twice_ref, norm_ref, pieces, acc_ref, cnt_ref):
    for x_ref, lse_ref, rc, part in pieces:
        at = 2 * (where_ref[1] ^ rc) + part
        x = x_ref[...].astype(jnp.bfloat16)
        add_block(twice_ref[...], norm_ref[...], x, lse_ref[pl.ds(at, 1), :], acc_ref, cnt_ref, False)


def own_kernel(cores, order, where_ref, points_ref, c_ref, lse_ref, acc_ref, cnt_ref, twice_ref, norm_ref, own_ref):
    size = own_ref.shape[0]
    plane, line = lax.rem(where_ref[0], 4), lax.div(where_ref[0], 4)
    for l in range(len(order)):
        c = c_ref[pl.ds(pl.multiple_of((4 * l + plane) * size, size), size), :]
        twice_ref[l * size : (l + 1) * size, :] = c + c
        norm_ref[l * size : (l + 1) * size, :] = norms(c)
    own_ref[...] = c_ref[pl.ds(pl.multiple_of((4 * line + plane) * size, size), size), :]
    half = points_ref.shape[0] // (2 * cores)
    for i in range(2 * cores):
        x = points_ref[i * half : (i + 1) * half, :]
        add_block(twice_ref[...], norm_ref[...], x, lse_ref[i : i + 1, :], acc_ref, cnt_ref, i == 0)


def near_kernel(cores, where_ref, twice_ref, norm_ref, acc_in_ref, cnt_in_ref, lse_x_ref, lse_y_ref, *refs):
    x_refs = refs[: 2 * cores]
    acc_ref, cnt_ref = refs[2 * cores :]
    acc_ref[...] = acc_in_ref[...]
    cnt_ref[...] = cnt_in_ref[...]
    pieces = [(x_refs[rc], lse_x_ref, rc, 0) for rc in range(cores)]
    pieces += [(x_refs[cores + rc], lse_y_ref, rc, 1) for rc in range(cores)]
    add_pieces(where_ref, twice_ref, norm_ref, pieces, acc_ref, cnt_ref)


def far_kernel(cores, order, where_ref, twice_ref, norm_ref, acc_in_ref, cnt_in_ref, lse_x_ref, lse_y_ref, lse_d_ref, *refs):
    lines = len(order)
    x_refs, out_refs = refs[: 4 * cores], refs[4 * cores : 4 * cores + lines]
    acc_ref, cnt_ref = refs[4 * cores + lines :]
    acc_ref[...] = acc_in_ref[...]
    cnt_ref[...] = cnt_in_ref[...]
    whose = ((lse_x_ref, 1), (lse_y_ref, 0), (lse_d_ref, 0), (lse_d_ref, 1))
    pieces = [
        (x_refs[k * cores + rc], lse, rc, part)
        for k, (lse, part) in enumerate(whose)
        for rc in range(cores)
    ]
    add_pieces(where_ref, twice_ref, norm_ref, pieces, acc_ref, cnt_ref)
    line = lax.div(where_ref[0], 4)
    width = acc_ref.shape[1]
    size = acc_ref.shape[0] // lines
    for s in range(lines):
        start = pl.multiple_of(behind(order, line, s) * size, size)
        out_refs[s][0:size, :] = acc_ref[pl.ds(start, size), :]
        turned = jnp.sum(cnt_ref[pl.ds(start, size), :].T, axis=0, keepdims=True)
        if size < width:
            turned = jnp.concatenate([turned, jnp.zeros((1, width - size), jnp.float32)], axis=1)
        out_refs[s][size : size + 8, :] = jnp.broadcast_to(turned, (8, width))


def behind(order, line, steps):
    n = len(order)
    return functools.reduce(
        jnp.add,
        [jnp.where(line == order[p], order[(p - steps) % n], 0) for p in range(n)],
    )


def add_kernel(a_ref, b_ref, out_ref):
    out_ref[...] = a_ref[...] + b_ref[...]


def finish_kernel(c_ref, mine_ref, moved_ref, out_ref):
    size, width = c_ref.shape
    total = mine_ref[...] + moved_ref[...]
    counts = total[size:, :]
    column = counts.T[:size, 0:1]
    out_ref[0:size, :] = (total[:size, :] + prior_mass * c_ref[...].astype(jnp.float32)) / (
        column + prior_mass
    )
    out_ref[size:, :] = counts


def body(n, cores, points, centroids):
    rows, width = points.shape
    local_cent = centroids.shape[0]
    lines = n // 4
    half = rows // (2 * cores)
    share = local_cent // 4
    size = share // lines
    order = tuple(range(0, lines, 2)) + tuple(range(1, lines, 2))[::-1]
    where = jnp.stack([lax.axis_index("dp"), lax.axis_index("cent")]).astype(jnp.int32)

    def flip(x, bits):
        return lax.ppermute(x, "dp", [(i, i ^ bits) for i in range(n)])

    def flip_core(x, bits):
        return lax.ppermute(x, "cent", [(i, i ^ bits) for i in range(cores)])

    def ring(x):
        pairs = [(order[p], order[(p + 1) % lines]) for p in range(lines)]
        return lax.ppermute(x, "dp", [(4 * a + i, 4 * b + i) for a, b in pairs for i in range(4)])

    first, second = call(
        open_kernel, (f32(half, width), f32(half, width)), [SMEM, VMEM], (where, points), "open"
    )
    x0, y1 = flip(first, 1), flip(second, 2)
    x1, y0 = flip(second, 1), flip(first, 2)

    pair = call(
        stats_kernel,
        f32(2, rows),
        [VMEM, VMEM],
        (points, centroids),
        "stats",
        scratch=[pltpu.VMEM((min(1024, local_cent), LANES), jnp.float32)],
        flops=2 * rows * local_cent * width,
    )
    pair, x0, y1 = lax.optimization_barrier((pair, x0, y1))
    d0, d1 = flip(x0, 2), flip(y1, 1)
    pairs = [pair] + [flip_core(pair, rc) for rc in range(1, cores)]
    top = functools.reduce(jnp.maximum, [p[0] for p in pairs])
    total = functools.reduce(jnp.add, [p[1] * jnp.exp(p[0] - top) for p in pairs])
    lse = top + jnp.log(total)
    log_evidence = lse - math.log(local_cent * cores)
    lse = lse.reshape(2 * cores, half)
    lse_x, lse_y, lse_d = flip(lse, 1), flip(lse, 2), flip(lse, 3)

    def with_siblings(pieces):
        return [a if rc == 0 else flip_core(a, rc) for a in pieces for rc in range(cores)]

    acc_shape, cnt_shape = f32(share, width), f32(share, min(LANES, half))
    acc, cnt, twice, norm, own = call(
        functools.partial(own_kernel, cores, order),
        (
            acc_shape,
            cnt_shape,
            jax.ShapeDtypeStruct((share, width), jnp.bfloat16),
            f32(share, LANES),
            jax.ShapeDtypeStruct((size, width), jnp.bfloat16),
        ),
        [SMEM] + [VMEM] * 3,
        (where, points, centroids, lse),
        "own",
        flops=4 * share * width * rows,
    )
    early = with_siblings((x0, y1))
    early, late, acc, cnt, lse_x, lse_y, lse_d = lax.optimization_barrier(
        (early, (x1, y0, d0, d1), acc, cnt, lse_x, lse_y, lse_d)
    )
    late = with_siblings(late)
    acc, cnt = call(
        functools.partial(near_kernel, cores),
        (acc_shape, cnt_shape),
        [SMEM] + [VMEM] * (6 + 2 * cores),
        (where, twice, norm, acc, cnt, lse_x, lse_y, *early),
        "near",
        flops=4 * share * width * rows,
        aliases={3: 0, 4: 1},
    )
    sums = call(
        functools.partial(far_kernel, cores, order),
        [f32(size + 8, width)] * lines,
        [SMEM] + [VMEM] * (7 + 4 * cores),
        (where, twice, norm, acc, cnt, lse_x, lse_y, lse_d, *late),
        "far",
        scratch=[
            pltpu.VMEM((share, width), jnp.float32),
            pltpu.VMEM((share, min(LANES, half)), jnp.float32),
        ],
        flops=4 * share * width * 2 * rows,
    )
    moving = ring(sums[1])
    for s in range(2, lines):
        moving = ring(call(add_kernel, f32(size + 8, width), [VMEM] * 2, (sums[s], moving), "add"))
    done = call(finish_kernel, f32(size + 8, width), [VMEM] * 3, (own, sums[0], moving), "finish")
    gathered = lax.all_gather(done, "dp", axis=0)
    new = gathered[:, :size, :].reshape(local_cent, width)
    counts = gathered[:, size, :size].reshape(-1)
    return new, counts, log_evidence


def solution(mesh):
    n, cores = mesh.shape["dp"], mesh.shape["cent"]
    return jax.shard_map(
        functools.partial(body, n, cores),
        mesh=mesh,
        in_specs=(P("dp", None), P("cent", None)),
        out_specs=(P("cent", None), P("cent"), P("dp")),
        check_vma=False,
    )
```

```python
import functools
import math

import jax
import jax.numpy as jnp
from jax import lax
from jax.experimental import pallas as pl
from jax.experimental.pallas import tpu as pltpu
from jax.sharding import PartitionSpec as P

prior_mass = 0.5
VMEM_LIMIT = 48 * 1024 * 1024
LANES = 128
NT = (((1,), (1,)), ((), ()))
NN = (((1,), (0,)), ((), ()))
VMEM = pl.BlockSpec(memory_space=pltpu.VMEM)
SMEM = pl.BlockSpec(memory_space=pltpu.SMEM)
ANY = pl.BlockSpec(memory_space=pl.ANY)
HBM = pl.BlockSpec(memory_space=pltpu.HBM)


def f32(*shape):
    return jax.ShapeDtypeStruct(shape, jnp.float32)


def call(kernel, out_shape, in_specs, args, name, out_specs=None, scratch=(), flops=0, aliases={}):
    return pl.pallas_call(
        kernel,
        out_shape=out_shape,
        in_specs=in_specs,
        out_specs=jax.tree.map(lambda _: VMEM, out_shape) if out_specs is None else out_specs,
        scratch_shapes=list(scratch),
        input_output_aliases=aliases,
        compiler_params=pltpu.CompilerParams(vmem_limit_bytes=VMEM_LIMIT),
        cost_estimate=pl.CostEstimate(
            flops=flops,
            bytes_accessed=sum(a.size * a.dtype.itemsize for a in args),
            transcendentals=0,
        ),
        name=name,
    )(*args)


def open_kernel(where_ref, points_ref, first_ref, second_ref, raw_ref, sem):
    half = first_ref.shape[0]
    start = pl.multiple_of(where_ref[1] * (2 * half), 2 * half)
    copy = pltpu.make_async_copy(points_ref.at[pl.ds(start, 2 * half), :], raw_ref, sem)
    copy.start()
    copy.wait()
    first_ref[...] = raw_ref[:half, :].astype(jnp.float32)
    second_ref[...] = raw_ref[half:, :].astype(jnp.float32)


def widen(norm, width):
    if width <= norm.shape[1]:
        return norm[:, :width]
    return jnp.concatenate([norm] * (width // norm.shape[1]), axis=1)


def norms(c):
    c = c.astype(jnp.float32)
    return jnp.broadcast_to(jnp.sum(c * c, axis=1, keepdims=True), (c.shape[0], LANES))


def stats_kernel(lines, where_ref, points_hbm, c_hbm, out_ref, twice_ref, norm_ref, points_ref, c_ref, all_norm_ref, sems):
    rows, local = points_ref.shape[0], c_ref.shape[0]
    chunk = local // lines
    tile, size = min(256, rows), chunk // 4
    fetch = [pltpu.make_async_copy(points_hbm, points_ref, sems.at[lines])]
    for l in range(lines):
        part = pl.ds(l * chunk, chunk)
        fetch.append(pltpu.make_async_copy(c_hbm.at[part, :], c_ref.at[part, :], sems.at[l]))
    for copy in fetch:
        copy.start()
    fetch[0].wait()
    kept = pl.multiple_of(lax.rem(where_ref[0], 4) * size, size)
    for l in range(lines):
        fetch[1 + l].wait()
        c = c_ref[l * chunk : (l + 1) * chunk, :]
        all_norm_ref[...] = norms(c)
        twice = c + c
        mine = c_ref[pl.ds(pl.multiple_of(l * chunk + kept, size), size), :]
        twice_ref[l * size : (l + 1) * size, :] = mine + mine
        norm_ref[l * size : (l + 1) * size, :] = all_norm_ref[pl.ds(kept, size), :]
        for start in range(0, rows, tile):
            at = slice(start, start + tile)
            dots = lax.dot_general(twice, points_ref[at, :], NT, preferred_element_type=jnp.float32)
            score = dots - widen(all_norm_ref[...], tile)
            top = jnp.max(score, axis=0, keepdims=True)
            total = jnp.sum(jnp.exp(score - top), axis=0, keepdims=True)
            if l:
                old_top, old_total = out_ref[0:1, at], out_ref[1:2, at]
                new_top = jnp.maximum(old_top, top)
                total = old_total * jnp.exp(old_top - new_top) + total * jnp.exp(top - new_top)
                top = new_top
            out_ref[0:1, at] = top
            out_ref[1:2, at] = total


def stats(where, points, centroids, lines):
    rows, width = points.shape
    local = centroids.shape[0]
    return call(
        functools.partial(stats_kernel, lines),
        (
            f32(2, rows),
            jax.ShapeDtypeStruct((local // 4, width), jnp.bfloat16),
            f32(local // 4, LANES),
        ),
        [SMEM, HBM, HBM],
        (where, points, centroids),
        "stats",
        scratch=[
            pltpu.VMEM(points.shape, points.dtype),
            pltpu.VMEM(centroids.shape, centroids.dtype),
            pltpu.VMEM((local // lines, LANES), jnp.float32),
            pltpu.SemaphoreType.DMA((lines + 1,)),
        ],
        flops=4 * rows * local * width,
    )


def lse_kernel(cores, every, x0_ref, y1_ref, *refs):
    pair_refs = refs[:cores]
    lse_ref, evidence_ref, pack_x_ref, pack_y_ref = refs[cores:]
    half = lse_ref.shape[1]
    top = functools.reduce(jnp.maximum, [p[0:1, :] for p in pair_refs])
    total = functools.reduce(jnp.add, [p[1:2, :] * jnp.exp(p[0:1, :] - top) for p in pair_refs])
    lse = top + jnp.log(total)
    evidence = lse - math.log(every)
    for k in range(evidence_ref.shape[0]):
        evidence_ref[k : k + 1, :] = evidence[:, k * LANES : (k + 1) * LANES]
    for i in range(2 * cores):
        lse_ref[i : i + 1, :] = lse[:, i * half : (i + 1) * half]
    for piece_ref, pack_ref in ((x0_ref, pack_x_ref), (y1_ref, pack_y_ref)):
        pack_ref[0:half, :] = piece_ref[...]
        pack_ref[half:, :] = jnp.zeros_like(pack_ref[half:, :])
        pack_ref[half : half + 2 * cores, 0:half] = lse_ref[...]


def add_block(twice, norm, x, lse, acc_ref, cnt_ref, first):
    dots = lax.dot_general(twice, x, NT, preferred_element_type=jnp.float32)
    score = dots - widen(norm, x.shape[0])
    resp = jnp.exp(score - lse).astype(jnp.bfloat16)
    part = lax.dot_general(resp, x, NN, preferred_element_type=jnp.float32)
    wide = resp.astype(jnp.float32)
    lanes = cnt_ref.shape[1]
    counted = functools.reduce(
        jnp.add, [wide[:, k : k + lanes] for k in range(0, x.shape[0], lanes)]
    )
    if first:
        acc_ref[...] = part
        cnt_ref[...] = counted
    else:
        acc_ref[...] += part
        cnt_ref[...] += counted


def add_pieces(where_ref, twice_ref, norm_ref, pieces, acc_ref, cnt_ref):
    for x_ref, lse_ref, above, rc, part in pieces:
        at = above + 2 * (where_ref[1] ^ rc) + part
        half = acc_rows(x_ref)
        x = x_ref[0:half, :].astype(jnp.bfloat16)
        lse = lse_ref[pl.ds(at, 1), :][:, 0:half]
        add_block(twice_ref[...], norm_ref[...], x, lse, acc_ref, cnt_ref, False)


def acc_rows(ref):
    rows = ref.shape[0]
    return 1 << (rows.bit_length() - 1)


def own_kernel(cores, points_ref, twice_ref, norm_ref, lse_ref, acc_ref, cnt_ref):
    half = points_ref.shape[0] // (2 * cores)
    for i in range(2 * cores):
        x = points_ref[i * half : (i + 1) * half, :]
        add_block(twice_ref[...], norm_ref[...], x, lse_ref[i : i + 1, :], acc_ref, cnt_ref, i == 0)


def near_kernel(cores, where_ref, twice_ref, norm_ref, acc_in_ref, cnt_in_ref, d0_ref, d1_ref, *refs):
    x_refs = refs[: 2 * cores]
    acc_ref, cnt_ref = refs[2 * cores :]
    above = acc_rows(d0_ref)
    acc_ref[...] = acc_in_ref[...]
    cnt_ref[...] = cnt_in_ref[...]
    pieces = [(x_refs[rc], d1_ref, above, rc, 0) for rc in range(cores)]
    pieces += [(x_refs[cores + rc], d0_ref, above, rc, 1) for rc in range(cores)]
    add_pieces(where_ref, twice_ref, norm_ref, pieces, acc_ref, cnt_ref)


def far_kernel(cores, order, where_ref, twice_ref, norm_ref, acc_in_ref, cnt_in_ref, lse_d_ref, *refs):
    lines = len(order)
    x_refs, out_refs = refs[: 4 * cores], refs[4 * cores : 4 * cores + lines]
    acc_ref, cnt_ref = refs[4 * cores + lines :]
    d0_ref, d1_ref = x_refs[2 * cores], x_refs[3 * cores]
    above = acc_rows(d0_ref)
    acc_ref[...] = acc_in_ref[...]
    cnt_ref[...] = cnt_in_ref[...]
    whose = ((d1_ref, above, 1), (d0_ref, above, 0), (lse_d_ref, 0, 0), (lse_d_ref, 0, 1))
    pieces = [
        (x_refs[k * cores + rc], lse, top, rc, part)
        for k, (lse, top, part) in enumerate(whose)
        for rc in range(cores)
    ]
    add_pieces(where_ref, twice_ref, norm_ref, pieces, acc_ref, cnt_ref)
    line = lax.div(where_ref[0], 4)
    width = acc_ref.shape[1]
    size = acc_ref.shape[0] // lines
    for s in range(lines):
        start = pl.multiple_of(ahead(order, line, s) * size, size)
        out_refs[s][0:size, :] = acc_ref[pl.ds(start, size), :]
        turned = jnp.sum(cnt_ref[pl.ds(start, size), :].T, axis=0, keepdims=True)
        if size < width:
            turned = jnp.concatenate([turned, jnp.zeros((1, width - size), jnp.float32)], axis=1)
        out_refs[s][size : size + 8, :] = jnp.broadcast_to(turned, (8, width))


def ahead(order, line, steps):
    n = len(order)
    return functools.reduce(
        jnp.add,
        [jnp.where(line == order[p], order[(p + steps) % n], 0) for p in range(n)],
    )


def add_kernel(a_ref, b_ref, out_ref):
    out_ref[...] = a_ref[...] + b_ref[...]


def finish_kernel(where_ref, twice_ref, mine_ref, first_ref, second_ref, out_ref):
    size, width = out_ref.shape[0] - 8, out_ref.shape[1]
    start = pl.multiple_of(lax.div(where_ref[0], 4) * size, size)
    c = 0.5 * twice_ref[pl.ds(start, size), :].astype(jnp.float32)
    total = mine_ref[...] + first_ref[...] + second_ref[...]
    counts = total[size:, :]
    column = counts.T[:size, 0:1]
    out_ref[0:size, :] = (total[:size, :] + prior_mass * c) / (column + prior_mass)
    row = lax.broadcasted_iota(jnp.int32, (8, LANES), 0)
    spread = jnp.zeros((8, LANES), jnp.float32)
    for k in range(size // LANES):
        spread = jnp.where(row == k, counts[:, k * LANES : (k + 1) * LANES], spread)
    out_ref[size:, :] = jnp.concatenate([spread] * (width // LANES), axis=1)


def place_kernel(names, order, later, where_ref, *refs):
    count, lines = len(names), len(order)
    block_refs = refs[:count]
    new_ref, counts_ref, sems = refs[-3:]
    size = block_refs[0].shape[0] - 8
    plane, line = lax.rem(where_ref[0], 4), lax.div(where_ref[0], 4)
    each = size // LANES
    places = [ahead(order, line, steps) * 4 + (plane ^ bits) for bits, steps in names]
    copies = []
    for i in range(count):
        at = pl.multiple_of(places[i] * size, size)
        copies.append(
            pltpu.make_async_copy(block_refs[i].at[0:size, :], new_ref.at[pl.ds(at, size), :], sems.at[i])
        )
        copies[-1].start()
    if later:
        counts_ref[...] = refs[count][...]
    for i in range(count):
        for k in range(each):
            counts_ref[pl.ds(places[i] * each + k, 1), :] = block_refs[i][size + k : size + k + 1, 0:LANES]
    for copy in copies:
        copy.wait()


def body(n, cores, points, centroids):
    rows, width = points.shape
    local_cent = centroids.shape[0]
    lines = n // 4
    half = rows // (2 * cores)
    share = local_cent // 4
    size = share // lines
    order = tuple(range(0, lines, 2)) + tuple(range(1, lines, 2))[::-1]
    where = jnp.stack([lax.axis_index("dp"), lax.axis_index("cent")]).astype(jnp.int32)

    def flip(x, bits):
        return lax.ppermute(x, "dp", [(i, i ^ bits) for i in range(n)])

    def flip_core(x, bits):
        return lax.ppermute(x, "cent", [(i, i ^ bits) for i in range(cores)])

    def ring(x, way):
        pairs = [(order[p], order[(p + way) % lines]) for p in range(lines)]
        return lax.ppermute(x, "dp", [(4 * a + i, 4 * b + i) for a, b in pairs for i in range(4)])

    def with_siblings(pieces):
        return [a if rc == 0 else flip_core(a, rc) for a in pieces for rc in range(cores)]

    first, second = call(
        open_kernel,
        (f32(half, width), f32(half, width)),
        [SMEM, HBM],
        (where, points),
        "open",
        scratch=[pltpu.VMEM((2 * half, width), points.dtype), pltpu.SemaphoreType.DMA(())],
    )
    x0, y1 = flip(first, 1), flip(second, 2)
    x1, y0 = flip(second, 1), flip(first, 2)

    pair, twice, norm = stats(where, points, centroids, lines)
    pair, x0, y1 = lax.optimization_barrier((pair, x0, y1))
    pairs = [pair] + [flip_core(pair, rc) for rc in range(1, cores)]
    tail = max(8, 2 * cores)
    lse, log_evidence, pack_x, pack_y = call(
        functools.partial(lse_kernel, cores, local_cent * cores),
        (f32(2 * cores, half), f32(rows // LANES, LANES), f32(half + tail, width), f32(half + tail, width)),
        [VMEM] * (2 + cores),
        (x0, y1, *pairs),
        "lse",
    )
    d0, d1, lse_d = flip(pack_x, 2), flip(pack_y, 1), flip(lse, 3)

    acc_shape, cnt_shape = f32(share, width), f32(share, min(LANES, half))
    acc, cnt = call(
        functools.partial(own_kernel, cores),
        (acc_shape, cnt_shape),
        [VMEM] * 4,
        (points, twice, norm, lse),
        "own",
        flops=4 * share * width * rows,
    )
    early = with_siblings((x0, y1))
    early, late, acc, cnt, lse_d = lax.optimization_barrier(
        (early, (x1, y0, d0, d1), acc, cnt, lse_d)
    )
    _, _, d0, d1 = late
    late = with_siblings(late)
    acc, cnt = call(
        functools.partial(near_kernel, cores),
        (acc_shape, cnt_shape),
        [SMEM] + [VMEM] * (6 + 2 * cores),
        (where, twice, norm, acc, cnt, d0, d1, *early),
        "near",
        flops=4 * share * width * rows,
        aliases={3: 0, 4: 1},
    )
    sums = call(
        functools.partial(far_kernel, cores, order),
        [f32(size + 8, width)] * lines,
        [SMEM] + [VMEM] * (5 + 4 * cores),
        (where, twice, norm, acc, cnt, lse_d, *late),
        "far",
        scratch=[
            pltpu.VMEM((share, width), jnp.float32),
            pltpu.VMEM((share, min(LANES, half)), jnp.float32),
        ],
        flops=4 * share * width * 2 * rows,
    )

    def reduced(way, steps):
        moving = sums[way * steps % lines]
        for s in range(steps, 0, -1):
            moving = ring(moving, way)
            if s > 1:
                mine = sums[way * (s - 1) % lines]
                moving = call(add_kernel, f32(size + 8, width), [VMEM] * 2, (mine, moving), "add")
        return moving

    done = call(
        finish_kernel,
        f32(size + 8, width),
        [SMEM] + [VMEM] * 4,
        (where, twice, sums[0], reduced(1, lines // 2), reduced(-1, lines // 2 - 1)),
        "finish",
    )

    got = {(0, 0): done}
    got[0, -1], got[1, 0], got[2, 0] = lax.optimization_barrier(
        (ring(done, 1), flip(done, 1), flip(done, 2))
    )
    got[3, 0] = flip(got[1, 0], 2)
    for s in range(2, lines // 2 + 1):
        got[0, -s] = ring(got[0, 1 - s], 1)
    for s in range(1, lines // 2):
        got[0, s] = ring(got[0, s - 1], -1)
    steps = sorted((s for b, s in got if b == 0 and s), key=lambda s: (abs(s), s))
    for s in steps:
        got[1, s] = flip(got[0, s], 1)
        got[2, s] = flip(got[0, s], 2)
    for s in steps:
        if abs(s) == 1:
            got[3, s] = ring(got[3, 0], -s)
        else:
            got[3, s] = flip(got[2, s], 1)
    last = [(3, 1), (2, 1), (3, -lines // 2), (1, -lines // 2), (3, -1)]
    groups = ([k for k in got if k not in last], last)
    new = counts = None
    for later, names in enumerate(groups):
        args = [where] + [got[k] for k in names]
        if later:
            args += [counts, new]
        new, counts = call(
            functools.partial(place_kernel, names, order, later),
            (f32(local_cent, width), f32(local_cent // LANES, LANES)),
            [SMEM] + [VMEM] * len(names) + [VMEM, ANY][: 2 * later],
            args,
            "place_late" if later else "place_early",
            out_specs=(ANY, VMEM),
            scratch=[pltpu.SemaphoreType.DMA((len(names),))],
            aliases={len(args) - 1: 0} if later else {},
        )
    return new, counts.reshape(-1), log_evidence.reshape(-1)


def solution(mesh):
    n, cores = mesh.shape["dp"], mesh.shape["cent"]
    return jax.shard_map(
        functools.partial(body, n, cores),
        mesh=mesh,
        in_specs=(P("dp", None), P("cent", None)),
        out_specs=(P("cent", None), P("cent"), P("dp")),
        check_vma=False,
    )
```

```python
import functools
import math

import jax
import jax.numpy as jnp
from jax import lax
from jax.experimental import pallas as pl
from jax.experimental.pallas import tpu as pltpu
from jax.sharding import PartitionSpec as P

prior_mass = 0.5
VMEM_LIMIT = 48 * 1024 * 1024
LANES = 128
NT = (((1,), (1,)), ((), ()))
NN = (((1,), (0,)), ((), ()))
VMEM = pl.BlockSpec(memory_space=pltpu.VMEM)
SMEM = pl.BlockSpec(memory_space=pltpu.SMEM)
ANY = pl.BlockSpec(memory_space=pl.ANY)
HBM = pl.BlockSpec(memory_space=pltpu.HBM)


def f32(*shape):
    return jax.ShapeDtypeStruct(shape, jnp.float32)


def call(kernel, out_shape, in_specs, args, name, out_specs=None, scratch=(), flops=0, aliases={}):
    return pl.pallas_call(
        kernel,
        out_shape=out_shape,
        in_specs=in_specs,
        out_specs=jax.tree.map(lambda _: VMEM, out_shape) if out_specs is None else out_specs,
        scratch_shapes=list(scratch),
        input_output_aliases=aliases,
        compiler_params=pltpu.CompilerParams(vmem_limit_bytes=VMEM_LIMIT),
        cost_estimate=pl.CostEstimate(
            flops=flops,
            bytes_accessed=sum(a.size * a.dtype.itemsize for a in args),
            transcendentals=0,
        ),
        name=name,
    )(*args)


def open_kernel(where_ref, points_ref, first_ref, second_ref, raw_ref, sem):
    half = first_ref.shape[0]
    start = pl.multiple_of(where_ref[1] * (2 * half), 2 * half)
    copy = pltpu.make_async_copy(points_ref.at[pl.ds(start, 2 * half), :], raw_ref, sem)
    copy.start()
    copy.wait()
    first_ref[...] = raw_ref[:half, :].astype(jnp.float32)
    second_ref[...] = raw_ref[half:, :].astype(jnp.float32)


def widen(norm, width):
    if width <= norm.shape[1]:
        return norm[:, :width]
    return jnp.concatenate([norm] * (width // norm.shape[1]), axis=1)


def norms(c):
    c = c.astype(jnp.float32)
    return jnp.broadcast_to(jnp.sum(c * c, axis=1, keepdims=True), (c.shape[0], LANES))


def stats_kernel(lines, where_ref, points_ref, c_ref, out_ref, twice_ref, norm_ref, all_norm_ref):
    rows, local = points_ref.shape[0], c_ref.shape[0]
    chunk = local // lines
    tile, size = min(256, rows), chunk // 4
    kept = pl.multiple_of(lax.rem(where_ref[0], 4) * size, size)
    for l in range(lines):
        c = c_ref[l * chunk : (l + 1) * chunk, :]
        all_norm_ref[...] = norms(c)
        twice = c + c
        for start in range(0, rows, tile):
            at = slice(start, start + tile)
            dots = lax.dot_general(twice, points_ref[at, :], NT, preferred_element_type=jnp.float32)
            score = dots - widen(all_norm_ref[...], tile)
            top = jnp.max(score, axis=0, keepdims=True)
            total = jnp.sum(jnp.exp(score - top), axis=0, keepdims=True)
            if l:
                old_top, old_total = out_ref[0:1, at], out_ref[1:2, at]
                new_top = jnp.maximum(old_top, top)
                total = old_total * jnp.exp(old_top - new_top) + total * jnp.exp(top - new_top)
                top = new_top
            out_ref[0:1, at] = top
            out_ref[1:2, at] = total
        mine = c_ref[pl.ds(pl.multiple_of(l * chunk + kept, size), size), :]
        twice_ref[l * size : (l + 1) * size, :] = mine + mine
        norm_ref[l * size : (l + 1) * size, :] = all_norm_ref[pl.ds(kept, size), :]


def stats(where, points, centroids, lines):
    rows, width = points.shape
    local = centroids.shape[0]
    return call(
        functools.partial(stats_kernel, lines),
        (
            f32(2, rows),
            jax.ShapeDtypeStruct((local // 4, width), jnp.bfloat16),
            f32(local // 4, LANES),
        ),
        [SMEM, VMEM, VMEM],
        (where, points, centroids),
        "stats",
        scratch=[pltpu.VMEM((local // lines, LANES), jnp.float32)],
        flops=4 * rows * local * width,
    )


def lse_kernel(cores, every, *refs):
    pair_refs = refs[:cores]
    lse_ref, evidence_ref = refs[cores:]
    half = lse_ref.shape[1]
    top = functools.reduce(jnp.maximum, [p[0:1, :] for p in pair_refs])
    total = functools.reduce(jnp.add, [p[1:2, :] * jnp.exp(p[0:1, :] - top) for p in pair_refs])
    lse = top + jnp.log(total)
    evidence = lse - math.log(every)
    for k in range(evidence_ref.shape[0]):
        evidence_ref[k : k + 1, :] = evidence[:, k * LANES : (k + 1) * LANES]
    for i in range(2 * cores):
        lse_ref[i : i + 1, :] = lse[:, i * half : (i + 1) * half]


def add_block(twice, norm, x, lse, acc_ref, cnt_ref, first):
    dots = lax.dot_general(twice, x, NT, preferred_element_type=jnp.float32)
    score = dots - widen(norm, x.shape[0])
    resp = jnp.exp(score - lse).astype(jnp.bfloat16)
    part = lax.dot_general(resp, x, NN, preferred_element_type=jnp.float32)
    wide = resp.astype(jnp.float32)
    lanes = cnt_ref.shape[1]
    counted = functools.reduce(
        jnp.add, [wide[:, k : k + lanes] for k in range(0, x.shape[0], lanes)]
    )
    if first:
        acc_ref[...] = part
        cnt_ref[...] = counted
    else:
        acc_ref[...] += part
        cnt_ref[...] += counted


def add_pieces(cores, where_ref, twice_ref, norm_ref, refs, whose, acc_ref, cnt_ref):
    for k, (lse_ref, part) in enumerate(whose):
        for rc in range(cores):
            x = refs[k * cores + rc][...].astype(jnp.bfloat16)
            lse = lse_ref[pl.ds(2 * (where_ref[1] ^ rc) + part, 1), :]
            add_block(twice_ref[...], norm_ref[...], x, lse, acc_ref, cnt_ref, False)


def own_kernel(cores, points_ref, twice_ref, norm_ref, lse_ref, acc_ref, cnt_ref):
    half = points_ref.shape[0] // (2 * cores)
    for i in range(2 * cores):
        x = points_ref[i * half : (i + 1) * half, :]
        add_block(twice_ref[...], norm_ref[...], x, lse_ref[i : i + 1, :], acc_ref, cnt_ref, i == 0)


def near_kernel(cores, where_ref, twice_ref, norm_ref, acc_in_ref, cnt_in_ref, lse_x_ref, lse_y_ref, *refs):
    acc_ref, cnt_ref = refs[4 * cores :]
    acc_ref[...] = acc_in_ref[...]
    cnt_ref[...] = cnt_in_ref[...]
    whose = ((lse_x_ref, 0), (lse_y_ref, 1), (lse_x_ref, 1), (lse_y_ref, 0))
    add_pieces(cores, where_ref, twice_ref, norm_ref, refs, whose, acc_ref, cnt_ref)


def far_kernel(cores, order, where_ref, twice_ref, norm_ref, acc_in_ref, cnt_in_ref, lse_ref, *refs):
    lines = len(order)
    out_refs = refs[2 * cores : 2 * cores + lines]
    acc_ref, cnt_ref = refs[2 * cores + lines :]
    acc_ref[...] = acc_in_ref[...]
    cnt_ref[...] = cnt_in_ref[...]
    whose = ((lse_ref, 0), (lse_ref, 1))
    add_pieces(cores, where_ref, twice_ref, norm_ref, refs, whose, acc_ref, cnt_ref)
    line = lax.div(where_ref[0], 4)
    width = acc_ref.shape[1]
    size = acc_ref.shape[0] // lines
    for s in range(lines):
        start = pl.multiple_of(ahead(order, line, s) * size, size)
        out_refs[s][0:size, :] = acc_ref[pl.ds(start, size), :]
        turned = jnp.sum(cnt_ref[pl.ds(start, size), :].T, axis=0, keepdims=True)
        if size < width:
            turned = jnp.concatenate([turned, jnp.zeros((1, width - size), jnp.float32)], axis=1)
        out_refs[s][size : size + 8, :] = jnp.broadcast_to(turned, (8, width))


def ahead(order, line, steps):
    n = len(order)
    return functools.reduce(
        jnp.add,
        [jnp.where(line == order[p], order[(p + steps) % n], 0) for p in range(n)],
    )


def add_kernel(a_ref, b_ref, out_ref):
    out_ref[...] = a_ref[...] + b_ref[...]


def finish_kernel(where_ref, twice_ref, mine_ref, first_ref, second_ref, out_ref):
    size, width = out_ref.shape[0] - 8, out_ref.shape[1]
    start = pl.multiple_of(lax.div(where_ref[0], 4) * size, size)
    c = 0.5 * twice_ref[pl.ds(start, size), :].astype(jnp.float32)
    total = mine_ref[...] + first_ref[...] + second_ref[...]
    counts = total[size:, :]
    column = counts.T[:size, 0:1]
    out_ref[0:size, :] = (total[:size, :] + prior_mass * c) / (column + prior_mass)
    row = lax.broadcasted_iota(jnp.int32, (8, LANES), 0)
    spread = jnp.zeros((8, LANES), jnp.float32)
    for k in range(size // LANES):
        spread = jnp.where(row == k, counts[:, k * LANES : (k + 1) * LANES], spread)
    out_ref[size:, :] = jnp.concatenate([spread] * (width // LANES), axis=1)


def place_kernel(names, order, later, where_ref, *refs):
    count, lines = len(names), len(order)
    block_refs = refs[:count]
    new_ref, counts_ref, sems = refs[-3:]
    size = block_refs[0].shape[0] - 8
    plane, line = lax.rem(where_ref[0], 4), lax.div(where_ref[0], 4)
    each = size // LANES
    places = [ahead(order, line, steps) * 4 + (plane ^ bits) for bits, steps in names]
    copies = []
    for i in range(count):
        at = pl.multiple_of(places[i] * size, size)
        copies.append(
            pltpu.make_async_copy(block_refs[i].at[0:size, :], new_ref.at[pl.ds(at, size), :], sems.at[i])
        )
        copies[-1].start()
    if later:
        counts_ref[...] = refs[count][...]
    for i in range(count):
        for k in range(each):
            counts_ref[pl.ds(places[i] * each + k, 1), :] = block_refs[i][size + k : size + k + 1, 0:LANES]
    for copy in copies:
        copy.wait()


def body(n, cores, points, centroids):
    rows, width = points.shape
    local_cent = centroids.shape[0]
    lines = n // 4
    half = rows // (2 * cores)
    share = local_cent // 4
    size = share // lines
    order = tuple(range(0, lines, 2)) + tuple(range(1, lines, 2))[::-1]
    where = jnp.stack([lax.axis_index("dp"), lax.axis_index("cent")]).astype(jnp.int32)

    def flip(x, bits):
        return lax.ppermute(x, "dp", [(i, i ^ bits) for i in range(n)])

    def flip_core(x, bits):
        return lax.ppermute(x, "cent", [(i, i ^ bits) for i in range(cores)])

    def ring(x, way):
        pairs = [(order[p], order[(p + way) % lines]) for p in range(lines)]
        return lax.ppermute(x, "dp", [(4 * a + i, 4 * b + i) for a, b in pairs for i in range(4)])

    def with_siblings(pieces):
        return [a if rc == 0 else flip_core(a, rc) for a in pieces for rc in range(cores)]

    first, second = call(
        open_kernel,
        (f32(half, width), f32(half, width)),
        [SMEM, HBM],
        (where, points),
        "open",
        scratch=[pltpu.VMEM((2 * half, width), points.dtype), pltpu.SemaphoreType.DMA(())],
    )
    x0, y1 = flip(first, 1), flip(second, 2)
    x1, y0 = flip(second, 1), flip(first, 2)

    pair, twice, norm = stats(where, points, centroids, lines)
    pair, x0, y1 = lax.optimization_barrier((pair, x0, y1))
    d0, d1 = flip(x0, 2), flip(y1, 1)
    pairs = [pair] + [flip_core(pair, rc) for rc in range(1, cores)]
    lse, log_evidence = call(
        functools.partial(lse_kernel, cores, local_cent * cores),
        (f32(2 * cores, half), f32(rows // LANES, LANES)),
        [VMEM] * cores,
        pairs,
        "lse",
    )
    lse_x, lse_y, lse_d = flip(lse, 1), flip(lse, 2), flip(lse, 3)

    acc_shape, cnt_shape = f32(share, width), f32(share, min(LANES, half))
    acc, cnt = call(
        functools.partial(own_kernel, cores),
        (acc_shape, cnt_shape),
        [VMEM] * 4,
        (points, twice, norm, lse),
        "own",
        flops=4 * share * width * rows,
    )
    near = with_siblings((x0, y1, x1, y0))
    d0, d1, acc, cnt, lse_x, lse_y, lse_d = lax.optimization_barrier(
        (d0, d1, acc, cnt, lse_x, lse_y, lse_d)
    )
    acc, cnt = call(
        functools.partial(near_kernel, cores),
        (acc_shape, cnt_shape),
        [SMEM] + [VMEM] * (6 + 4 * cores),
        (where, twice, norm, acc, cnt, lse_x, lse_y, *near),
        "near",
        flops=4 * share * width * 2 * rows,
        aliases={3: 0, 4: 1},
    )
    sums = call(
        functools.partial(far_kernel, cores, order),
        [f32(size + 8, width)] * lines,
        [SMEM] + [VMEM] * (5 + 2 * cores),
        (where, twice, norm, acc, cnt, lse_d, *with_siblings((d0, d1))),
        "far",
        scratch=[
            pltpu.VMEM((share, width), jnp.float32),
            pltpu.VMEM((share, min(LANES, half)), jnp.float32),
        ],
        flops=4 * share * width * rows,
    )

    def reduced(way, steps):
        moving = sums[way * steps % lines]
        for s in range(steps, 0, -1):
            moving = ring(moving, way)
            if s > 1:
                mine = sums[way * (s - 1) % lines]
                moving = call(add_kernel, f32(size + 8, width), [VMEM] * 2, (mine, moving), "add")
        return moving

    done = call(
        finish_kernel,
        f32(size + 8, width),
        [SMEM] + [VMEM] * 4,
        (where, twice, sums[0], reduced(1, lines // 2), reduced(-1, lines // 2 - 1)),
        "finish",
    )

    got = {(0, 0): done}
    chains = {}

    def send(chain, target, source, move, *how):
        x = got[source]
        if chain in chains:
            x, chains[chain] = lax.optimization_barrier((x, got[chains[chain]]))[0], None
        got[target] = move(x, *how)
        chains[chain] = target

    steps = [-s for s in range(1, lines // 2 + 1)] + list(range(1, lines // 2))
    for s in steps:
        send("z", (0, s), (0, s + 1 if s < 0 else s - 1), ring, 1 if s < 0 else -1)
    send("x", (1, 0), (0, 0), flip, 1)
    send("y", (2, 0), (0, 0), flip, 2)
    send("y", (3, 0), (1, 0), flip, 2)
    for s in steps:
        send("x", (1, s), (0, s), flip, 1)
        send("y", (2, s), (0, s), flip, 2)
    for s in steps:
        if abs(s) == 1:
            send("z", (3, s), (3, 0), ring, -s)
        else:
            send("x", (3, s), (2, s), flip, 1)
    late = [chains["x"], chains["y"], chains["z"]]
    middle = [(2, -2), (1, 1), (3, -1), (1, -2), (2, -1)]
    groups = ([k for k in got if k not in middle + late], middle, late)
    new = counts = None
    for later, names in enumerate(groups):
        args = [where] + [got[k] for k in names]
        if later:
            args += [counts, new]
        new, counts = call(
            functools.partial(place_kernel, names, order, later),
            (f32(local_cent, width), f32(local_cent // LANES, LANES)),
            [SMEM] + [VMEM] * len(names) + ([VMEM, ANY] if later else []),
            args,
            ("place_early", "place_middle", "place_late")[later],
            out_specs=(ANY, VMEM),
            scratch=[pltpu.SemaphoreType.DMA((len(names),))],
            aliases={len(args) - 1: 0} if later else {},
        )
    return new, counts.reshape(-1), log_evidence.reshape(-1)


def solution(mesh):
    n, cores = mesh.shape["dp"], mesh.shape["cent"]
    return jax.shard_map(
        functools.partial(body, n, cores),
        mesh=mesh,
        in_specs=(P("dp", None), P("cent", None)),
        out_specs=(P("cent", None), P("cent"), P("dp")),
        check_vma=False,
    )
```

```python
import functools
import math

import jax
import jax.numpy as jnp
from jax import lax
from jax.experimental import pallas as pl
from jax.experimental.pallas import tpu as pltpu
from jax.sharding import PartitionSpec as P

prior_mass = 0.5
VMEM_LIMIT = 48 * 1024 * 1024
LANES = 128
NT = (((1,), (1,)), ((), ()))
NN = (((1,), (0,)), ((), ()))
VMEM = pl.BlockSpec(memory_space=pltpu.VMEM)
SMEM = pl.BlockSpec(memory_space=pltpu.SMEM)
ANY = pl.BlockSpec(memory_space=pl.ANY)
HBM = pl.BlockSpec(memory_space=pltpu.HBM)


def f32(*shape):
    return jax.ShapeDtypeStruct(shape, jnp.float32)


def call(kernel, out_shape, in_specs, args, name, out_specs=None, scratch=(), flops=0, aliases={}):
    return pl.pallas_call(
        kernel,
        out_shape=out_shape,
        in_specs=in_specs,
        out_specs=jax.tree.map(lambda _: VMEM, out_shape) if out_specs is None else out_specs,
        scratch_shapes=list(scratch),
        input_output_aliases=aliases,
        compiler_params=pltpu.CompilerParams(vmem_limit_bytes=VMEM_LIMIT),
        cost_estimate=pl.CostEstimate(
            flops=flops,
            bytes_accessed=sum(a.size * a.dtype.itemsize for a in args),
            transcendentals=0,
        ),
        name=name,
    )(*args)


def open_kernel(where_ref, points_ref, first_ref, second_ref, raw_ref, sem):
    half = first_ref.shape[0]
    start = pl.multiple_of(where_ref[1] * (2 * half), 2 * half)
    copy = pltpu.make_async_copy(points_ref.at[pl.ds(start, 2 * half), :], raw_ref, sem)
    copy.start()
    copy.wait()
    first_ref[...] = raw_ref[:half, :].astype(jnp.float32)
    second_ref[...] = raw_ref[half:, :].astype(jnp.float32)


def widen(norm, width):
    if width <= norm.shape[1]:
        return norm[:, :width]
    return jnp.concatenate([norm] * (width // norm.shape[1]), axis=1)


def norms(c):
    c = c.astype(jnp.float32)
    return jnp.broadcast_to(jnp.sum(c * c, axis=1, keepdims=True), (c.shape[0], LANES))


def stats_kernel(lines, where_ref, points_ref, c_ref, out_ref, twice_ref, norm_ref, all_norm_ref):
    rows, local = points_ref.shape[0], c_ref.shape[0]
    chunk = local // lines
    tile, size = min(256, rows), chunk // 4
    kept = pl.multiple_of(lax.rem(where_ref[0], 4) * size, size)
    for l in range(lines):
        c = c_ref[l * chunk : (l + 1) * chunk, :]
        all_norm_ref[...] = norms(c)
        twice = c + c
        for start in range(0, rows, tile):
            at = slice(start, start + tile)
            dots = lax.dot_general(twice, points_ref[at, :], NT, preferred_element_type=jnp.float32)
            score = dots - widen(all_norm_ref[...], tile)
            top = jnp.max(score, axis=0, keepdims=True)
            total = jnp.sum(jnp.exp(score - top), axis=0, keepdims=True)
            if l:
                old_top, old_total = out_ref[0:1, at], out_ref[1:2, at]
                new_top = jnp.maximum(old_top, top)
                total = old_total * jnp.exp(old_top - new_top) + total * jnp.exp(top - new_top)
                top = new_top
            out_ref[0:1, at] = top
            out_ref[1:2, at] = total
        mine = c_ref[pl.ds(pl.multiple_of(l * chunk + kept, size), size), :]
        twice_ref[l * size : (l + 1) * size, :] = mine + mine
        norm_ref[l * size : (l + 1) * size, :] = all_norm_ref[pl.ds(kept, size), :]


def stats(where, points, centroids, lines):
    rows, width = points.shape
    local = centroids.shape[0]
    return call(
        functools.partial(stats_kernel, lines),
        (
            f32(2, rows),
            jax.ShapeDtypeStruct((local // 4, width), jnp.bfloat16),
            f32(local // 4, LANES),
        ),
        [SMEM, VMEM, VMEM],
        (where, points, centroids),
        "stats",
        scratch=[pltpu.VMEM((local // lines, LANES), jnp.float32)],
        flops=4 * rows * local * width,
    )


def lse_kernel(cores, every, x0_ref, y1_ref, *refs):
    pair_refs = refs[:cores]
    lse_ref, evidence_ref, pack_x_ref, pack_y_ref = refs[cores:]
    half = lse_ref.shape[1]
    top = functools.reduce(jnp.maximum, [p[0:1, :] for p in pair_refs])
    total = functools.reduce(jnp.add, [p[1:2, :] * jnp.exp(p[0:1, :] - top) for p in pair_refs])
    lse = top + jnp.log(total)
    evidence = lse - math.log(every)
    for k in range(evidence_ref.shape[0]):
        evidence_ref[k : k + 1, :] = evidence[:, k * LANES : (k + 1) * LANES]
    for i in range(2 * cores):
        lse_ref[i : i + 1, :] = lse[:, i * half : (i + 1) * half]
    for piece_ref, pack_ref in ((x0_ref, pack_x_ref), (y1_ref, pack_y_ref)):
        pack_ref[0:half, :] = piece_ref[...]
        pack_ref[half:, :] = jnp.zeros_like(pack_ref[half:, :])
        pack_ref[half : half + 2 * cores, 0:half] = lse_ref[...]


def weigh(twice, norm, x, lse, lanes):
    dots = lax.dot_general(twice, x, NT, preferred_element_type=jnp.float32)
    score = dots - widen(norm, x.shape[0])
    resp = jnp.exp(score - lse).astype(jnp.bfloat16)
    part = lax.dot_general(resp, x, NN, preferred_element_type=jnp.float32)
    wide = resp.astype(jnp.float32)
    counted = functools.reduce(
        jnp.add, [wide[:, k : k + lanes] for k in range(0, x.shape[0], lanes)]
    )
    return part, counted


def own_kernel(cores, points_ref, twice_ref, norm_ref, lse_ref, acc_ref, cnt_ref):
    half = points_ref.shape[0] // (2 * cores)
    for i in range(2 * cores):
        x = points_ref[i * half : (i + 1) * half, :]
        part, counted = weigh(
            twice_ref[...], norm_ref[...], x, lse_ref[i : i + 1, :], cnt_ref.shape[1]
        )
        if i == 0:
            acc_ref[...] = part
            cnt_ref[...] = counted
        else:
            acc_ref[...] += part
            cnt_ref[...] += counted


def near_rows(cores, half, core, refs, d0_ref, d1_ref):
    whose = ((d1_ref, 0), (d0_ref, 1), (d1_ref, 1), (d0_ref, 0))
    for k, (tail_ref, part) in enumerate(whose):
        for rc in range(cores):
            at = half + 2 * (core ^ rc) + part
            yield refs[k * cores + rc], (lambda at=at, tail_ref=tail_ref: tail_ref[pl.ds(at, 1), :][:, 0:half])


def far_rows(cores, half, core, refs, lse_ref):
    for part in range(2):
        for rc in range(cores):
            at = 2 * (core ^ rc) + part
            yield refs[part * cores + rc], (lambda at=at: lse_ref[pl.ds(at, 1), :])


def add_rows(rows, half, twice, norm, acc, cnt):
    for x_ref, lse in rows:
        part, counted = weigh(twice, norm, x_ref[0:half, :].astype(jnp.bfloat16), lse(), cnt.shape[1])
        acc, cnt = acc + part, cnt + counted
    return acc, cnt


def store_sums(out_ref, acc, cnt):
    size, width = acc.shape
    turned = jnp.sum(cnt.T, axis=0, keepdims=True)
    if size < width:
        turned = jnp.concatenate([turned, jnp.zeros((1, width - size), jnp.float32)], axis=1)
    out_ref[0:size, :] = acc
    out_ref[size : size + 8, :] = jnp.broadcast_to(turned, (8, width))


def lead_kernel(cores, order, half, where_ref, twice_ref, norm_ref, acc_ref, cnt_ref, *refs):
    out_acc_ref, out_cnt_ref = refs[-2:]
    near, (d0_ref, d1_ref) = refs[: 4 * cores], refs[4 * cores : 4 * cores + 2]
    size = out_acc_ref.shape[0]
    place = ahead(order, lax.div(where_ref[0], 4), len(order) // 2)
    at = pl.ds(pl.multiple_of(place * size, size), size)
    out_acc_ref[...], out_cnt_ref[...] = add_rows(
        near_rows(cores, half, where_ref[1], near, d0_ref, d1_ref),
        half,
        twice_ref[at, :],
        norm_ref[at, :],
        acc_ref[at, :],
        cnt_ref[at, :],
    )


def block_sums(cores, order, half, steps, where_ref, twice_ref, norm_ref, acc_ref, cnt_ref, lse_ref, near, far, out_ref):
    size = out_ref.shape[0] - 8
    place = ahead(order, lax.div(where_ref[0], 4), steps)
    at = pl.ds(pl.multiple_of(place * size, size), size)
    twice, norm = twice_ref[at, :], norm_ref[at, :]
    acc, cnt = add_rows(
        near_rows(cores, half, where_ref[1], near, far[0], far[cores]),
        half,
        twice,
        norm,
        acc_ref[at, :],
        cnt_ref[at, :],
    )
    acc, cnt = add_rows(far_rows(cores, half, where_ref[1], far, lse_ref), half, twice, norm, acc, cnt)
    store_sums(out_ref, acc, cnt)


def first_kernel(cores, order, half, ahead_steps, where_ref, twice_ref, norm_ref, acc_ref, cnt_ref, lse_ref, lead_acc_ref, lead_cnt_ref, *refs):
    near, far = refs[: 4 * cores], refs[4 * cores : 6 * cores]
    out_refs = refs[6 * cores :]
    size = lead_acc_ref.shape[0]
    place = ahead(order, lax.div(where_ref[0], 4), len(order) // 2)
    at = pl.ds(pl.multiple_of(place * size, size), size)
    acc, cnt = add_rows(
        far_rows(cores, half, where_ref[1], far, lse_ref),
        half,
        twice_ref[at, :],
        norm_ref[at, :],
        lead_acc_ref[...],
        lead_cnt_ref[...],
    )
    store_sums(out_refs[0], acc, cnt)

    @pl.when(lax.rem(where_ref[1], 2) == 1)
    def _():
        for steps, out_ref in zip(ahead_steps, out_refs[1:]):
            block_sums(cores, order, half, steps, where_ref, twice_ref, norm_ref, acc_ref, cnt_ref, lse_ref, near, far, out_ref)


def rest_kernel(cores, order, half, made, missing, where_ref, twice_ref, norm_ref, acc_ref, cnt_ref, lse_ref, *refs):
    near, far = refs[: 4 * cores], refs[4 * cores : 6 * cores]
    made_refs = refs[6 * cores : 6 * cores + len(made)]
    out_refs = refs[6 * cores + len(made) :]
    given = (where_ref, twice_ref, norm_ref, acc_ref, cnt_ref, lse_ref, near, far)
    odd = lax.rem(where_ref[1], 2) == 1

    @pl.when(odd)
    def _():
        for made_ref, out_ref in zip(made_refs, out_refs):
            out_ref[...] = made_ref[...]

    @pl.when(jnp.logical_not(odd))
    def _():
        for steps, out_ref in zip(made, out_refs):
            block_sums(cores, order, half, steps, *given, out_ref)

    for steps, out_ref in zip(missing, out_refs[len(made) :]):
        block_sums(cores, order, half, steps, *given, out_ref)


def ahead(order, line, steps):
    n = len(order)
    return functools.reduce(
        jnp.add,
        [jnp.where(line == order[p], order[(p + steps) % n], 0) for p in range(n)],
    )


def add_kernel(a_ref, b_ref, out_ref):
    out_ref[...] = a_ref[...] + b_ref[...]


def finish_kernel(where_ref, twice_ref, mine_ref, first_ref, second_ref, out_ref):
    size, width = out_ref.shape[0] - 8, out_ref.shape[1]
    start = pl.multiple_of(lax.div(where_ref[0], 4) * size, size)
    c = 0.5 * twice_ref[pl.ds(start, size), :].astype(jnp.float32)
    total = mine_ref[...] + first_ref[...] + second_ref[...]
    counts = total[size:, :]
    column = counts.T[:size, 0:1]
    out_ref[0:size, :] = (total[:size, :] + prior_mass * c) / (column + prior_mass)
    row = lax.broadcasted_iota(jnp.int32, (8, LANES), 0)
    spread = jnp.zeros((8, LANES), jnp.float32)
    for k in range(size // LANES):
        spread = jnp.where(row == k, counts[:, k * LANES : (k + 1) * LANES], spread)
    out_ref[size:, :] = jnp.concatenate([spread] * (width // LANES), axis=1)


def place_kernel(names, order, later, where_ref, *refs):
    count, lines = len(names), len(order)
    block_refs = refs[:count]
    new_ref, counts_ref, sems = refs[-3:]
    size = block_refs[0].shape[0] - 8
    plane, line = lax.rem(where_ref[0], 4), lax.div(where_ref[0], 4)
    each = size // LANES
    places = [ahead(order, line, steps) * 4 + (plane ^ bits) for bits, steps in names]
    copies = []
    for i in range(count):
        at = pl.multiple_of(places[i] * size, size)
        copies.append(
            pltpu.make_async_copy(block_refs[i].at[0:size, :], new_ref.at[pl.ds(at, size), :], sems.at[i])
        )
        copies[-1].start()
    if later:
        counts_ref[...] = refs[count][...]
    for i in range(count):
        for k in range(each):
            counts_ref[pl.ds(places[i] * each + k, 1), :] = block_refs[i][size + k : size + k + 1, 0:LANES]
    for copy in copies:
        copy.wait()


def body(n, cores, points, centroids):
    rows, width = points.shape
    local_cent = centroids.shape[0]
    lines = n // 4
    half = rows // (2 * cores)
    share = local_cent // 4
    size = share // lines
    order = tuple(range(0, lines, 2)) + tuple(range(1, lines, 2))[::-1]
    where = jnp.stack([lax.axis_index("dp"), lax.axis_index("cent")]).astype(jnp.int32)

    def flip(x, bits):
        return lax.ppermute(x, "dp", [(i, i ^ bits) for i in range(n)])

    def flip_core(x, bits):
        return lax.ppermute(x, "cent", [(i, i ^ bits) for i in range(cores)])

    def ring(x, way):
        pairs = [(order[p], order[(p + way) % lines]) for p in range(lines)]
        return lax.ppermute(x, "dp", [(4 * a + i, 4 * b + i) for a, b in pairs for i in range(4)])

    def with_siblings(pieces):
        return [a if rc == 0 else flip_core(a, rc) for a in pieces for rc in range(cores)]

    first, second = call(
        open_kernel,
        (f32(half, width), f32(half, width)),
        [SMEM, HBM],
        (where, points),
        "open",
        scratch=[pltpu.VMEM((2 * half, width), points.dtype), pltpu.SemaphoreType.DMA(())],
    )
    x0, y1 = flip(first, 1), flip(second, 2)
    x1, y0 = flip(second, 1), flip(first, 2)

    pair, twice, norm = stats(where, points, centroids, lines)
    pair, x0, y1 = lax.optimization_barrier((pair, x0, y1))
    pairs = [pair] + [flip_core(pair, rc) for rc in range(1, cores)]
    tail = max(8, 2 * cores)
    lse, log_evidence, pack_x, pack_y = call(
        functools.partial(lse_kernel, cores, local_cent * cores),
        (f32(2 * cores, half), f32(rows // LANES, LANES), f32(half + tail, width), f32(half + tail, width)),
        [VMEM] * (2 + cores),
        (x0, y1, *pairs),
        "lse",
    )
    d0, d1 = flip(pack_x, 2), flip(pack_y, 1)

    lanes = min(LANES, half)
    acc, cnt = call(
        functools.partial(own_kernel, cores),
        (f32(share, width), f32(share, lanes)),
        [VMEM] * 4,
        (points, twice, norm, lse),
        "own",
        flops=4 * share * width * rows,
    )
    near = with_siblings((x0, y1, x1, y0))
    lse, acc, cnt = lax.optimization_barrier((lse, acc, cnt))
    lse_d = flip(lse, 3)
    near, d0, d1, acc, cnt, lse_d = lax.optimization_barrier((near, d0, d1, acc, cnt, lse_d))
    lead = call(
        functools.partial(lead_kernel, cores, order, half),
        (f32(size, width), f32(size, lanes)),
        [SMEM] + [VMEM] * (6 + 4 * cores),
        (where, twice, norm, acc, cnt, *near, d0, d1),
        "lead",
        flops=4 * size * width * 2 * rows,
    )
    given = (where, twice, norm, acc, cnt, lse_d)
    rows_given = (*near, *with_siblings((d0, d1)))
    block_sum = f32(size + 8, width)
    turn = lines // 2
    others = [s % lines for s in range(-1, -turn, -1)] + list(range(turn - 1, -1, -1))
    made, missing = others[:2], others[2:]
    first, *made_sums = call(
        functools.partial(first_kernel, cores, order, half, made),
        [block_sum] * 3,
        [SMEM] + [VMEM] * (7 + 6 * cores),
        (*given, *lead, *rows_given),
        "first",
        flops=4 * size * width * rows,
    )
    rest = call(
        functools.partial(rest_kernel, cores, order, half, made, missing),
        [block_sum] * (lines - 1),
        [SMEM] + [VMEM] * (7 + 6 * cores),
        (*given, *rows_given, *made_sums),
        "rest",
        flops=4 * (share - size) * width * 3 * rows,
    )
    sums = {turn: first, **dict(zip(others, rest))}

    def reduced(way, steps, moving):
        for s in range(steps, 0, -1):
            moving = ring(moving, way)
            if s > 1:
                mine = sums[way * (s - 1) % lines]
                moving = call(add_kernel, block_sum, [VMEM] * 2, (mine, moving), "add")
        return moving

    ahead_sum = reduced(1, turn, first)
    behind_sum = reduced(-1, turn - 1, sums[(1 - turn) % lines])
    done = call(
        finish_kernel,
        block_sum,
        [SMEM] + [VMEM] * 4,
        (where, twice, sums[0], ahead_sum, behind_sum),
        "finish",
    )

    got = {(0, 0): done}
    chains = {}

    def send(chain, target, source, move, *how):
        x = got[source]
        if chain in chains:
            x, chains[chain] = lax.optimization_barrier((x, got[chains[chain]]))[0], None
        got[target] = move(x, *how)
        chains[chain] = target

    steps = [-s for s in range(1, lines // 2 + 1)] + list(range(1, lines // 2))
    for s in steps:
        send("z", (0, s), (0, s + 1 if s < 0 else s - 1), ring, 1 if s < 0 else -1)
    send("x", (1, 0), (0, 0), flip, 1)
    send("y", (2, 0), (0, 0), flip, 2)
    send("y", (3, 0), (1, 0), flip, 2)
    for s in steps:
        send("x", (1, s), (0, s), flip, 1)
        send("y", (2, s), (0, s), flip, 2)
    for s in steps:
        if abs(s) == 1:
            send("z", (3, s), (3, 0), ring, -s)
        else:
            send("x", (3, s), (2, s), flip, 1)
    late = [chains["x"], chains["y"], chains["z"]]
    middle = [(2, -2), (1, 1), (3, -1), (1, -2), (2, -1)]
    groups = ([k for k in got if k not in middle + late], middle, late)
    new = counts = None
    for later, names in enumerate(groups):
        args = [where] + [got[k] for k in names]
        if later:
            args += [counts, new]
        new, counts = call(
            functools.partial(place_kernel, names, order, later),
            (f32(local_cent, width), f32(local_cent // LANES, LANES)),
            [SMEM] + [VMEM] * len(names) + ([VMEM, ANY] if later else []),
            args,
            ("place_early", "place_middle", "place_late")[later],
            out_specs=(ANY, VMEM),
            scratch=[pltpu.SemaphoreType.DMA((len(names),))],
            aliases={len(args) - 1: 0} if later else {},
        )
    return new, counts.reshape(-1), log_evidence.reshape(-1)


def solution(mesh):
    n, cores = mesh.shape["dp"], mesh.shape["cent"]
    return jax.shard_map(
        functools.partial(body, n, cores),
        mesh=mesh,
        in_specs=(P("dp", None), P("cent", None)),
        out_specs=(P("cent", None), P("cent"), P("dp")),
        check_vma=False,
    )
```

```python
import functools
import math

import jax
import jax.numpy as jnp
from jax import lax
from jax.experimental import pallas as pl
from jax.experimental.pallas import tpu as pltpu
from jax.sharding import PartitionSpec as P

prior_mass = 0.5
VMEM_LIMIT = 48 * 1024 * 1024
LANES = 128
NT = (((1,), (1,)), ((), ()))
NN = (((1,), (0,)), ((), ()))
VMEM = pl.BlockSpec(memory_space=pltpu.VMEM)
SMEM = pl.BlockSpec(memory_space=pltpu.SMEM)
ANY = pl.BlockSpec(memory_space=pl.ANY)
HBM = pl.BlockSpec(memory_space=pltpu.HBM)


def f32(*shape):
    return jax.ShapeDtypeStruct(shape, jnp.float32)


def call(kernel, out_shape, in_specs, args, name, out_specs=None, scratch=(), flops=0, aliases={}):
    return pl.pallas_call(
        kernel,
        out_shape=out_shape,
        in_specs=in_specs,
        out_specs=jax.tree.map(lambda _: VMEM, out_shape) if out_specs is None else out_specs,
        scratch_shapes=list(scratch),
        input_output_aliases=aliases,
        compiler_params=pltpu.CompilerParams(vmem_limit_bytes=VMEM_LIMIT),
        cost_estimate=pl.CostEstimate(
            flops=flops,
            bytes_accessed=sum(a.size * a.dtype.itemsize for a in args),
            transcendentals=0,
        ),
        name=name,
    )(*args)


def open_kernel(where_ref, points_ref, first_ref, second_ref, raw_ref, sem):
    half = first_ref.shape[0]
    start = pl.multiple_of(where_ref[1] * (2 * half), 2 * half)
    copy = pltpu.make_async_copy(points_ref.at[pl.ds(start, 2 * half), :], raw_ref, sem)
    copy.start()
    copy.wait()
    first_ref[...] = raw_ref[:half, :].astype(jnp.float32)
    second_ref[...] = raw_ref[half:, :].astype(jnp.float32)


def widen(norm, width):
    if width <= norm.shape[1]:
        return norm[:, :width]
    return jnp.concatenate([norm] * (width // norm.shape[1]), axis=1)


def norms(c):
    c = c.astype(jnp.float32)
    return jnp.broadcast_to(jnp.sum(c * c, axis=1, keepdims=True), (c.shape[0], LANES))


def stats_kernel(lines, where_ref, points_ref, c_ref, out_ref, twice_ref, norm_ref, all_norm_ref):
    rows, local = points_ref.shape[0], c_ref.shape[0]
    chunk = local // lines
    tile, size = min(256, rows), chunk // 4
    kept = pl.multiple_of(lax.rem(where_ref[0], 4) * size, size)
    for l in range(lines):
        c = c_ref[l * chunk : (l + 1) * chunk, :]
        all_norm_ref[...] = norms(c)
        twice = c + c
        for start in range(0, rows, tile):
            at = slice(start, start + tile)
            dots = lax.dot_general(twice, points_ref[at, :], NT, preferred_element_type=jnp.float32)
            score = dots - widen(all_norm_ref[...], tile)
            top = jnp.max(score, axis=0, keepdims=True)
            total = jnp.sum(jnp.exp(score - top), axis=0, keepdims=True)
            if l:
                old_top, old_total = out_ref[0:1, at], out_ref[1:2, at]
                new_top = jnp.maximum(old_top, top)
                total = old_total * jnp.exp(old_top - new_top) + total * jnp.exp(top - new_top)
                top = new_top
            out_ref[0:1, at] = top
            out_ref[1:2, at] = total
        mine = c_ref[pl.ds(pl.multiple_of(l * chunk + kept, size), size), :]
        twice_ref[l * size : (l + 1) * size, :] = mine + mine
        norm_ref[l * size : (l + 1) * size, :] = all_norm_ref[pl.ds(kept, size), :]


def stats(where, points, centroids, lines):
    rows, width = points.shape
    local = centroids.shape[0]
    return call(
        functools.partial(stats_kernel, lines),
        (
            f32(2, rows),
            jax.ShapeDtypeStruct((local // 4, width), jnp.bfloat16),
            f32(local // 4, LANES),
        ),
        [SMEM, VMEM, VMEM],
        (where, points, centroids),
        "stats",
        scratch=[pltpu.VMEM((local // lines, LANES), jnp.float32)],
        flops=4 * rows * local * width,
    )


def lse_kernel(cores, every, x0_ref, y1_ref, *refs):
    pair_refs = refs[:cores]
    lse_ref, evidence_ref, pack_x_ref, pack_y_ref = refs[cores:]
    half = lse_ref.shape[1]
    top = functools.reduce(jnp.maximum, [p[0:1, :] for p in pair_refs])
    total = functools.reduce(jnp.add, [p[1:2, :] * jnp.exp(p[0:1, :] - top) for p in pair_refs])
    lse = top + jnp.log(total)
    evidence = lse - math.log(every)
    for k in range(evidence_ref.shape[0]):
        evidence_ref[k : k + 1, :] = evidence[:, k * LANES : (k + 1) * LANES]
    for i in range(2 * cores):
        lse_ref[i : i + 1, :] = lse[:, i * half : (i + 1) * half]
    for piece_ref, pack_ref in ((x0_ref, pack_x_ref), (y1_ref, pack_y_ref)):
        pack_ref[0:half, :] = piece_ref[...]
        pack_ref[half:, :] = jnp.zeros_like(pack_ref[half:, :])
        pack_ref[half : half + 2 * cores, 0:half] = lse_ref[...]


def weigh(twice, norm, x, lse, lanes):
    dots = lax.dot_general(twice, x, NT, preferred_element_type=jnp.float32)
    score = dots - widen(norm, x.shape[0])
    resp = jnp.exp(score - lse).astype(jnp.bfloat16)
    part = lax.dot_general(resp, x, NN, preferred_element_type=jnp.float32)
    wide = resp.astype(jnp.float32)
    counted = functools.reduce(
        jnp.add, [wide[:, k : k + lanes] for k in range(0, x.shape[0], lanes)]
    )
    return part, counted


def own_kernel(cores, points_ref, twice_ref, norm_ref, lse_ref, acc_ref, cnt_ref):
    half = points_ref.shape[0] // (2 * cores)
    for i in range(2 * cores):
        x = points_ref[i * half : (i + 1) * half, :]
        part, counted = weigh(
            twice_ref[...], norm_ref[...], x, lse_ref[i : i + 1, :], cnt_ref.shape[1]
        )
        if i == 0:
            acc_ref[...] = part
            cnt_ref[...] = counted
        else:
            acc_ref[...] += part
            cnt_ref[...] += counted


def near_rows(cores, half, core, refs, d0_ref, d1_ref):
    whose = ((d1_ref, 0), (d0_ref, 1), (d1_ref, 1), (d0_ref, 0))
    for k, (tail_ref, part) in enumerate(whose):
        for rc in range(cores):
            at = half + 2 * (core ^ rc) + part
            yield refs[k * cores + rc], (lambda at=at, tail_ref=tail_ref: tail_ref[pl.ds(at, 1), :][:, 0:half])


def far_rows(cores, half, core, refs, lse_ref):
    for part in range(2):
        for rc in range(cores):
            at = 2 * (core ^ rc) + part
            yield refs[part * cores + rc], (lambda at=at: lse_ref[pl.ds(at, 1), :])


def add_rows(rows, half, twice, norm, acc, cnt):
    for x_ref, lse in rows:
        part, counted = weigh(twice, norm, x_ref[0:half, :].astype(jnp.bfloat16), lse(), cnt.shape[1])
        acc, cnt = acc + part, cnt + counted
    return acc, cnt


def store_sums(out_ref, acc, cnt):
    size, width = acc.shape
    turned = jnp.sum(cnt.T, axis=0, keepdims=True)
    if size < width:
        turned = jnp.concatenate([turned, jnp.zeros((1, width - size), jnp.float32)], axis=1)
    out_ref[0:size, :] = acc
    out_ref[size : size + 8, :] = jnp.broadcast_to(turned, (8, width))


def lead_kernel(cores, order, half, where_ref, twice_ref, norm_ref, acc_ref, cnt_ref, *refs):
    out_acc_ref, out_cnt_ref = refs[-2:]
    near, (d0_ref, d1_ref) = refs[: 4 * cores], refs[4 * cores : 4 * cores + 2]
    size = out_acc_ref.shape[0]
    place = ahead(order, lax.div(where_ref[0], 4), len(order) // 2)
    at = pl.ds(pl.multiple_of(place * size, size), size)
    out_acc_ref[...], out_cnt_ref[...] = add_rows(
        near_rows(cores, half, where_ref[1], near, d0_ref, d1_ref),
        half,
        twice_ref[at, :],
        norm_ref[at, :],
        acc_ref[at, :],
        cnt_ref[at, :],
    )


def block_sums(cores, order, half, steps, where_ref, twice_ref, norm_ref, acc_ref, cnt_ref, lse_ref, near, far, out_ref):
    size = out_ref.shape[0] - 8
    place = ahead(order, lax.div(where_ref[0], 4), steps)
    at = pl.ds(pl.multiple_of(place * size, size), size)
    twice, norm = twice_ref[at, :], norm_ref[at, :]
    acc, cnt = add_rows(
        near_rows(cores, half, where_ref[1], near, far[0], far[cores]),
        half,
        twice,
        norm,
        acc_ref[at, :],
        cnt_ref[at, :],
    )
    acc, cnt = add_rows(far_rows(cores, half, where_ref[1], far, lse_ref), half, twice, norm, acc, cnt)
    store_sums(out_ref, acc, cnt)


def first_kernel(cores, order, half, ahead_steps, where_ref, twice_ref, norm_ref, acc_ref, cnt_ref, lse_ref, lead_acc_ref, lead_cnt_ref, *refs):
    near, far = refs[: 4 * cores], refs[4 * cores : 6 * cores]
    out_refs = refs[6 * cores :]
    size = lead_acc_ref.shape[0]
    place = ahead(order, lax.div(where_ref[0], 4), len(order) // 2)
    at = pl.ds(pl.multiple_of(place * size, size), size)
    acc, cnt = add_rows(
        far_rows(cores, half, where_ref[1], far, lse_ref),
        half,
        twice_ref[at, :],
        norm_ref[at, :],
        lead_acc_ref[...],
        lead_cnt_ref[...],
    )
    store_sums(out_refs[0], acc, cnt)

    @pl.when(lax.rem(where_ref[1], 2) == 1)
    def _():
        for steps, out_ref in zip(ahead_steps, out_refs[1:]):
            block_sums(cores, order, half, steps, where_ref, twice_ref, norm_ref, acc_ref, cnt_ref, lse_ref, near, far, out_ref)


def rest_kernel(cores, order, half, steps, where_ref, twice_ref, norm_ref, acc_ref, cnt_ref, lse_ref, *refs):
    near, far = refs[: 4 * cores], refs[4 * cores : 6 * cores]
    given, out_ref = refs[6 * cores : -1], refs[-1]
    make = functools.partial(
        block_sums, cores, order, half, steps,
        where_ref, twice_ref, norm_ref, acc_ref, cnt_ref, lse_ref, near, far, out_ref,
    )
    if not given:
        make()
        return
    odd = lax.rem(where_ref[1], 2) == 1

    @pl.when(odd)
    def _():
        out_ref[...] = given[0][...]

    pl.when(jnp.logical_not(odd))(make)


def ahead(order, line, steps):
    n = len(order)
    return functools.reduce(
        jnp.add,
        [jnp.where(line == order[p], order[(p + steps) % n], 0) for p in range(n)],
    )


def add_kernel(a_ref, b_ref, out_ref):
    out_ref[...] = a_ref[...] + b_ref[...]


def finish_kernel(where_ref, twice_ref, mine_ref, first_ref, second_ref, out_ref):
    size, width = out_ref.shape[0] - 8, out_ref.shape[1]
    start = pl.multiple_of(lax.div(where_ref[0], 4) * size, size)
    c = 0.5 * twice_ref[pl.ds(start, size), :].astype(jnp.float32)
    total = mine_ref[...] + first_ref[...] + second_ref[...]
    counts = total[size:, :]
    column = counts.T[:size, 0:1]
    out_ref[0:size, :] = (total[:size, :] + prior_mass * c) / (column + prior_mass)
    row = lax.broadcasted_iota(jnp.int32, (8, LANES), 0)
    spread = jnp.zeros((8, LANES), jnp.float32)
    for k in range(size // LANES):
        spread = jnp.where(row == k, counts[:, k * LANES : (k + 1) * LANES], spread)
    out_ref[size:, :] = jnp.concatenate([spread] * (width // LANES), axis=1)


def place_kernel(names, order, later, where_ref, *refs):
    count, lines = len(names), len(order)
    block_refs = refs[:count]
    new_ref, counts_ref, sems = refs[-3:]
    size = block_refs[0].shape[0] - 8
    plane, line = lax.rem(where_ref[0], 4), lax.div(where_ref[0], 4)
    each = size // LANES
    places = [ahead(order, line, steps) * 4 + (plane ^ bits) for bits, steps in names]
    copies = []
    for i in range(count):
        at = pl.multiple_of(places[i] * size, size)
        copies.append(
            pltpu.make_async_copy(block_refs[i].at[0:size, :], new_ref.at[pl.ds(at, size), :], sems.at[i])
        )
        copies[-1].start()
    if later:
        counts_ref[...] = refs[count][...]
    for i in range(count):
        for k in range(each):
            counts_ref[pl.ds(places[i] * each + k, 1), :] = block_refs[i][size + k : size + k + 1, 0:LANES]
    for copy in copies:
        copy.wait()


def body(n, cores, points, centroids):
    rows, width = points.shape
    local_cent = centroids.shape[0]
    lines = n // 4
    half = rows // (2 * cores)
    share = local_cent // 4
    size = share // lines
    order = tuple(range(0, lines, 2)) + tuple(range(1, lines, 2))[::-1]
    where = jnp.stack([lax.axis_index("dp"), lax.axis_index("cent")]).astype(jnp.int32)

    def flip(x, bits):
        return lax.ppermute(x, "dp", [(i, i ^ bits) for i in range(n)])

    def flip_core(x, bits):
        return lax.ppermute(x, "cent", [(i, i ^ bits) for i in range(cores)])

    def ring(x, way):
        pairs = [(order[p], order[(p + way) % lines]) for p in range(lines)]
        return lax.ppermute(x, "dp", [(4 * a + i, 4 * b + i) for a, b in pairs for i in range(4)])

    def with_siblings(pieces):
        return [a if rc == 0 else flip_core(a, rc) for a in pieces for rc in range(cores)]

    first, second = call(
        open_kernel,
        (f32(half, width), f32(half, width)),
        [SMEM, HBM],
        (where, points),
        "open",
        scratch=[pltpu.VMEM((2 * half, width), points.dtype), pltpu.SemaphoreType.DMA(())],
    )
    x0, y1 = flip(first, 1), flip(second, 2)
    x1, y0 = flip(second, 1), flip(first, 2)

    pair, twice, norm = stats(where, points, centroids, lines)
    pairs = [pair] + [flip_core(pair, rc) for rc in range(1, cores)]
    tail = max(8, 2 * cores)
    lse, log_evidence, pack_x, pack_y = call(
        functools.partial(lse_kernel, cores, local_cent * cores),
        (f32(2 * cores, half), f32(rows // LANES, LANES), f32(half + tail, width), f32(half + tail, width)),
        [VMEM] * (2 + cores),
        (x0, y1, *pairs),
        "lse",
    )
    d0, d1 = flip(pack_x, 2), flip(pack_y, 1)

    lanes = min(LANES, half)
    acc, cnt = call(
        functools.partial(own_kernel, cores),
        (f32(share, width), f32(share, lanes)),
        [VMEM] * 4,
        (points, twice, norm, lse),
        "own",
        flops=4 * share * width * rows,
    )
    x0, y1, x1, y0, lse = lax.optimization_barrier((x0, y1, x1, y0, lse))
    near = with_siblings((x0, y1, x1, y0))
    near, d0, d1, acc, cnt = lax.optimization_barrier((near, d0, d1, acc, cnt))
    lse_d = flip(d1[half : half + 2 * cores, :half], 2)
    lead = call(
        functools.partial(lead_kernel, cores, order, half),
        (f32(size, width), f32(size, lanes)),
        [SMEM] + [VMEM] * (6 + 4 * cores),
        (where, twice, norm, acc, cnt, *near, d0, d1),
        "lead",
        flops=4 * size * width * 2 * rows,
    )
    given = (where, twice, norm, acc, cnt, lse_d)
    rows_given = (*near, *with_siblings((d0, d1)))
    block_sum = f32(size + 8, width)
    turn = lines // 2
    forward = list(range(turn - 1, 0, -1))
    backward = [lines - s for s in range(turn - 1, 0, -1)]
    made = (forward + backward)[:2]
    first, *made_sums = call(
        functools.partial(first_kernel, cores, order, half, made),
        [block_sum] * 3,
        [SMEM] + [VMEM] * (7 + 6 * cores),
        (*given, *lead, *rows_given),
        "first",
        flops=4 * size * width * rows,
    )
    made_sums = dict(zip(made, made_sums))

    def sum_of(steps):
        extra = [made_sums[steps]] if steps in made_sums else []
        return call(
            functools.partial(rest_kernel, cores, order, half, steps),
            block_sum,
            [SMEM] + [VMEM] * (5 + 6 * cores + len(extra)),
            (*given, *rows_given, *extra),
            "rest",
            flops=4 * size * width * 3 * rows,
        )

    def plus(a, b):
        return call(add_kernel, block_sum, [VMEM] * 2, (a, b), "add")

    moving = ring(first, 1)
    for s in forward:
        moving = ring(plus(sum_of(s), moving), 1)
    sides = [moving]
    moving = None
    for s in backward:
        mine = sum_of(s)
        mine, sides[0] = lax.optimization_barrier((mine, sides[0]))
        moving = ring(mine if moving is None else plus(mine, moving), -1)
    sides.append(moving)
    done = call(
        finish_kernel,
        block_sum,
        [SMEM] + [VMEM] * 4,
        (where, twice, sum_of(0), *sides),
        "finish",
    )

    got = {(0, 0): done}
    chains = {}

    def send(chain, target, source, move, *how):
        x = got[source]
        if chain in chains:
            x, chains[chain] = lax.optimization_barrier((x, got[chains[chain]]))[0], None
        got[target] = move(x, *how)
        chains[chain] = target

    steps = [-s for s in range(1, lines // 2 + 1)] + list(range(1, lines // 2))
    for s in steps:
        send("z", (0, s), (0, s + 1 if s < 0 else s - 1), ring, 1 if s < 0 else -1)
    send("x", (1, 0), (0, 0), flip, 1)
    send("y", (2, 0), (0, 0), flip, 2)
    send("y", (3, 0), (1, 0), flip, 2)
    for s in steps:
        send("x", (1, s), (0, s), flip, 1)
        send("y", (2, s), (0, s), flip, 2)
    for s in steps:
        if abs(s) == 1:
            send("z", (3, s), (3, 0), ring, -s)
        else:
            send("x", (3, s), (2, s), flip, 1)
    late = [chains["x"], chains["y"], chains["z"]]
    middle = [(2, -2), (1, 1), (3, -1), (1, -2), (2, -1)]
    groups = ([k for k in got if k not in middle + late], middle, late)
    new = counts = None
    for later, names in enumerate(groups):
        args = [where] + [got[k] for k in names]
        if later:
            args += [counts, new]
        new, counts = call(
            functools.partial(place_kernel, names, order, later),
            (f32(local_cent, width), f32(local_cent // LANES, LANES)),
            [SMEM] + [VMEM] * len(names) + ([VMEM, ANY] if later else []),
            args,
            ("place_early", "place_middle", "place_late")[later],
            out_specs=(ANY, VMEM),
            scratch=[pltpu.SemaphoreType.DMA((len(names),))],
            aliases={len(args) - 1: 0} if later else {},
        )
    return new, counts.reshape(-1), log_evidence.reshape(-1)


def solution(mesh):
    n, cores = mesh.shape["dp"], mesh.shape["cent"]
    return jax.shard_map(
        functools.partial(body, n, cores),
        mesh=mesh,
        in_specs=(P("dp", None), P("cent", None)),
        out_specs=(P("cent", None), P("cent"), P("dp")),
        check_vma=False,
    )
```

```python
import functools
import math

import jax
import jax.numpy as jnp
from jax import lax
from jax.experimental import pallas as pl
from jax.experimental.pallas import tpu as pltpu
from jax.sharding import PartitionSpec as P

prior_mass = 0.5
VMEM_LIMIT = 48 * 1024 * 1024
LANES = 128
NT = (((1,), (1,)), ((), ()))
NN = (((1,), (0,)), ((), ()))
VMEM = pl.BlockSpec(memory_space=pltpu.VMEM)
SMEM = pl.BlockSpec(memory_space=pltpu.SMEM)
ANY = pl.BlockSpec(memory_space=pl.ANY)
HBM = pl.BlockSpec(memory_space=pltpu.HBM)


def f32(*shape):
    return jax.ShapeDtypeStruct(shape, jnp.float32)


def call(kernel, out_shape, in_specs, args, name, out_specs=None, scratch=(), flops=0, aliases={}):
    return pl.pallas_call(
        kernel,
        out_shape=out_shape,
        in_specs=in_specs,
        out_specs=jax.tree.map(lambda _: VMEM, out_shape) if out_specs is None else out_specs,
        scratch_shapes=list(scratch),
        input_output_aliases=aliases,
        compiler_params=pltpu.CompilerParams(vmem_limit_bytes=VMEM_LIMIT),
        cost_estimate=pl.CostEstimate(
            flops=flops,
            bytes_accessed=sum(a.size * a.dtype.itemsize for a in args),
            transcendentals=0,
        ),
        name=name,
    )(*args)


def open_kernel(where_ref, points_ref, first_ref, second_ref, raw_ref, sem):
    half = first_ref.shape[0]
    start = pl.multiple_of(where_ref[1] * (2 * half), 2 * half)
    copy = pltpu.make_async_copy(points_ref.at[pl.ds(start, 2 * half), :], raw_ref, sem)
    copy.start()
    copy.wait()
    first_ref[...] = raw_ref[:half, :].astype(jnp.float32)
    second_ref[...] = raw_ref[half:, :].astype(jnp.float32)


def widen(norm, width):
    if width <= norm.shape[1]:
        return norm[:, :width]
    return jnp.concatenate([norm] * (width // norm.shape[1]), axis=1)


def norms(c):
    c = c.astype(jnp.float32)
    return jnp.broadcast_to(jnp.sum(c * c, axis=1, keepdims=True), (c.shape[0], LANES))


def stats_kernel(lines, where_ref, points_ref, c_ref, out_ref, twice_ref, norm_ref, all_norm_ref):
    rows, local = points_ref.shape[0], c_ref.shape[0]
    chunk = local // lines
    tile, size = min(256, rows), chunk // 4
    kept = pl.multiple_of(lax.rem(where_ref[0], 4) * size, size)
    for l in range(lines):
        c = c_ref[l * chunk : (l + 1) * chunk, :]
        all_norm_ref[...] = norms(c)
        twice = c + c
        for start in range(0, rows, tile):
            at = slice(start, start + tile)
            dots = lax.dot_general(twice, points_ref[at, :], NT, preferred_element_type=jnp.float32)
            score = dots - widen(all_norm_ref[...], tile)
            top = jnp.max(score, axis=0, keepdims=True)
            total = jnp.sum(jnp.exp(score - top), axis=0, keepdims=True)
            if l:
                old_top, old_total = out_ref[0:1, at], out_ref[1:2, at]
                new_top = jnp.maximum(old_top, top)
                total = old_total * jnp.exp(old_top - new_top) + total * jnp.exp(top - new_top)
                top = new_top
            out_ref[0:1, at] = top
            out_ref[1:2, at] = total
        mine = c_ref[pl.ds(pl.multiple_of(l * chunk + kept, size), size), :]
        twice_ref[l * size : (l + 1) * size, :] = mine + mine
        norm_ref[l * size : (l + 1) * size, :] = all_norm_ref[pl.ds(kept, size), :]


def stats(where, points, centroids, lines):
    rows, width = points.shape
    local = centroids.shape[0]
    return call(
        functools.partial(stats_kernel, lines),
        (
            f32(2, rows),
            jax.ShapeDtypeStruct((local // 4, width), jnp.bfloat16),
            f32(local // 4, LANES),
        ),
        [SMEM, VMEM, VMEM],
        (where, points, centroids),
        "stats",
        scratch=[pltpu.VMEM((local // lines, LANES), jnp.float32)],
        flops=4 * rows * local * width,
    )


def lse_kernel(cores, every, x0_ref, y1_ref, *refs):
    pair_refs = refs[:cores]
    lse_ref, evidence_ref, pack_x_ref, pack_y_ref = refs[cores:]
    half = lse_ref.shape[1]
    top = functools.reduce(jnp.maximum, [p[0:1, :] for p in pair_refs])
    total = functools.reduce(jnp.add, [p[1:2, :] * jnp.exp(p[0:1, :] - top) for p in pair_refs])
    lse = top + jnp.log(total)
    evidence = lse - math.log(every)
    for k in range(evidence_ref.shape[0]):
        evidence_ref[k : k + 1, :] = evidence[:, k * LANES : (k + 1) * LANES]
    for i in range(2 * cores):
        lse_ref[i : i + 1, :] = lse[:, i * half : (i + 1) * half]
    for piece_ref, pack_ref in ((x0_ref, pack_x_ref), (y1_ref, pack_y_ref)):
        pack_ref[0:half, :] = piece_ref[...]
        pack_ref[half:, :] = jnp.zeros_like(pack_ref[half:, :])
        pack_ref[half : half + 2 * cores, 0:half] = lse_ref[...]


def weigh(twice, norm, x, lse, lanes):
    dots = lax.dot_general(twice, x, NT, preferred_element_type=jnp.float32)
    score = dots - widen(norm, x.shape[0])
    resp = jnp.exp(score - lse).astype(jnp.bfloat16)
    part = lax.dot_general(resp, x, NN, preferred_element_type=jnp.float32)
    wide = resp.astype(jnp.float32)
    counted = functools.reduce(
        jnp.add, [wide[:, k : k + lanes] for k in range(0, x.shape[0], lanes)]
    )
    return part, counted


def own_kernel(cores, points_ref, twice_ref, norm_ref, lse_ref, acc_ref, cnt_ref):
    half = points_ref.shape[0] // (2 * cores)
    for i in range(2 * cores):
        x = points_ref[i * half : (i + 1) * half, :]
        part, counted = weigh(
            twice_ref[...], norm_ref[...], x, lse_ref[i : i + 1, :], cnt_ref.shape[1]
        )
        if i == 0:
            acc_ref[...] = part
            cnt_ref[...] = counted
        else:
            acc_ref[...] += part
            cnt_ref[...] += counted


def near_rows(cores, half, core, refs, d0_ref, d1_ref):
    whose = ((d1_ref, 0), (d0_ref, 1), (d1_ref, 1), (d0_ref, 0))
    for k, (tail_ref, part) in enumerate(whose):
        for rc in range(cores):
            at = half + 2 * (core ^ rc) + part
            yield refs[k * cores + rc], (lambda at=at, tail_ref=tail_ref: tail_ref[pl.ds(at, 1), :][:, 0:half])


def far_rows(cores, half, core, refs, lse_ref):
    for part in range(2):
        for rc in range(cores):
            at = 2 * (core ^ rc) + part
            yield refs[part * cores + rc], (lambda at=at: lse_ref[pl.ds(at, 1), :])


def add_rows(rows, half, twice_ref, norm_ref, acc_ref, cnt_ref):
    for x_ref, lse in rows:
        part, counted = weigh(
            twice_ref[...], norm_ref[...], x_ref[0:half, :].astype(jnp.bfloat16), lse(), cnt_ref.shape[1]
        )
        acc_ref[...] += part
        cnt_ref[...] += counted


def near_kernel(cores, half, where_ref, twice_ref, norm_ref, acc_in_ref, cnt_in_ref, *refs):
    near, (d0_ref, d1_ref, acc_ref, cnt_ref) = refs[: 4 * cores], refs[4 * cores :]
    acc_ref[...] = acc_in_ref[...]
    cnt_ref[...] = cnt_in_ref[...]
    rows = near_rows(cores, half, where_ref[1], near, d0_ref, d1_ref)
    add_rows(rows, half, twice_ref, norm_ref, acc_ref, cnt_ref)


def far_kernel(cores, half, where_ref, twice_ref, norm_ref, acc_in_ref, cnt_in_ref, lse_ref, *refs):
    far, (out_ref, acc_ref, cnt_ref) = refs[: 2 * cores], refs[2 * cores :]
    acc_ref[...] = acc_in_ref[...]
    cnt_ref[...] = cnt_in_ref[...]
    add_rows(far_rows(cores, half, where_ref[1], far, lse_ref), half, twice_ref, norm_ref, acc_ref, cnt_ref)
    lines, width = out_ref.shape[0], out_ref.shape[2]
    size = out_ref.shape[1] - 8
    for l in range(lines):
        turned = jnp.sum(cnt_ref[l * size : (l + 1) * size, :].T, axis=0, keepdims=True)
        if size < width:
            turned = jnp.concatenate([turned, jnp.zeros((1, width - size), jnp.float32)], axis=1)
        out_ref[l, 0:size, :] = acc_ref[l * size : (l + 1) * size, :]
        out_ref[l, size : size + 8, :] = jnp.broadcast_to(turned, (8, width))


def finish_kernel(where_ref, twice_ref, total_ref, out_ref):
    size, width = out_ref.shape[0] - 8, out_ref.shape[1]
    start = pl.multiple_of(lax.div(where_ref[0], 4) * size, size)
    c = 0.5 * twice_ref[pl.ds(start, size), :].astype(jnp.float32)
    counts = total_ref[size:, :]
    column = counts.T[:size, 0:1]
    out_ref[0:size, :] = (total_ref[0:size, :] + prior_mass * c) / (column + prior_mass)
    row = lax.broadcasted_iota(jnp.int32, (8, LANES), 0)
    spread = jnp.zeros((8, LANES), jnp.float32)
    for k in range(size // LANES):
        spread = jnp.where(row == k, counts[:, k * LANES : (k + 1) * LANES], spread)
    out_ref[size:, :] = jnp.concatenate([spread] * (width // LANES), axis=1)


def others_kernel(where_ref, column_ref, out_ref, sems):
    lines = column_ref.shape[0]
    line = lax.div(where_ref[0], 4)
    copies = [
        pltpu.make_async_copy(column_ref.at[lax.rem(line + k, lines)], out_ref.at[k - 1], sems.at[k - 1])
        for k in range(1, lines)
    ]
    for copy in copies:
        copy.start()
    for copy in copies:
        copy.wait()


def place_kernel(blocks, size, lines, later, where_ref, *refs):
    new_ref, counts_ref, tiles_ref, sems = refs[-4:]
    plane, line = lax.rem(where_ref[0], 4), lax.div(where_ref[0], 4)
    each = size // LANES
    copies, places = [], []
    for i, (array, index, bits, place, steps) in enumerate(blocks):
        ref = refs[array] if index is None else refs[array].at[index]
        at = lax.rem(line + steps, lines) if place is None else place
        places.append(at * 4 + (plane ^ bits))
        rows = pl.ds(pl.multiple_of(places[-1] * size, size), size)
        copies.append(pltpu.make_async_copy(ref.at[size : size + 8, :], tiles_ref.at[i], sems.at[0, i]))
        copies.append(pltpu.make_async_copy(ref.at[0:size, :], new_ref.at[rows, :], sems.at[1, i]))
    for copy in copies:
        copy.start()
    if later:
        counts_ref[...] = refs[-6][...]
    for copy in copies[::2]:
        copy.wait()
    for i in range(len(blocks)):
        for k in range(each):
            counts_ref[pl.ds(places[i] * each + k, 1), :] = tiles_ref[i, k : k + 1, 0:LANES]
    for copy in copies[1::2]:
        copy.wait()


def body(n, cores, points, centroids):
    rows, width = points.shape
    local_cent = centroids.shape[0]
    lines = n // 4
    half = rows // (2 * cores)
    share = local_cent // 4
    size = share // lines
    where = jnp.stack([lax.axis_index("dp"), lax.axis_index("cent")]).astype(jnp.int32)

    def flip(x, bits):
        return lax.ppermute(x, "dp", [(i, i ^ bits) for i in range(n)])

    def flip_core(x, bits):
        return lax.ppermute(x, "cent", [(i, i ^ bits) for i in range(cores)])

    def with_siblings(pieces):
        return [a if rc == 0 else flip_core(a, rc) for a in pieces for rc in range(cores)]

    first, second = call(
        open_kernel,
        (f32(half, width), f32(half, width)),
        [SMEM, HBM],
        (where, points),
        "open",
        scratch=[pltpu.VMEM((2 * half, width), points.dtype), pltpu.SemaphoreType.DMA(())],
    )
    x0, y1 = flip(first, 1), flip(second, 2)
    x1, y0 = flip(second, 1), flip(first, 2)

    pair, twice, norm = stats(where, points, centroids, lines)
    pairs = [pair] + [flip_core(pair, rc) for rc in range(1, cores)]
    tail = max(8, 2 * cores)
    lse, log_evidence, pack_x, pack_y = call(
        functools.partial(lse_kernel, cores, local_cent * cores),
        (f32(2 * cores, half), f32(rows // LANES, LANES), f32(half + tail, width), f32(half + tail, width)),
        [VMEM] * (2 + cores),
        (x0, y1, *pairs),
        "lse",
    )
    d0, d1 = flip(pack_x, 2), flip(pack_y, 1)

    lanes = min(LANES, half)
    acc, cnt = call(
        functools.partial(own_kernel, cores),
        (f32(share, width), f32(share, lanes)),
        [VMEM] * 4,
        (points, twice, norm, lse),
        "own",
        flops=4 * share * width * rows,
    )
    x0, y1, x1, y0, lse = lax.optimization_barrier((x0, y1, x1, y0, lse))
    near = with_siblings((x0, y1, x1, y0))
    near, d0, d1, acc, cnt = lax.optimization_barrier((near, d0, d1, acc, cnt))
    lse_d = flip(d1[half : half + 2 * cores, :half], 2)
    acc, cnt = call(
        functools.partial(near_kernel, cores, half),
        (f32(share, width), f32(share, lanes)),
        [SMEM] + [VMEM] * (6 + 4 * cores),
        (where, twice, norm, acc, cnt, *near, d0, d1),
        "near",
        flops=4 * share * width * 2 * rows,
        aliases={3: 0, 4: 1},
    )
    sums = call(
        functools.partial(far_kernel, cores, half),
        f32(lines, size + 8, width),
        [SMEM] + [VMEM] * (5 + 2 * cores),
        (where, twice, norm, acc, cnt, lse_d, *with_siblings((d0, d1))),
        "far",
        scratch=[pltpu.VMEM((share, width), jnp.float32), pltpu.VMEM((share, lanes), jnp.float32)],
        flops=4 * share * width * rows,
    )

    groups = [[4 * l + p for l in range(lines)] for p in range(4)]
    total = lax.psum_scatter(sums, "dp", scatter_dimension=0, axis_index_groups=groups, tiled=False)
    block_sum = f32(size + 8, width)
    done = call(finish_kernel, block_sum, [SMEM, VMEM, VMEM], (where, twice, total), "finish")

    column = lax.all_gather(done, "dp", axis_index_groups=groups)
    over_x, over_y = flip(done, 1), flip(done, 2)
    diagonal = flip(over_x, 2)
    diagonal, over_y, column = lax.optimization_barrier((diagonal, over_y, column))
    far_column = lax.all_gather(diagonal, "dp", axis_index_groups=groups)
    others = call(
        others_kernel,
        f32(lines - 1, size + 8, width),
        [SMEM, ANY],
        (where, column),
        "others",
        scratch=[pltpu.SemaphoreType.DMA((lines - 1,))],
    )
    others_x, others_y = flip(others, 1), flip(others, 2)

    steps = range(1, lines)
    stages = (
        (
            (column, over_x, over_y),
            [(0, l, 0, l, None) for l in range(lines)] + [(1, None, 1, None, 0), (2, None, 2, None, 0)],
        ),
        ((far_column,), [(0, l, 3, l, None) for l in range(lines)]),
        (
            (others_x, others_y),
            [(a, k - 1, a + 1, None, k) for a in range(2) for k in steps],
        ),
    )
    new = counts = None
    for later, (arrays, blocks) in enumerate(stages):
        args = [where, *arrays] + ([counts, new] if later else [])
        new, counts = call(
            functools.partial(place_kernel, blocks, size, lines, later),
            (f32(local_cent, width), f32(local_cent // LANES, LANES)),
            [SMEM] + [ANY] * len(arrays) + ([VMEM, ANY] if later else []),
            args,
            ("place_early", "place_middle", "place_late")[later],
            out_specs=(ANY, VMEM),
            scratch=[
                pltpu.VMEM((len(blocks), 8, width), jnp.float32),
                pltpu.SemaphoreType.DMA((2, len(blocks))),
            ],
            aliases={len(args) - 1: 0} if later else {},
        )
    return new, counts.reshape(-1), log_evidence.reshape(-1)


def solution(mesh):
    n, cores = mesh.shape["dp"], mesh.shape["cent"]
    return jax.shard_map(
        functools.partial(body, n, cores),
        mesh=mesh,
        in_specs=(P("dp", None), P("cent", None)),
        out_specs=(P("cent", None), P("cent"), P("dp")),
        check_vma=False,
    )
```

```python
import functools
import math

import jax
import jax.numpy as jnp
from jax import lax
from jax.experimental import pallas as pl
from jax.experimental.pallas import tpu as pltpu
from jax.sharding import PartitionSpec as P

prior_mass = 0.5
VMEM_LIMIT = 48 * 1024 * 1024
LANES = 128
NT = (((1,), (1,)), ((), ()))
NN = (((1,), (0,)), ((), ()))
VMEM = pl.BlockSpec(memory_space=pltpu.VMEM)
SMEM = pl.BlockSpec(memory_space=pltpu.SMEM)
ANY = pl.BlockSpec(memory_space=pl.ANY)
HBM = pl.BlockSpec(memory_space=pltpu.HBM)


def f32(*shape):
    return jax.ShapeDtypeStruct(shape, jnp.float32)


def call(kernel, out_shape, in_specs, args, name, out_specs=None, scratch=(), flops=0, aliases={}):
    return pl.pallas_call(
        kernel,
        out_shape=out_shape,
        in_specs=in_specs,
        out_specs=jax.tree.map(lambda _: VMEM, out_shape) if out_specs is None else out_specs,
        scratch_shapes=list(scratch),
        input_output_aliases=aliases,
        compiler_params=pltpu.CompilerParams(vmem_limit_bytes=VMEM_LIMIT),
        cost_estimate=pl.CostEstimate(
            flops=flops,
            bytes_accessed=sum(a.size * a.dtype.itemsize for a in args),
            transcendentals=0,
        ),
        name=name,
    )(*args)


def open_kernel(where_ref, points_ref, first_ref, second_ref, raw_ref, sem):
    half = first_ref.shape[0]
    start = pl.multiple_of(where_ref[1] * (2 * half), 2 * half)
    copy = pltpu.make_async_copy(points_ref.at[pl.ds(start, 2 * half), :], raw_ref, sem)
    copy.start()
    copy.wait()
    first_ref[...] = raw_ref[:half, :].astype(jnp.float32)
    second_ref[...] = raw_ref[half:, :].astype(jnp.float32)


def widen(norm, width):
    if width <= norm.shape[1]:
        return norm[:, :width]
    return jnp.concatenate([norm] * (width // norm.shape[1]), axis=1)


def norms(c):
    c = c.astype(jnp.float32)
    return jnp.broadcast_to(jnp.sum(c * c, axis=1, keepdims=True), (c.shape[0], LANES))


def stats_kernel(lines, where_ref, points_ref, c_ref, out_ref, twice_ref, norm_ref, all_norm_ref):
    rows, local = points_ref.shape[0], c_ref.shape[0]
    chunk = local // lines
    tile, size = min(256, rows), chunk // 4
    kept = pl.multiple_of(lax.rem(where_ref[0], 4) * size, size)
    for l in range(lines):
        c = c_ref[l * chunk : (l + 1) * chunk, :]
        all_norm_ref[...] = norms(c)
        twice = c + c
        for start in range(0, rows, tile):
            at = slice(start, start + tile)
            dots = lax.dot_general(twice, points_ref[at, :], NT, preferred_element_type=jnp.float32)
            score = dots - widen(all_norm_ref[...], tile)
            top = jnp.max(score, axis=0, keepdims=True)
            total = jnp.sum(jnp.exp(score - top), axis=0, keepdims=True)
            if l:
                old_top, old_total = out_ref[0:1, at], out_ref[1:2, at]
                new_top = jnp.maximum(old_top, top)
                total = old_total * jnp.exp(old_top - new_top) + total * jnp.exp(top - new_top)
                top = new_top
            out_ref[0:1, at] = top
            out_ref[1:2, at] = total
        mine = c_ref[pl.ds(pl.multiple_of(l * chunk + kept, size), size), :]
        twice_ref[l * size : (l + 1) * size, :] = mine + mine
        norm_ref[l * size : (l + 1) * size, :] = all_norm_ref[pl.ds(kept, size), :]


def stats(where, points, centroids, lines):
    rows, width = points.shape
    local = centroids.shape[0]
    return call(
        functools.partial(stats_kernel, lines),
        (
            f32(2, rows),
            jax.ShapeDtypeStruct((local // 4, width), jnp.bfloat16),
            f32(local // 4, LANES),
        ),
        [SMEM, VMEM, VMEM],
        (where, points, centroids),
        "stats",
        scratch=[pltpu.VMEM((local // lines, LANES), jnp.float32)],
        flops=4 * rows * local * width,
    )


def lse_kernel(cores, every, a0_ref, b1_ref, *refs):
    pair_refs = refs[:cores]
    lse_ref, evidence_ref, pack_a_ref, pack_b_ref = refs[cores:]
    half = lse_ref.shape[1]
    top = functools.reduce(jnp.maximum, [p[0:1, :] for p in pair_refs])
    total = functools.reduce(jnp.add, [p[1:2, :] * jnp.exp(p[0:1, :] - top) for p in pair_refs])
    lse = top + jnp.log(total)
    evidence = lse - math.log(every)
    for k in range(evidence_ref.shape[0]):
        evidence_ref[k : k + 1, :] = evidence[:, k * LANES : (k + 1) * LANES]
    for i in range(2 * cores):
        lse_ref[i : i + 1, :] = lse[:, i * half : (i + 1) * half]
    for piece_ref, pack_ref in ((a0_ref, pack_a_ref), (b1_ref, pack_b_ref)):
        pack_ref[0:half, :] = piece_ref[...]
        pack_ref[half:, :] = jnp.zeros_like(pack_ref[half:, :])
        pack_ref[half : half + 2 * cores, 0:half] = lse_ref[...]


def weigh(twice, norm, x, lse, lanes):
    dots = lax.dot_general(twice, x, NT, preferred_element_type=jnp.float32)
    score = dots - widen(norm, x.shape[0])
    resp = jnp.exp(score - lse).astype(jnp.bfloat16)
    part = lax.dot_general(resp, x, NN, preferred_element_type=jnp.float32)
    wide = resp.astype(jnp.float32)
    counted = functools.reduce(
        jnp.add, [wide[:, k : k + lanes] for k in range(0, x.shape[0], lanes)]
    )
    return part, counted


def own_kernel(cores, points_ref, twice_ref, norm_ref, lse_ref, acc_ref, cnt_ref):
    half = points_ref.shape[0] // (2 * cores)
    for i in range(2 * cores):
        x = points_ref[i * half : (i + 1) * half, :]
        part, counted = weigh(
            twice_ref[...], norm_ref[...], x, lse_ref[i : i + 1, :], cnt_ref.shape[1]
        )
        if i == 0:
            acc_ref[...] = part
            cnt_ref[...] = counted
        else:
            acc_ref[...] += part
            cnt_ref[...] += counted


def near_rows(cores, half, core, refs, d0_ref, d1_ref):
    for k, (kind, part) in enumerate(((0, 0), (1, 1), (0, 1), (1, 0))):
        for rc in range(cores):
            at = half + 2 * (core ^ rc) + part
            tail_ref = d1_ref if (kind + rc) % 2 == 0 else d0_ref
            yield refs[k * cores + rc], (lambda at=at, tail_ref=tail_ref: tail_ref[pl.ds(at, 1), :][:, 0:half])


def far_rows(cores, half, core, refs, lse_ref):
    for part in range(2):
        for rc in range(cores):
            at = 2 * (core ^ rc) + part
            yield refs[part * cores + rc], (lambda at=at: lse_ref[pl.ds(at, 1), :])


def add_rows(rows, half, twice, norm, acc, cnt):
    for x_ref, lse in rows:
        part, counted = weigh(twice, norm, x_ref[0:half, :].astype(jnp.bfloat16), lse(), cnt.shape[1])
        acc, cnt = acc + part, cnt + counted
    return acc, cnt


def store_sums(out_ref, acc, cnt):
    size, width = acc.shape
    turned = jnp.sum(cnt.T, axis=0, keepdims=True)
    if size < width:
        turned = jnp.concatenate([turned, jnp.zeros((1, width - size), jnp.float32)], axis=1)
    out_ref[0:size, :] = acc
    out_ref[size : size + 8, :] = jnp.broadcast_to(turned, (8, width))


def lead_kernel(cores, order, half, where_ref, twice_ref, norm_ref, acc_ref, cnt_ref, *refs):
    out_acc_ref, out_cnt_ref = refs[-2:]
    near, (d0_ref, d1_ref) = refs[: 4 * cores], refs[4 * cores : 4 * cores + 2]
    size = out_acc_ref.shape[0]
    place = ahead(order, lax.div(where_ref[0], 4), len(order) // 2)
    at = pl.ds(pl.multiple_of(place * size, size), size)
    out_acc_ref[...], out_cnt_ref[...] = add_rows(
        near_rows(cores, half, where_ref[1], near, d0_ref, d1_ref),
        half,
        twice_ref[at, :],
        norm_ref[at, :],
        acc_ref[at, :],
        cnt_ref[at, :],
    )


def block_sums(cores, order, half, steps, where_ref, twice_ref, norm_ref, acc_ref, cnt_ref, lse_ref, near, far, out_ref):
    size = out_ref.shape[0] - 8
    place = ahead(order, lax.div(where_ref[0], 4), steps)
    at = pl.ds(pl.multiple_of(place * size, size), size)
    twice, norm = twice_ref[at, :], norm_ref[at, :]
    acc, cnt = add_rows(
        near_rows(cores, half, where_ref[1], near, far[0], far[cores]),
        half,
        twice,
        norm,
        acc_ref[at, :],
        cnt_ref[at, :],
    )
    acc, cnt = add_rows(far_rows(cores, half, where_ref[1], far, lse_ref), half, twice, norm, acc, cnt)
    store_sums(out_ref, acc, cnt)


def first_kernel(cores, order, half, where_ref, twice_ref, norm_ref, lse_ref, lead_acc_ref, lead_cnt_ref, *refs):
    far, out_ref = refs[: 2 * cores], refs[2 * cores]
    size = lead_acc_ref.shape[0]
    place = ahead(order, lax.div(where_ref[0], 4), len(order) // 2)
    at = pl.ds(pl.multiple_of(place * size, size), size)
    acc, cnt = add_rows(
        far_rows(cores, half, where_ref[1], far, lse_ref),
        half,
        twice_ref[at, :],
        norm_ref[at, :],
        lead_acc_ref[...],
        lead_cnt_ref[...],
    )
    store_sums(out_ref, acc, cnt)


def rest_kernel(cores, order, half, steps, where_ref, twice_ref, norm_ref, acc_ref, cnt_ref, lse_ref, *refs):
    near, far = refs[: 4 * cores], refs[4 * cores : 6 * cores]
    for s, out_ref in zip(steps, refs[6 * cores :]):
        block_sums(
            cores, order, half, s, where_ref, twice_ref, norm_ref, acc_ref, cnt_ref, lse_ref, near, far, out_ref
        )


def ahead(order, line, steps):
    n = len(order)
    return functools.reduce(
        jnp.add,
        [jnp.where(line == order[p], order[(p + steps) % n], 0) for p in range(n)],
    )


def add_kernel(a_ref, b_ref, out_ref):
    out_ref[...] = a_ref[...] + b_ref[...]


def finish_kernel(where_ref, twice_ref, mine_ref, first_ref, second_ref, out_ref):
    size, width = out_ref.shape[0] - 8, out_ref.shape[1]
    start = pl.multiple_of(lax.div(where_ref[0], 4) * size, size)
    c = 0.5 * twice_ref[pl.ds(start, size), :].astype(jnp.float32)
    total = mine_ref[...] + first_ref[...] + second_ref[...]
    counts = total[size:, :]
    column = counts.T[:size, 0:1]
    out_ref[0:size, :] = (total[:size, :] + prior_mass * c) / (column + prior_mass)
    row = lax.broadcasted_iota(jnp.int32, (8, LANES), 0)
    spread = jnp.zeros((8, LANES), jnp.float32)
    for k in range(size // LANES):
        spread = jnp.where(row == k, counts[:, k * LANES : (k + 1) * LANES], spread)
    out_ref[size:, :] = jnp.concatenate([spread] * (width // LANES), axis=1)


def place_kernel(names, order, later, where_ref, *refs):
    count, lines = len(names), len(order)
    block_refs = refs[:count]
    new_ref, counts_ref, sems = refs[-3:]
    size = block_refs[0].shape[0] - 8
    plane, line = lax.rem(where_ref[0], 4), lax.div(where_ref[0], 4)
    each = size // LANES
    odd = lax.rem(where_ref[1], 2)
    bits = (0, 1 + odd, 2 - odd, 3)
    places = [ahead(order, line, steps) * 4 + (plane ^ bits[way]) for way, steps in names]
    copies = []
    for i in range(count):
        at = pl.multiple_of(places[i] * size, size)
        copies.append(
            pltpu.make_async_copy(block_refs[i].at[0:size, :], new_ref.at[pl.ds(at, size), :], sems.at[i])
        )
        copies[-1].start()
    if later:
        counts_ref[...] = refs[count][...]
    for i in range(count):
        for k in range(each):
            counts_ref[pl.ds(places[i] * each + k, 1), :] = block_refs[i][size + k : size + k + 1, 0:LANES]
    for copy in copies:
        copy.wait()


def body(n, cores, points, centroids):
    rows, width = points.shape
    local_cent = centroids.shape[0]
    lines = n // 4
    half = rows // (2 * cores)
    share = local_cent // 4
    size = share // lines
    order = tuple(range(0, lines, 2)) + tuple(range(1, lines, 2))[::-1]
    where = jnp.stack([lax.axis_index("dp"), lax.axis_index("cent")]).astype(jnp.int32)

    def exchange(x, kind):
        pairs = [
            (i * cores + c, (i ^ (1 if (kind + c) % 2 == 0 else 2)) * cores + c)
            for i in range(n)
            for c in range(cores)
        ]
        return lax.ppermute(x, ("dp", "cent"), pairs)

    def flip_core(x, bits):
        return lax.ppermute(x, "cent", [(i, i ^ bits) for i in range(cores)])

    def ring(x, way):
        pairs = [(order[p], order[(p + way) % lines]) for p in range(lines)]
        return lax.ppermute(x, "dp", [(4 * a + i, 4 * b + i) for a, b in pairs for i in range(4)])

    def with_siblings(pieces):
        return [a if rc == 0 else flip_core(a, rc) for a in pieces for rc in range(cores)]

    first, second = call(
        open_kernel,
        (f32(half, width), f32(half, width)),
        [SMEM, HBM],
        (where, points),
        "open",
        scratch=[pltpu.VMEM((2 * half, width), points.dtype), pltpu.SemaphoreType.DMA(())],
    )
    a0, b1 = exchange(first, 0), exchange(second, 1)
    a1, b0 = exchange(second, 0), exchange(first, 1)

    pair, twice, norm = stats(where, points, centroids, lines)
    pairs = [pair] + [flip_core(pair, rc) for rc in range(1, cores)]
    tail = max(8, 2 * cores)
    lse, log_evidence, pack_a, pack_b = call(
        functools.partial(lse_kernel, cores, local_cent * cores),
        (f32(2 * cores, half), f32(rows // LANES, LANES), f32(half + tail, width), f32(half + tail, width)),
        [VMEM] * (2 + cores),
        (a0, b1, *pairs),
        "lse",
    )
    d0, d1 = exchange(pack_a, 1), exchange(pack_b, 0)

    lanes = min(LANES, half)
    acc, cnt = call(
        functools.partial(own_kernel, cores),
        (f32(share, width), f32(share, lanes)),
        [VMEM] * 4,
        (points, twice, norm, lse),
        "own",
        flops=4 * share * width * rows,
    )
    a0, b1, a1, b0, lse = lax.optimization_barrier((a0, b1, a1, b0, lse))
    near = with_siblings((a0, b1, a1, b0))
    lse_d = exchange(d1[half : half + 2 * cores, :half], 1)
    near, d0, d1, acc, cnt = lax.optimization_barrier((near, d0, d1, acc, cnt))
    lead = call(
        functools.partial(lead_kernel, cores, order, half),
        (f32(size, width), f32(size, lanes)),
        [SMEM] + [VMEM] * (6 + 4 * cores),
        (where, twice, norm, acc, cnt, *near, d0, d1),
        "lead",
        flops=4 * size * width * 2 * rows,
    )
    given = (where, twice, norm, acc, cnt, lse_d)
    far = with_siblings((d0, d1))
    rows_given = (*near, *far)
    block_sum = f32(size + 8, width)
    turn = lines // 2
    forward = list(range(turn - 1, 0, -1))
    backward = [lines - s for s in range(turn - 1, 0, -1)]
    first = call(
        functools.partial(first_kernel, cores, order, half),
        block_sum,
        [SMEM] + [VMEM] * (5 + 2 * cores),
        (where, twice, norm, lse_d, *lead, *far),
        "first",
        flops=4 * size * width * rows,
    )

    def sums_of(steps):
        made = call(
            functools.partial(rest_kernel, cores, order, half, steps),
            [block_sum] * len(steps),
            [SMEM] + [VMEM] * (5 + 6 * cores),
            (*given, *rows_given),
            "rest",
            flops=4 * size * width * 3 * rows * len(steps),
        )
        return dict(zip(steps, made))

    def plus(a, b):
        return call(add_kernel, block_sum, [VMEM] * 2, (a, b), "add")

    sums = {**sums_of(backward), **sums_of(forward + [0])}
    from_ahead = ring(sums[backward[0]], -1)
    for s in backward[1:]:
        from_ahead = ring(plus(sums[s], from_ahead), -1)
    from_behind = ring(first, 1)
    for s in forward:
        from_behind = ring(plus(sums[s], from_behind), 1)
    done = call(
        finish_kernel,
        block_sum,
        [SMEM] + [VMEM] * 4,
        (where, twice, sums[0], from_behind, from_ahead),
        "finish",
    )

    steps = [-s for s in range(1, lines // 2 + 1)] + list(range(1, lines // 2))
    got = {(0, 0): done}
    previous, older = (), ()
    for s in [0] + steps:
        x = got[0, s]
        if previous:
            x = lax.optimization_barrier((x, *previous))[0]
        got[1, s], got[2, s] = exchange(x, 0), exchange(x, 1)
        if s == steps[-1]:
            break
        got[3, s] = exchange(got[1, s], 1)
        previous, older = (got[2, s], *older), (got[3, s],)
        ahead_of = steps[([0] + steps).index(s)]
        x = got[0, ahead_of + (1 if ahead_of < 0 else -1)]
        if ahead_of > 0:
            x = lax.optimization_barrier((x, got[0, s]))[0]
        got[0, ahead_of] = ring(x, 1 if ahead_of < 0 else -1)
    before = got[3, steps[-1] - 1] if steps[-1] > 0 else got[3, steps[-1] + 1]
    before = lax.optimization_barrier((before, got[0, steps[-1]]))[0]
    got[3, steps[-1]] = ring(before, -1 if steps[-1] > 0 else 1)
    late = [(1, steps[-1]), (2, steps[-1]), (3, steps[-1])]
    middle = [(w, steps[-2]) for w in (1, 2, 3)] + [(0, steps[-1])]
    groups = ([k for k in got if k not in middle + late], middle, late)
    new = counts = None
    for later, names in enumerate(groups):
        args = [where] + [got[k] for k in names]
        if later:
            args += [counts, new]
        new, counts = call(
            functools.partial(place_kernel, names, order, later),
            (f32(local_cent, width), f32(local_cent // LANES, LANES)),
            [SMEM] + [VMEM] * len(names) + ([VMEM, ANY] if later else []),
            args,
            ("place_early", "place_middle", "place_late")[later],
            out_specs=(ANY, VMEM),
            scratch=[pltpu.SemaphoreType.DMA((len(names),))],
            aliases={len(args) - 1: 0} if later else {},
        )
    return new, counts.reshape(-1), log_evidence.reshape(-1)


def solution(mesh):
    n, cores = mesh.shape["dp"], mesh.shape["cent"]
    return jax.shard_map(
        functools.partial(body, n, cores),
        mesh=mesh,
        in_specs=(P("dp", None), P("cent", None)),
        out_specs=(P("cent", None), P("cent"), P("dp")),
        check_vma=False,
    )
```

```python
import functools
import math

import jax
import jax.numpy as jnp
from jax import lax
from jax.experimental import pallas as pl
from jax.experimental.pallas import tpu as pltpu
from jax.sharding import PartitionSpec as P

prior_mass = 0.5
VMEM_LIMIT = 48 * 1024 * 1024
LANES = 128
NT = (((1,), (1,)), ((), ()))
NN = (((1,), (0,)), ((), ()))
VMEM = pl.BlockSpec(memory_space=pltpu.VMEM)
SMEM = pl.BlockSpec(memory_space=pltpu.SMEM)
ANY = pl.BlockSpec(memory_space=pl.ANY)
HBM = pl.BlockSpec(memory_space=pltpu.HBM)


def f32(*shape):
    return jax.ShapeDtypeStruct(shape, jnp.float32)


def call(kernel, out_shape, in_specs, args, name, out_specs=None, scratch=(), flops=0, aliases={}):
    return pl.pallas_call(
        kernel,
        out_shape=out_shape,
        in_specs=in_specs,
        out_specs=jax.tree.map(lambda _: VMEM, out_shape) if out_specs is None else out_specs,
        scratch_shapes=list(scratch),
        input_output_aliases=aliases,
        compiler_params=pltpu.CompilerParams(vmem_limit_bytes=VMEM_LIMIT),
        cost_estimate=pl.CostEstimate(
            flops=flops,
            bytes_accessed=sum(a.size * a.dtype.itemsize for a in args),
            transcendentals=0,
        ),
        name=name,
    )(*args)


def open_kernel(where_ref, points_ref, first_ref, second_ref, raw_ref, sem):
    half = first_ref.shape[0]
    start = pl.multiple_of(where_ref[1] * (2 * half), 2 * half)
    copy = pltpu.make_async_copy(points_ref.at[pl.ds(start, 2 * half), :], raw_ref, sem)
    copy.start()
    copy.wait()
    first_ref[...] = raw_ref[:half, :].astype(jnp.float32)
    second_ref[...] = raw_ref[half:, :].astype(jnp.float32)


def widen(norm, width):
    if width <= norm.shape[1]:
        return norm[:, :width]
    return jnp.concatenate([norm] * (width // norm.shape[1]), axis=1)


def norms(c):
    c = c.astype(jnp.float32)
    return jnp.broadcast_to(jnp.sum(c * c, axis=1, keepdims=True), (c.shape[0], LANES))


def stats_kernel(lines, chunks, where_ref, points_ref, c_ref, *refs):
    out_ref, twice_ref, norm_ref, all_norm_ref = refs[-4:]
    rows, local = points_ref.shape[0], c_ref.shape[0]
    chunk = local // lines
    tile, size = min(256, rows), chunk // 4
    kept = pl.multiple_of(lax.rem(where_ref[0], 4) * size, size)
    if len(refs) > 4:
        out_ref[...] = refs[0][...]
    for i, l in enumerate(chunks):
        c = c_ref[l * chunk : (l + 1) * chunk, :]
        all_norm_ref[...] = norms(c)
        twice = c + c
        for start in range(0, rows, tile):
            at = slice(start, start + tile)
            dots = lax.dot_general(twice, points_ref[at, :], NT, preferred_element_type=jnp.float32)
            score = dots - widen(all_norm_ref[...], tile)
            top = jnp.max(score, axis=0, keepdims=True)
            total = jnp.sum(jnp.exp(score - top), axis=0, keepdims=True)
            if l:
                old_top, old_total = out_ref[0:1, at], out_ref[1:2, at]
                new_top = jnp.maximum(old_top, top)
                total = old_total * jnp.exp(old_top - new_top) + total * jnp.exp(top - new_top)
                top = new_top
            out_ref[0:1, at] = top
            out_ref[1:2, at] = total
        mine = c_ref[pl.ds(pl.multiple_of(l * chunk + kept, size), size), :]
        twice_ref[i * size : (i + 1) * size, :] = mine + mine
        norm_ref[i * size : (i + 1) * size, :] = all_norm_ref[pl.ds(kept, size), :]


def stats(where, points, centroids, lines, chunks, before=()):
    rows, width = points.shape
    local = centroids.shape[0]
    kept = len(chunks) * local // lines // 4
    return call(
        functools.partial(stats_kernel, lines, chunks),
        (f32(2, rows), jax.ShapeDtypeStruct((kept, width), jnp.bfloat16), f32(kept, LANES)),
        [SMEM] + [VMEM] * (2 + len(before)),
        (where, points, centroids, *before),
        "stats",
        scratch=[pltpu.VMEM((local // lines, LANES), jnp.float32)],
        flops=4 * rows * local * width * len(chunks) // lines,
    )


def lse_kernel(cores, every, a0_ref, b1_ref, *refs):
    pair_refs = refs[:cores]
    lse_ref, evidence_ref, pack_a_ref, pack_b_ref = refs[cores:]
    half = lse_ref.shape[1]
    top = functools.reduce(jnp.maximum, [p[0:1, :] for p in pair_refs])
    total = functools.reduce(jnp.add, [p[1:2, :] * jnp.exp(p[0:1, :] - top) for p in pair_refs])
    lse = top + jnp.log(total)
    evidence = lse - math.log(every)
    for k in range(evidence_ref.shape[0]):
        evidence_ref[k : k + 1, :] = evidence[:, k * LANES : (k + 1) * LANES]
    for i in range(2 * cores):
        lse_ref[i : i + 1, :] = lse[:, i * half : (i + 1) * half]
    for piece_ref, pack_ref in ((a0_ref, pack_a_ref), (b1_ref, pack_b_ref)):
        pack_ref[0:half, :] = piece_ref[...]
        pack_ref[half:, :] = jnp.zeros_like(pack_ref[half:, :])
        pack_ref[half : half + 2 * cores, 0:half] = lse_ref[...]


def weigh(twice, norm, x, lse, lanes):
    dots = lax.dot_general(twice, x, NT, preferred_element_type=jnp.float32)
    score = dots - widen(norm, x.shape[0])
    resp = jnp.exp(score - lse).astype(jnp.bfloat16)
    part = lax.dot_general(resp, x, NN, preferred_element_type=jnp.float32)
    wide = resp.astype(jnp.float32)
    counted = functools.reduce(
        jnp.add, [wide[:, k : k + lanes] for k in range(0, x.shape[0], lanes)]
    )
    return part, counted


def own_kernel(cores, points_ref, low_ref, high_ref, norm_low_ref, norm_high_ref, lse_ref, acc_ref, cnt_ref, twice_ref, norm_ref):
    half = points_ref.shape[0] // (2 * cores)
    cut = low_ref.shape[0]
    twice_ref[0:cut, :], twice_ref[cut:, :] = low_ref[...], high_ref[...]
    norm_ref[0:cut, :], norm_ref[cut:, :] = norm_low_ref[...], norm_high_ref[...]
    for i in range(2 * cores):
        x = points_ref[i * half : (i + 1) * half, :]
        part, counted = weigh(
            twice_ref[...], norm_ref[...], x, lse_ref[i : i + 1, :], cnt_ref.shape[1]
        )
        if i == 0:
            acc_ref[...] = part
            cnt_ref[...] = counted
        else:
            acc_ref[...] += part
            cnt_ref[...] += counted


KINDS = ((0, 0), (1, 1), (0, 1), (1, 0))


def near_rows(cores, half, core, refs, d0_ref, d1_ref):
    for k, (kind, part) in enumerate(KINDS):
        for rc in range(cores):
            at = half + 2 * (core ^ rc) + part
            tail_ref = d1_ref if (kind + rc) % 2 == 0 else d0_ref
            yield refs[k * cores + rc], (lambda at=at, tail_ref=tail_ref: tail_ref[pl.ds(at, 1), :][:, 0:half])


def far_rows(cores, half, core, refs, lse_ref):
    for part in range(2):
        for rc in range(cores):
            at = 2 * (core ^ rc) + part
            yield refs[part * cores + rc], (lambda at=at: lse_ref[pl.ds(at, 1), :])


def add_rows(rows, half, twice, norm, acc, cnt):
    for x_ref, lse in rows:
        part, counted = weigh(twice, norm, x_ref[0:half, :].astype(jnp.bfloat16), lse(), cnt.shape[1])
        acc, cnt = acc + part, cnt + counted
    return acc, cnt


def store_sums(out_ref, acc, cnt):
    size, width = acc.shape
    turned = jnp.sum(cnt.T, axis=0, keepdims=True)
    if size < width:
        turned = jnp.concatenate([turned, jnp.zeros((1, width - size), jnp.float32)], axis=1)
    out_ref[0:size, :] = acc
    out_ref[size : size + 8, :] = jnp.broadcast_to(turned, (8, width))


def lead_kernel(cores, order, half, where_ref, twice_ref, norm_ref, acc_ref, cnt_ref, *refs):
    out_acc_ref, out_cnt_ref = refs[-2:]
    near, (d0_ref, d1_ref) = refs[: 4 * cores], refs[4 * cores : 4 * cores + 2]
    size = out_acc_ref.shape[0]
    place = ahead(order, lax.div(where_ref[0], 4), len(order) // 2)
    at = pl.ds(pl.multiple_of(place * size, size), size)
    out_acc_ref[...], out_cnt_ref[...] = add_rows(
        near_rows(cores, half, where_ref[1], near, d0_ref, d1_ref),
        half,
        twice_ref[at, :],
        norm_ref[at, :],
        acc_ref[at, :],
        cnt_ref[at, :],
    )


def block_sums(cores, order, half, steps, where_ref, twice_ref, norm_ref, acc_ref, cnt_ref, lse_ref, near, far, out_ref):
    size = out_ref.shape[0] - 8
    place = ahead(order, lax.div(where_ref[0], 4), steps)
    at = pl.ds(pl.multiple_of(place * size, size), size)
    twice, norm = twice_ref[at, :], norm_ref[at, :]
    acc, cnt = add_rows(
        near_rows(cores, half, where_ref[1], near, far[0], far[cores]),
        half,
        twice,
        norm,
        acc_ref[at, :],
        cnt_ref[at, :],
    )
    acc, cnt = add_rows(far_rows(cores, half, where_ref[1], far, lse_ref), half, twice, norm, acc, cnt)
    store_sums(out_ref, acc, cnt)


def first_kernel(cores, order, half, where_ref, twice_ref, norm_ref, lse_ref, lead_acc_ref, lead_cnt_ref, *refs):
    far, out_ref = refs[: 2 * cores], refs[2 * cores]
    size = lead_acc_ref.shape[0]
    place = ahead(order, lax.div(where_ref[0], 4), len(order) // 2)
    at = pl.ds(pl.multiple_of(place * size, size), size)
    acc, cnt = add_rows(
        far_rows(cores, half, where_ref[1], far, lse_ref),
        half,
        twice_ref[at, :],
        norm_ref[at, :],
        lead_acc_ref[...],
        lead_cnt_ref[...],
    )
    store_sums(out_ref, acc, cnt)


def rest_kernel(cores, order, half, steps, where_ref, twice_ref, norm_ref, acc_ref, cnt_ref, lse_ref, *refs):
    near, far = refs[: 4 * cores], refs[4 * cores : 6 * cores]
    for s, out_ref in zip(steps, refs[6 * cores :]):
        block_sums(
            cores, order, half, s, where_ref, twice_ref, norm_ref, acc_ref, cnt_ref, lse_ref, near, far, out_ref
        )


def ahead(order, line, steps):
    n = len(order)
    return functools.reduce(
        jnp.add,
        [jnp.where(line == order[p], order[(p + steps) % n], 0) for p in range(n)],
    )


def add_kernel(a_ref, b_ref, out_ref):
    out_ref[...] = a_ref[...] + b_ref[...]


def finish_kernel(where_ref, twice_ref, mine_ref, first_ref, second_ref, out_ref):
    size, width = out_ref.shape[0] - 8, out_ref.shape[1]
    start = pl.multiple_of(lax.div(where_ref[0], 4) * size, size)
    c = 0.5 * twice_ref[pl.ds(start, size), :].astype(jnp.float32)
    total = mine_ref[...] + first_ref[...] + second_ref[...]
    counts = total[size:, :]
    column = counts.T[:size, 0:1]
    out_ref[0:size, :] = (total[:size, :] + prior_mass * c) / (column + prior_mass)
    row = lax.broadcasted_iota(jnp.int32, (8, LANES), 0)
    spread = jnp.zeros((8, LANES), jnp.float32)
    for k in range(size // LANES):
        spread = jnp.where(row == k, counts[:, k * LANES : (k + 1) * LANES], spread)
    out_ref[size:, :] = jnp.concatenate([spread] * (width // LANES), axis=1)


def place_kernel(names, order, later, where_ref, *refs):
    count, lines = len(names), len(order)
    block_refs = refs[:count]
    new_ref, counts_ref, sems = refs[-3:]
    size = block_refs[0].shape[0] - 8
    plane, line = lax.rem(where_ref[0], 4), lax.div(where_ref[0], 4)
    each = size // LANES
    odd = lax.rem(where_ref[1], 2)
    bits = (0, 1 + odd, 2 - odd, 3)
    places = [ahead(order, line, steps) * 4 + (plane ^ bits[way]) for way, steps in names]
    copies = []
    for i in range(count):
        at = pl.multiple_of(places[i] * size, size)
        copies.append(
            pltpu.make_async_copy(block_refs[i].at[0:size, :], new_ref.at[pl.ds(at, size), :], sems.at[i])
        )
        copies[-1].start()
    if later:
        counts_ref[...] = refs[count][...]
    for i in range(count):
        for k in range(each):
            counts_ref[pl.ds(places[i] * each + k, 1), :] = block_refs[i][size + k : size + k + 1, 0:LANES]
    for copy in copies:
        copy.wait()


def body(n, cores, points, centroids):
    rows, width = points.shape
    local_cent = centroids.shape[0]
    lines = n // 4
    half = rows // (2 * cores)
    share = local_cent // 4
    size = share // lines
    order = tuple(range(0, lines, 2)) + tuple(range(1, lines, 2))[::-1]
    where = jnp.stack([lax.axis_index("dp"), lax.axis_index("cent")]).astype(jnp.int32)

    def exchange(x, kind):
        pairs = [
            (i * cores + c, (i ^ (1 if (kind + c) % 2 == 0 else 2)) * cores + c)
            for i in range(n)
            for c in range(cores)
        ]
        return lax.ppermute(x, ("dp", "cent"), pairs)

    def flip_core(x, bits):
        return lax.ppermute(x, "cent", [(i, i ^ bits) for i in range(cores)])

    def ring(x, way):
        pairs = [(order[p], order[(p + way) % lines]) for p in range(lines)]
        return lax.ppermute(x, "dp", [(4 * a + i, 4 * b + i) for a, b in pairs for i in range(4)])

    def with_siblings(pieces):
        return [a if rc == 0 else flip_core(a, rc) for a in pieces for rc in range(cores)]

    first, second = call(
        open_kernel,
        (f32(half, width), f32(half, width)),
        [SMEM, HBM],
        (where, points),
        "open",
        scratch=[pltpu.VMEM((2 * half, width), points.dtype), pltpu.SemaphoreType.DMA(())],
    )
    a0, b1 = exchange(first, 0), exchange(second, 1)

    cut = lines // 2
    pair, twice_low, norm_low = stats(where, points, centroids, lines, range(cut))
    first, second, pair, a0, b1 = lax.optimization_barrier((first, second, pair, a0, b1))
    a1, b0 = exchange(second, 0), exchange(first, 1)
    pair, twice_high, norm_high = stats(where, points, centroids, lines, range(cut, lines), (pair,))
    kept = [twice_low, twice_high, norm_low, norm_high]
    early = with_siblings((a0, b1))
    early, pair = lax.optimization_barrier((early, pair))
    a0, b1 = early[0], early[cores]
    pairs = [pair] + [flip_core(pair, rc) for rc in range(1, cores)]
    tail = max(8, 2 * cores)
    lse, log_evidence, pack_a, pack_b = call(
        functools.partial(lse_kernel, cores, local_cent * cores),
        (f32(2 * cores, half), f32(rows // LANES, LANES), f32(half + tail, width), f32(half + tail, width)),
        [VMEM] * (2 + cores),
        (a0, b1, *pairs),
        "lse",
    )
    d0, d1 = exchange(pack_a, 1), exchange(pack_b, 0)

    lanes = min(LANES, half)
    a1, b0, lse = lax.optimization_barrier((a1, b0, lse))
    near = early + with_siblings((a1, b0))
    near, lse = lax.optimization_barrier((near, lse))
    acc, cnt, twice, norm = call(
        functools.partial(own_kernel, cores),
        (
            f32(share, width),
            f32(share, lanes),
            jax.ShapeDtypeStruct((share, width), jnp.bfloat16),
            f32(share, LANES),
        ),
        [VMEM] * 6,
        (points, *kept, lse),
        "own",
        flops=4 * share * width * rows,
    )
    lse, acc, cnt = lax.optimization_barrier((lse, acc, cnt))
    lse_d = lax.ppermute(lse, "dp", [(i, i ^ 3) for i in range(n)])
    d0, d1, acc, cnt, lse_d = lax.optimization_barrier((d0, d1, acc, cnt, lse_d))
    lead = call(
        functools.partial(lead_kernel, cores, order, half),
        (f32(size, width), f32(size, lanes)),
        [SMEM] + [VMEM] * (6 + 4 * cores),
        (where, twice, norm, acc, cnt, *near, d0, d1),
        "lead",
        flops=4 * size * width * 2 * rows,
    )
    given = (where, twice, norm, acc, cnt, lse_d)
    far = with_siblings((d0, d1))
    rows_given = (*near, *far)
    block_sum = f32(size + 8, width)
    turn = lines // 2
    forward = list(range(turn - 1, 0, -1))
    backward = [lines - s for s in range(turn - 1, 0, -1)]
    first = call(
        functools.partial(first_kernel, cores, order, half),
        block_sum,
        [SMEM] + [VMEM] * (5 + 2 * cores),
        (where, twice, norm, lse_d, *lead, *far),
        "first",
        flops=4 * size * width * 2 * rows,
    )

    def sums_of(steps):
        made = call(
            functools.partial(rest_kernel, cores, order, half, steps),
            [block_sum] * len(steps),
            [SMEM] + [VMEM] * (5 + 6 * cores),
            (*given, *rows_given),
            "rest",
            flops=4 * size * width * 3 * rows * len(steps),
        )
        return dict(zip(steps, made))

    def plus(a, b):
        return call(add_kernel, block_sum, [VMEM] * 2, (a, b), "add")

    sums = {**sums_of(backward), **sums_of(forward + [0])}
    from_ahead = ring(sums[backward[0]], -1)
    for s in backward[1:]:
        from_ahead = ring(plus(sums[s], from_ahead), -1)
    from_behind = ring(first, 1)
    for s in forward:
        from_behind = ring(plus(sums[s], from_behind), 1)
    done = call(
        finish_kernel,
        block_sum,
        [SMEM] + [VMEM] * 4,
        (where, twice, sums[0], from_behind, from_ahead),
        "finish",
    )

    steps = [-s for s in range(1, lines // 2 + 1)] + list(range(1, lines // 2))
    got = {(0, 0): done}
    previous, older = (), (done, done)
    for s in [0] + steps:
        x = got[0, s]
        if previous:
            x = lax.optimization_barrier((x, *previous))[0]
        got[1, s], got[2, s] = exchange(x, 0), exchange(x, 1)
        if s == steps[-1]:
            break
        got[3, s] = exchange(got[1, s], 1)
        previous, older = (got[2, s], *older[:1]), (*older[1:], got[3, s])
        ahead_of = steps[([0] + steps).index(s)]
        x = got[0, ahead_of + (1 if ahead_of < 0 else -1)]
        if ahead_of > 0:
            x = lax.optimization_barrier((x, got[0, s]))[0]
        got[0, ahead_of] = ring(x, 1 if ahead_of < 0 else -1)
    before = got[3, steps[-1] - 1] if steps[-1] > 0 else got[3, steps[-1] + 1]
    before = lax.optimization_barrier((before, got[0, steps[-1]]))[0]
    got[3, steps[-1]] = ring(before, -1 if steps[-1] > 0 else 1)
    late = [(1, steps[-1]), (2, steps[-1]), (3, steps[-1])]
    middle = [(w, steps[-2]) for w in (1, 2, 3)] + [(0, steps[-1])]
    groups = ([k for k in got if k not in middle + late], middle, late)
    new = counts = None
    for later, names in enumerate(groups):
        args = [where] + [got[k] for k in names]
        if later:
            args += [counts, new]
        new, counts = call(
            functools.partial(place_kernel, names, order, later),
            (f32(local_cent, width), f32(local_cent // LANES, LANES)),
            [SMEM] + [VMEM] * len(names) + ([VMEM, ANY] if later else []),
            args,
            ("place_early", "place_middle", "place_late")[later],
            out_specs=(ANY, VMEM),
            scratch=[pltpu.SemaphoreType.DMA((len(names),))],
            aliases={len(args) - 1: 0} if later else {},
        )
    return new, counts.reshape(-1), log_evidence.reshape(-1)


def solution(mesh):
    n, cores = mesh.shape["dp"], mesh.shape["cent"]
    return jax.shard_map(
        functools.partial(body, n, cores),
        mesh=mesh,
        in_specs=(P("dp", None), P("cent", None)),
        out_specs=(P("cent", None), P("cent"), P("dp")),
        check_vma=False,
    )
```

```python
import functools
import math

import jax
import jax.numpy as jnp
from jax import lax
from jax.experimental import pallas as pl
from jax.experimental.pallas import tpu as pltpu
from jax.sharding import PartitionSpec as P

prior_mass = 0.5
VMEM_LIMIT = 48 * 1024 * 1024
LANES = 128
NT = (((1,), (1,)), ((), ()))
NN = (((1,), (0,)), ((), ()))
VMEM = pl.BlockSpec(memory_space=pltpu.VMEM)
SMEM = pl.BlockSpec(memory_space=pltpu.SMEM)
ANY = pl.BlockSpec(memory_space=pl.ANY)
HBM = pl.BlockSpec(memory_space=pltpu.HBM)


def f32(*shape):
    return jax.ShapeDtypeStruct(shape, jnp.float32)


def call(kernel, out_shape, in_specs, args, name, out_specs=None, scratch=(), flops=0, aliases={}):
    return pl.pallas_call(
        kernel,
        out_shape=out_shape,
        in_specs=in_specs,
        out_specs=jax.tree.map(lambda _: VMEM, out_shape) if out_specs is None else out_specs,
        scratch_shapes=list(scratch),
        input_output_aliases=aliases,
        compiler_params=pltpu.CompilerParams(vmem_limit_bytes=VMEM_LIMIT),
        cost_estimate=pl.CostEstimate(
            flops=flops,
            bytes_accessed=sum(a.size * a.dtype.itemsize for a in args),
            transcendentals=0,
        ),
        name=name,
    )(*args)


def open_kernel(where_ref, points_ref, first_ref, second_ref, raw_ref, sem):
    half = first_ref.shape[0]
    start = pl.multiple_of(where_ref[1] * (2 * half), 2 * half)
    copy = pltpu.make_async_copy(points_ref.at[pl.ds(start, 2 * half), :], raw_ref, sem)
    copy.start()
    copy.wait()
    first_ref[...] = raw_ref[:half, :].astype(jnp.float32)
    second_ref[...] = raw_ref[half:, :].astype(jnp.float32)


def widen(norm, width):
    if width <= norm.shape[1]:
        return norm[:, :width]
    return jnp.concatenate([norm] * (width // norm.shape[1]), axis=1)


def norms(c):
    c = c.astype(jnp.float32)
    return jnp.broadcast_to(jnp.sum(c * c, axis=1, keepdims=True), (c.shape[0], LANES))


def stats_kernel(lines, where_ref, points_ref, c_ref, out_ref, twice_ref, norm_ref, all_norm_ref):
    rows, local = points_ref.shape[0], c_ref.shape[0]
    chunk = local // lines
    tile, size = min(256, rows), chunk // 4
    kept = pl.multiple_of(lax.rem(where_ref[0], 4) * size, size)
    for l in range(lines):
        c = c_ref[l * chunk : (l + 1) * chunk, :]
        all_norm_ref[...] = norms(c)
        twice = c + c
        for start in range(0, rows, tile):
            at = slice(start, start + tile)
            dots = lax.dot_general(twice, points_ref[at, :], NT, preferred_element_type=jnp.float32)
            score = dots - widen(all_norm_ref[...], tile)
            top = jnp.max(score, axis=0, keepdims=True)
            total = jnp.sum(jnp.exp(score - top), axis=0, keepdims=True)
            if l:
                old_top, old_total = out_ref[0:1, at], out_ref[1:2, at]
                new_top = jnp.maximum(old_top, top)
                total = old_total * jnp.exp(old_top - new_top) + total * jnp.exp(top - new_top)
                top = new_top
            out_ref[0:1, at] = top
            out_ref[1:2, at] = total
        mine = c_ref[pl.ds(pl.multiple_of(l * chunk + kept, size), size), :]
        twice_ref[l * size : (l + 1) * size, :] = mine + mine
        norm_ref[l * size : (l + 1) * size, :] = all_norm_ref[pl.ds(kept, size), :]


def stats(where, points, centroids, lines):
    rows, width = points.shape
    local = centroids.shape[0]
    return call(
        functools.partial(stats_kernel, lines),
        (
            f32(2, rows),
            jax.ShapeDtypeStruct((local // 4, width), jnp.bfloat16),
            f32(local // 4, LANES),
        ),
        [SMEM, VMEM, VMEM],
        (where, points, centroids),
        "stats",
        scratch=[pltpu.VMEM((local // lines, LANES), jnp.float32)],
        flops=4 * rows * local * width,
    )


def lse_kernel(cores, every, a0_ref, b1_ref, *refs):
    pair_refs = refs[:cores]
    lse_ref, evidence_ref, pack_a_ref, pack_b_ref = refs[cores:]
    half = lse_ref.shape[1]
    top = functools.reduce(jnp.maximum, [p[0:1, :] for p in pair_refs])
    total = functools.reduce(jnp.add, [p[1:2, :] * jnp.exp(p[0:1, :] - top) for p in pair_refs])
    lse = top + jnp.log(total)
    evidence = lse - math.log(every)
    for k in range(evidence_ref.shape[0]):
        evidence_ref[k : k + 1, :] = evidence[:, k * LANES : (k + 1) * LANES]
    for i in range(2 * cores):
        lse_ref[i : i + 1, :] = lse[:, i * half : (i + 1) * half]
    for piece_ref, pack_ref in ((a0_ref, pack_a_ref), (b1_ref, pack_b_ref)):
        pack_ref[0:half, :] = piece_ref[...]
        pack_ref[half:, :] = jnp.zeros_like(pack_ref[half:, :])
        pack_ref[half : half + 2 * cores, 0:half] = lse_ref[...]


def weigh(twice, norm, x, lse, lanes):
    dots = lax.dot_general(twice, x, NT, preferred_element_type=jnp.float32)
    score = dots - widen(norm, x.shape[0])
    resp = jnp.exp(score - lse).astype(jnp.bfloat16)
    part = lax.dot_general(resp, x, NN, preferred_element_type=jnp.float32)
    wide = resp.astype(jnp.float32)
    counted = functools.reduce(
        jnp.add, [wide[:, k : k + lanes] for k in range(0, x.shape[0], lanes)]
    )
    return part, counted


def own_kernel(cores, points_ref, twice_ref, norm_ref, lse_ref, acc_ref, cnt_ref):
    half = points_ref.shape[0] // (2 * cores)
    for i in range(2 * cores):
        x = points_ref[i * half : (i + 1) * half, :]
        part, counted = weigh(
            twice_ref[...], norm_ref[...], x, lse_ref[i : i + 1, :], cnt_ref.shape[1]
        )
        if i == 0:
            acc_ref[...] = part
            cnt_ref[...] = counted
        else:
            acc_ref[...] += part
            cnt_ref[...] += counted


KINDS = ((0, 0), (1, 1), (0, 1), (1, 0))


def near_rows(cores, half, core, refs, d0_ref, d1_ref):
    for k, (kind, part) in enumerate(KINDS):
        for rc in range(cores):
            at = half + 2 * (core ^ rc) + part
            tail_ref = d1_ref if (kind + rc) % 2 == 0 else d0_ref
            yield refs[k * cores + rc], (lambda at=at, tail_ref=tail_ref: tail_ref[pl.ds(at, 1), :][:, 0:half])


def far_rows(cores, half, core, refs, lse_ref):
    for part in range(2):
        for rc in range(cores):
            at = 2 * (core ^ rc) + part
            yield refs[part * cores + rc], (lambda at=at: lse_ref[pl.ds(at, 1), :])


def add_rows(rows, half, twice, norm, acc, cnt):
    for x_ref, lse in rows:
        part, counted = weigh(twice, norm, x_ref[0:half, :].astype(jnp.bfloat16), lse(), cnt.shape[1])
        acc, cnt = acc + part, cnt + counted
    return acc, cnt


def store_sums(out_ref, acc, cnt):
    size, width = acc.shape
    turned = jnp.sum(cnt.T, axis=0, keepdims=True)
    if size < width:
        turned = jnp.concatenate([turned, jnp.zeros((1, width - size), jnp.float32)], axis=1)
    out_ref[0:size, :] = acc
    out_ref[size : size + 8, :] = jnp.broadcast_to(turned, (8, width))


def lead_kernel(cores, order, half, where_ref, twice_ref, norm_ref, acc_ref, cnt_ref, *refs):
    out_acc_ref, out_cnt_ref = refs[-2:]
    near, (d0_ref, d1_ref) = refs[: 4 * cores], refs[4 * cores : 4 * cores + 2]
    size = out_acc_ref.shape[0]
    place = ahead(order, lax.div(where_ref[0], 4), len(order) // 2)
    at = pl.ds(pl.multiple_of(place * size, size), size)
    out_acc_ref[...], out_cnt_ref[...] = add_rows(
        near_rows(cores, half, where_ref[1], near, d0_ref, d1_ref),
        half,
        twice_ref[at, :],
        norm_ref[at, :],
        acc_ref[at, :],
        cnt_ref[at, :],
    )


def block_sums(cores, order, half, steps, where_ref, twice_ref, norm_ref, acc_ref, cnt_ref, lse_ref, near, far, out_ref):
    size = out_ref.shape[0] - 8
    place = ahead(order, lax.div(where_ref[0], 4), steps)
    at = pl.ds(pl.multiple_of(place * size, size), size)
    twice, norm = twice_ref[at, :], norm_ref[at, :]
    acc, cnt = add_rows(
        near_rows(cores, half, where_ref[1], near, far[0], far[cores]),
        half,
        twice,
        norm,
        acc_ref[at, :],
        cnt_ref[at, :],
    )
    acc, cnt = add_rows(far_rows(cores, half, where_ref[1], far, lse_ref), half, twice, norm, acc, cnt)
    store_sums(out_ref, acc, cnt)


def first_kernel(cores, order, half, where_ref, twice_ref, norm_ref, lse_ref, lead_acc_ref, lead_cnt_ref, *refs):
    far, out_ref = refs[: 2 * cores], refs[2 * cores]
    size = lead_acc_ref.shape[0]
    place = ahead(order, lax.div(where_ref[0], 4), len(order) // 2)
    at = pl.ds(pl.multiple_of(place * size, size), size)
    acc, cnt = add_rows(
        far_rows(cores, half, where_ref[1], far, lse_ref),
        half,
        twice_ref[at, :],
        norm_ref[at, :],
        lead_acc_ref[...],
        lead_cnt_ref[...],
    )
    store_sums(out_ref, acc, cnt)


def rest_kernel(cores, order, half, steps, where_ref, twice_ref, norm_ref, acc_ref, cnt_ref, lse_ref, *refs):
    near, far = refs[: 4 * cores], refs[4 * cores : 6 * cores]
    for s, out_ref in zip(steps, refs[6 * cores :]):
        block_sums(
            cores, order, half, s, where_ref, twice_ref, norm_ref, acc_ref, cnt_ref, lse_ref, near, far, out_ref
        )


def ahead(order, line, steps):
    n = len(order)
    return functools.reduce(
        jnp.add,
        [jnp.where(line == order[p], order[(p + steps) % n], 0) for p in range(n)],
    )


def add_kernel(a_ref, b_ref, out_ref):
    out_ref[...] = a_ref[...] + b_ref[...]


def finish_kernel(where_ref, twice_ref, mine_ref, first_ref, second_ref, out_ref):
    size, width = out_ref.shape[0] - 8, out_ref.shape[1]
    start = pl.multiple_of(lax.div(where_ref[0], 4) * size, size)
    c = 0.5 * twice_ref[pl.ds(start, size), :].astype(jnp.float32)
    total = mine_ref[...] + first_ref[...] + second_ref[...]
    counts = total[size:, :]
    column = counts.T[:size, 0:1]
    out_ref[0:size, :] = (total[:size, :] + prior_mass * c) / (column + prior_mass)
    row = lax.broadcasted_iota(jnp.int32, (8, LANES), 0)
    spread = jnp.zeros((8, LANES), jnp.float32)
    for k in range(size // LANES):
        spread = jnp.where(row == k, counts[:, k * LANES : (k + 1) * LANES], spread)
    out_ref[size:, :] = jnp.concatenate([spread] * (width // LANES), axis=1)


def place_kernel(names, order, later, where_ref, *refs):
    count, lines = len(names), len(order)
    block_refs = refs[:count]
    new_ref, counts_ref, sems = refs[-3:]
    size = block_refs[0].shape[0] - 8
    plane, line = lax.rem(where_ref[0], 4), lax.div(where_ref[0], 4)
    each = size // LANES
    odd = lax.rem(where_ref[1], 2)
    bits = (0, 1 + odd, 2 - odd, 3)
    places = [ahead(order, line, steps) * 4 + (plane ^ bits[way]) for way, steps in names]
    copies = []
    for i in range(count):
        at = pl.multiple_of(places[i] * size, size)
        copies.append(
            pltpu.make_async_copy(block_refs[i].at[0:size, :], new_ref.at[pl.ds(at, size), :], sems.at[i])
        )
        copies[-1].start()
    if later:
        counts_ref[...] = refs[count][...]
    for i in range(count):
        for k in range(each):
            counts_ref[pl.ds(places[i] * each + k, 1), :] = block_refs[i][size + k : size + k + 1, 0:LANES]
    for copy in copies:
        copy.wait()


def body(n, cores, points, centroids):
    rows, width = points.shape
    local_cent = centroids.shape[0]
    lines = n // 4
    half = rows // (2 * cores)
    share = local_cent // 4
    size = share // lines
    order = tuple(range(0, lines, 2)) + tuple(range(1, lines, 2))[::-1]
    where = jnp.stack([lax.axis_index("dp"), lax.axis_index("cent")]).astype(jnp.int32)

    def exchange(x, kind):
        pairs = [
            (i * cores + c, (i ^ (1 if (kind + c) % 2 == 0 else 2)) * cores + c)
            for i in range(n)
            for c in range(cores)
        ]
        return lax.ppermute(x, ("dp", "cent"), pairs)

    def flip_core(x, bits):
        return lax.ppermute(x, "cent", [(i, i ^ bits) for i in range(cores)])

    def ring(x, way):
        pairs = [(order[p], order[(p + way) % lines]) for p in range(lines)]
        return lax.ppermute(x, "dp", [(4 * a + i, 4 * b + i) for a, b in pairs for i in range(4)])

    def with_siblings(pieces):
        return [a if rc == 0 else flip_core(a, rc) for a in pieces for rc in range(cores)]

    first, second = call(
        open_kernel,
        (f32(half, width), f32(half, width)),
        [SMEM, HBM],
        (where, points),
        "open",
        scratch=[pltpu.VMEM((2 * half, width), points.dtype), pltpu.SemaphoreType.DMA(())],
    )
    a0, b1 = exchange(first, 0), exchange(second, 1)
    a1, b0 = exchange(second, 0), exchange(first, 1)

    pair, twice, norm = stats(where, points, centroids, lines)
    pairs = [pair] + [flip_core(pair, rc) for rc in range(1, cores)]
    tail = max(8, 2 * cores)
    lse, log_evidence, pack_a, pack_b = call(
        functools.partial(lse_kernel, cores, local_cent * cores),
        (f32(2 * cores, half), f32(rows // LANES, LANES), f32(half + tail, width), f32(half + tail, width)),
        [VMEM] * (2 + cores),
        (a0, b1, *pairs),
        "lse",
    )
    d0, d1 = exchange(pack_a, 1), exchange(pack_b, 0)

    a0, b1, a1, b0, lse = lax.optimization_barrier((a0, b1, a1, b0, lse))
    near = with_siblings((a0, b1, a1, b0))
    lanes = min(LANES, half)
    acc, cnt = call(
        functools.partial(own_kernel, cores),
        (f32(share, width), f32(share, lanes)),
        [VMEM] * 4,
        (points, twice, norm, lse),
        "own",
        flops=4 * share * width * rows,
    )
    lse, acc, cnt, near = lax.optimization_barrier((lse, acc, cnt, near))
    lse_d = lax.ppermute(lse, "dp", [(i, i ^ 3) for i in range(n)])
    near, d0, d1, acc, cnt, lse_d = lax.optimization_barrier((near, d0, d1, acc, cnt, lse_d))
    lead = call(
        functools.partial(lead_kernel, cores, order, half),
        (f32(size, width), f32(size, lanes)),
        [SMEM] + [VMEM] * (6 + 4 * cores),
        (where, twice, norm, acc, cnt, *near, d0, d1),
        "lead",
        flops=4 * size * width * 2 * rows,
    )
    given = (where, twice, norm, acc, cnt, lse_d)
    far = with_siblings((d0, d1))
    rows_given = (*near, *far)
    block_sum = f32(size + 8, width)
    turn = lines // 2
    forward = list(range(turn - 1, 0, -1))
    backward = [lines - s for s in range(turn - 1, 0, -1)]
    first = call(
        functools.partial(first_kernel, cores, order, half),
        block_sum,
        [SMEM] + [VMEM] * (5 + 2 * cores),
        (where, twice, norm, lse_d, *lead, *far),
        "first",
        flops=4 * size * width * 2 * rows,
    )

    def sums_of(steps):
        made = call(
            functools.partial(rest_kernel, cores, order, half, steps),
            [block_sum] * len(steps),
            [SMEM] + [VMEM] * (5 + 6 * cores),
            (*given, *rows_given),
            "rest",
            flops=4 * size * width * 3 * rows * len(steps),
        )
        return dict(zip(steps, made))

    def plus(a, b):
        return call(add_kernel, block_sum, [VMEM] * 2, (a, b), "add")

    sums = {**sums_of(backward), **sums_of(forward + [0])}
    from_ahead = ring(sums[backward[0]], -1)
    for s in backward[1:]:
        from_ahead = ring(plus(sums[s], from_ahead), -1)
    from_behind = ring(first, 1)
    for s in forward:
        from_behind = ring(plus(sums[s], from_behind), 1)
    done = call(
        finish_kernel,
        block_sum,
        [SMEM] + [VMEM] * 4,
        (where, twice, sums[0], from_behind, from_ahead),
        "finish",
    )

    steps = [-s for s in range(1, lines // 2 + 1)] + list(range(1, lines // 2))
    got = {(0, 0): done}
    previous, older, plane_b = (), (done, done), [done]
    for s in [0] + steps:
        x = got[0, s]
        if previous:
            x = lax.optimization_barrier((x, *previous))[0]
        got[1, s], got[2, s] = exchange(x, 0), exchange(x, 1)
        if s == steps[-1]:
            break
        got[3, s] = exchange(got[1, s], 1)
        plane_b.append(got[2, s])
        previous, older = (plane_b[-2 if s == steps[-2] else -1], *older[:1]), (*older[1:], got[3, s])
        ahead_of = steps[([0] + steps).index(s)]
        x = got[0, ahead_of + (1 if ahead_of < 0 else -1)]
        if ahead_of > 0:
            x = lax.optimization_barrier((x, got[0, s]))[0]
        got[0, ahead_of] = ring(x, 1 if ahead_of < 0 else -1)
    before = got[3, steps[-1] - 1] if steps[-1] > 0 else got[3, steps[-1] + 1]
    before = lax.optimization_barrier((before, got[0, steps[-1]]))[0]
    got[3, steps[-1]] = ring(before, -1 if steps[-1] > 0 else 1)
    late = [(1, steps[-1]), (2, steps[-1]), (3, steps[-1])]
    middle = [(w, steps[-2]) for w in (1, 2, 3)] + [(0, steps[-1])]
    groups = ([k for k in got if k not in middle + late], middle, late)
    new = counts = None
    for later, names in enumerate(groups):
        args = [where] + [got[k] for k in names]
        if later:
            args += [counts, new]
        new, counts = call(
            functools.partial(place_kernel, names, order, later),
            (f32(local_cent, width), f32(local_cent // LANES, LANES)),
            [SMEM] + [VMEM] * len(names) + ([VMEM, ANY] if later else []),
            args,
            ("place_early", "place_middle", "place_late")[later],
            out_specs=(ANY, VMEM),
            scratch=[pltpu.SemaphoreType.DMA((len(names),))],
            aliases={len(args) - 1: 0} if later else {},
        )
    return new, counts.reshape(-1), log_evidence.reshape(-1)


def solution(mesh):
    n, cores = mesh.shape["dp"], mesh.shape["cent"]
    return jax.shard_map(
        functools.partial(body, n, cores),
        mesh=mesh,
        in_specs=(P("dp", None), P("cent", None)),
        out_specs=(P("cent", None), P("cent"), P("dp")),
        check_vma=False,
    )
```

```python
import functools
import math

import jax
import jax.numpy as jnp
from jax import lax
from jax.experimental import pallas as pl
from jax.experimental.pallas import tpu as pltpu
from jax.sharding import PartitionSpec as P

prior_mass = 0.5
VMEM_LIMIT = 24 * 1024 * 1024
LANES = 128
NT = (((1,), (1,)), ((), ()))
NN = (((1,), (0,)), ((), ()))
VMEM = pl.BlockSpec(memory_space=pltpu.VMEM)
SMEM = pl.BlockSpec(memory_space=pltpu.SMEM)
ANY = pl.BlockSpec(memory_space=pl.ANY)
HBM = pl.BlockSpec(memory_space=pltpu.HBM)


def f32(*shape):
    return jax.ShapeDtypeStruct(shape, jnp.float32)


def call(kernel, out_shape, in_specs, args, name, out_specs=None, scratch=(), flops=0, aliases={}, vmem=VMEM_LIMIT):
    return pl.pallas_call(
        kernel,
        out_shape=out_shape,
        in_specs=in_specs,
        out_specs=jax.tree.map(lambda _: VMEM, out_shape) if out_specs is None else out_specs,
        scratch_shapes=list(scratch),
        input_output_aliases=aliases,
        compiler_params=pltpu.CompilerParams(vmem_limit_bytes=vmem),
        cost_estimate=pl.CostEstimate(
            flops=flops,
            bytes_accessed=sum(a.size * a.dtype.itemsize for a in args),
            transcendentals=0,
        ),
        name=name,
    )(*args)


def open_kernel(where_ref, points_ref, first_ref, second_ref, raw_ref, sem):
    half = first_ref.shape[0]
    start = pl.multiple_of(where_ref[1] * (2 * half), 2 * half)
    copy = pltpu.make_async_copy(points_ref.at[pl.ds(start, 2 * half), :], raw_ref, sem)
    copy.start()
    copy.wait()
    first_ref[...] = raw_ref[:half, :].astype(jnp.float32)
    second_ref[...] = raw_ref[half:, :].astype(jnp.float32)


def widen(norm, width):
    if width <= norm.shape[1]:
        return norm[:, :width]
    return jnp.concatenate([norm] * (width // norm.shape[1]), axis=1)


def norms(c):
    c = c.astype(jnp.float32)
    return jnp.broadcast_to(jnp.sum(c * c, axis=1, keepdims=True), (c.shape[0], LANES))


def stats_kernel(lines, where_ref, points_ref, c_ref, out_ref, twice_ref, norm_ref, all_norm_ref):
    rows, local = points_ref.shape[0], c_ref.shape[0]
    chunk = local // lines
    tile, size = min(256, rows), chunk // 4
    kept = pl.multiple_of(lax.rem(where_ref[0], 4) * size, size)
    for l in range(lines):
        c = c_ref[l * chunk : (l + 1) * chunk, :]
        all_norm_ref[...] = norms(c)
        twice = c + c
        for start in range(0, rows, tile):
            at = slice(start, start + tile)
            dots = lax.dot_general(twice, points_ref[at, :], NT, preferred_element_type=jnp.float32)
            score = dots - widen(all_norm_ref[...], tile)
            top = jnp.max(score, axis=0, keepdims=True)
            total = jnp.sum(jnp.exp(score - top), axis=0, keepdims=True)
            if l:
                old_top, old_total = out_ref[0:1, at], out_ref[1:2, at]
                new_top = jnp.maximum(old_top, top)
                total = old_total * jnp.exp(old_top - new_top) + total * jnp.exp(top - new_top)
                top = new_top
            out_ref[0:1, at] = top
            out_ref[1:2, at] = total
        mine = c_ref[pl.ds(pl.multiple_of(l * chunk + kept, size), size), :]
        twice_ref[l * size : (l + 1) * size, :] = mine + mine
        norm_ref[l * size : (l + 1) * size, :] = all_norm_ref[pl.ds(kept, size), :]


def stats(where, points, centroids, lines):
    rows, width = points.shape
    local = centroids.shape[0]
    return call(
        functools.partial(stats_kernel, lines),
        (
            f32(2, rows),
            jax.ShapeDtypeStruct((local // 4, width), jnp.bfloat16),
            f32(local // 4, LANES),
        ),
        [SMEM, VMEM, VMEM],
        (where, points, centroids),
        "stats",
        scratch=[pltpu.VMEM((local // lines, LANES), jnp.float32)],
        flops=4 * rows * local * width,
    )


def lse_kernel(cores, every, a0_ref, b1_ref, *refs):
    pair_refs = refs[:cores]
    lse_ref, evidence_ref, pack_a_ref, pack_b_ref = refs[cores:]
    half = lse_ref.shape[1]
    top = functools.reduce(jnp.maximum, [p[0:1, :] for p in pair_refs])
    total = functools.reduce(jnp.add, [p[1:2, :] * jnp.exp(p[0:1, :] - top) for p in pair_refs])
    lse = top + jnp.log(total)
    evidence = lse - math.log(every)
    for k in range(evidence_ref.shape[0]):
        evidence_ref[k : k + 1, :] = evidence[:, k * LANES : (k + 1) * LANES]
    for i in range(2 * cores):
        lse_ref[i : i + 1, :] = lse[:, i * half : (i + 1) * half]
    for piece_ref, pack_ref in ((a0_ref, pack_a_ref), (b1_ref, pack_b_ref)):
        pack_ref[0:half, :] = piece_ref[...]
        pack_ref[half:, :] = jnp.zeros_like(pack_ref[half:, :])
        pack_ref[half : half + 2 * cores, 0:half] = lse_ref[...]


def weigh(twice, norm, x, lse, lanes):
    dots = lax.dot_general(twice, x, NT, preferred_element_type=jnp.float32)
    score = dots - widen(norm, x.shape[0])
    resp = jnp.exp(score - lse).astype(jnp.bfloat16)
    part = lax.dot_general(resp, x, NN, preferred_element_type=jnp.float32)
    wide = resp.astype(jnp.float32)
    counted = functools.reduce(
        jnp.add, [wide[:, k : k + lanes] for k in range(0, x.shape[0], lanes)]
    )
    return part, counted


def own_kernel(cores, points_ref, twice_ref, norm_ref, lse_ref, acc_ref, cnt_ref):
    half = points_ref.shape[0] // (2 * cores)
    for i in range(2 * cores):
        x = points_ref[i * half : (i + 1) * half, :]
        part, counted = weigh(
            twice_ref[...], norm_ref[...], x, lse_ref[i : i + 1, :], cnt_ref.shape[1]
        )
        if i == 0:
            acc_ref[...] = part
            cnt_ref[...] = counted
        else:
            acc_ref[...] += part
            cnt_ref[...] += counted


KINDS = ((0, 0), (1, 1), (0, 1), (1, 0))


def near_rows(cores, half, core, refs, d0_ref, d1_ref):
    for k, (kind, part) in enumerate(KINDS):
        for rc in range(cores):
            at = half + 2 * (core ^ rc) + part
            tail_ref = d1_ref if (kind + rc) % 2 == 0 else d0_ref
            yield refs[k * cores + rc], (lambda at=at, tail_ref=tail_ref: tail_ref[pl.ds(at, 1), :][:, 0:half])


def far_rows(cores, half, core, refs, lse_ref):
    for part in range(2):
        for rc in range(cores):
            at = 2 * (core ^ rc) + part
            yield refs[part * cores + rc], (lambda at=at: lse_ref[pl.ds(at, 1), :])


def add_rows(rows, half, twice, norm, acc, cnt):
    for x_ref, lse in rows:
        part, counted = weigh(twice, norm, x_ref[0:half, :].astype(jnp.bfloat16), lse(), cnt.shape[1])
        acc, cnt = acc + part, cnt + counted
    return acc, cnt


def store_sums(out_ref, acc, cnt):
    size, width = acc.shape
    turned = jnp.sum(cnt.T, axis=0, keepdims=True)
    if size < width:
        turned = jnp.concatenate([turned, jnp.zeros((1, width - size), jnp.float32)], axis=1)
    out_ref[0:size, :] = acc
    out_ref[size : size + 8, :] = jnp.broadcast_to(turned, (8, width))


def lead_kernel(cores, order, half, where_ref, twice_ref, norm_ref, acc_ref, cnt_ref, *refs):
    out_acc_ref, out_cnt_ref = refs[-2:]
    near, (d0_ref, d1_ref) = refs[: 4 * cores], refs[4 * cores : 4 * cores + 2]
    size = out_acc_ref.shape[0]
    place = ahead(order, lax.div(where_ref[0], 4), len(order) // 2)
    at = pl.ds(pl.multiple_of(place * size, size), size)
    out_acc_ref[...], out_cnt_ref[...] = add_rows(
        near_rows(cores, half, where_ref[1], near, d0_ref, d1_ref),
        half,
        twice_ref[at, :],
        norm_ref[at, :],
        acc_ref[at, :],
        cnt_ref[at, :],
    )


def block_sums(cores, order, half, steps, where_ref, twice_ref, norm_ref, acc_ref, cnt_ref, lse_ref, near, far, out_ref):
    size = out_ref.shape[0] - 8
    place = ahead(order, lax.div(where_ref[0], 4), steps)
    at = pl.ds(pl.multiple_of(place * size, size), size)
    twice, norm = twice_ref[at, :], norm_ref[at, :]
    acc, cnt = add_rows(
        near_rows(cores, half, where_ref[1], near, far[0], far[cores]),
        half,
        twice,
        norm,
        acc_ref[at, :],
        cnt_ref[at, :],
    )
    acc, cnt = add_rows(far_rows(cores, half, where_ref[1], far, lse_ref), half, twice, norm, acc, cnt)
    store_sums(out_ref, acc, cnt)


def first_kernel(cores, order, half, where_ref, twice_ref, norm_ref, lse_ref, lead_acc_ref, lead_cnt_ref, *refs):
    far, out_ref = refs[: 2 * cores], refs[2 * cores]
    size = lead_acc_ref.shape[0]
    place = ahead(order, lax.div(where_ref[0], 4), len(order) // 2)
    at = pl.ds(pl.multiple_of(place * size, size), size)
    acc, cnt = add_rows(
        far_rows(cores, half, where_ref[1], far, lse_ref),
        half,
        twice_ref[at, :],
        norm_ref[at, :],
        lead_acc_ref[...],
        lead_cnt_ref[...],
    )
    store_sums(out_ref, acc, cnt)


def rest_kernel(cores, order, half, steps, where_ref, twice_ref, norm_ref, acc_ref, cnt_ref, lse_ref, *refs):
    near, far = refs[: 4 * cores], refs[4 * cores : 6 * cores]
    for s, out_ref in zip(steps, refs[6 * cores :]):
        block_sums(
            cores, order, half, s, where_ref, twice_ref, norm_ref, acc_ref, cnt_ref, lse_ref, near, far, out_ref
        )


def ahead(order, line, steps):
    n = len(order)
    return functools.reduce(
        jnp.add,
        [jnp.where(line == order[p], order[(p + steps) % n], 0) for p in range(n)],
    )


def add_kernel(a_ref, b_ref, out_ref):
    out_ref[...] = a_ref[...] + b_ref[...]


def finish_kernel(where_ref, twice_ref, mine_ref, first_ref, second_ref, out_ref):
    size, width = out_ref.shape[0] - 8, out_ref.shape[1]
    start = pl.multiple_of(lax.div(where_ref[0], 4) * size, size)
    c = 0.5 * twice_ref[pl.ds(start, size), :].astype(jnp.float32)
    total = mine_ref[...] + first_ref[...] + second_ref[...]
    counts = total[size:, :]
    column = counts.T[:size, 0:1]
    out_ref[0:size, :] = (total[:size, :] + prior_mass * c) / (column + prior_mass)
    row = lax.broadcasted_iota(jnp.int32, (8, LANES), 0)
    spread = jnp.zeros((8, LANES), jnp.float32)
    for k in range(size // LANES):
        spread = jnp.where(row == k, counts[:, k * LANES : (k + 1) * LANES], spread)
    out_ref[size:, :] = jnp.concatenate([spread] * (width // LANES), axis=1)


def place_kernel(names, order, later, where_ref, *refs):
    count, lines = len(names), len(order)
    block_refs = refs[:count]
    new_ref, counts_out_ref, counts_ref, sems = refs[-4:]
    size = block_refs[0].shape[0] - 8
    plane, line = lax.rem(where_ref[0], 4), lax.div(where_ref[0], 4)
    each = size // LANES
    odd = lax.rem(where_ref[1], 2)
    bits = (0, 1 + odd, 2 - odd, 3)
    places = [ahead(order, line, steps) * 4 + (plane ^ bits[way]) for way, steps in names]
    copies = []
    for i in range(count):
        at = pl.multiple_of(places[i] * size, size)
        copies.append(
            pltpu.make_async_copy(block_refs[i].at[0:size, :], new_ref.at[pl.ds(at, size), :], sems.at[i])
        )
        copies[-1].start()
    if later:
        counts_ref[...] = refs[count][...]
    for i in range(count):
        for k in range(each):
            counts_ref[pl.ds(places[i] * each + k, 1), :] = block_refs[i][size + k : size + k + 1, 0:LANES]
    copies.append(pltpu.make_async_copy(counts_ref, counts_out_ref, sems.at[count]))
    copies[-1].start()
    for copy in copies:
        copy.wait()


def body(n, cores, points, centroids):
    rows, width = points.shape
    local_cent = centroids.shape[0]
    lines = n // 4
    half = rows // (2 * cores)
    share = local_cent // 4
    size = share // lines
    order = tuple(range(0, lines, 2)) + tuple(range(1, lines, 2))[::-1]
    where = jnp.stack([lax.axis_index("dp"), lax.axis_index("cent")]).astype(jnp.int32)

    def exchange(x, kind):
        pairs = [
            (i * cores + c, (i ^ (1 if (kind + c) % 2 == 0 else 2)) * cores + c)
            for i in range(n)
            for c in range(cores)
        ]
        return lax.ppermute(x, ("dp", "cent"), pairs)

    def flip_core(x, bits):
        return lax.ppermute(x, "cent", [(i, i ^ bits) for i in range(cores)])

    def ring(x, way):
        pairs = [(order[p], order[(p + way) % lines]) for p in range(lines)]
        return lax.ppermute(x, "dp", [(4 * a + i, 4 * b + i) for a, b in pairs for i in range(4)])

    def with_siblings(pieces):
        return [a if rc == 0 else flip_core(a, rc) for a in pieces for rc in range(cores)]

    first, second = call(
        open_kernel,
        (f32(half, width), f32(half, width)),
        [SMEM, HBM],
        (where, points),
        "open",
        scratch=[pltpu.VMEM((2 * half, width), points.dtype), pltpu.SemaphoreType.DMA(())],
        vmem=62 * 1024 * 1024,
    )
    a0, b1 = exchange(first, 0), exchange(second, 1)
    a1, b0 = exchange(second, 0), exchange(first, 1)

    pair, twice, norm = stats(where, points, centroids, lines)
    pairs = [pair] + [flip_core(pair, rc) for rc in range(1, cores)]
    tail = max(8, 2 * cores)
    lse, log_evidence, pack_a, pack_b = call(
        functools.partial(lse_kernel, cores, local_cent * cores),
        (f32(2 * cores, half), f32(rows // LANES, LANES), f32(half + tail, width), f32(half + tail, width)),
        [VMEM] * (2 + cores),
        (a0, b1, *pairs),
        "lse",
    )
    d0, d1 = exchange(pack_a, 1), exchange(pack_b, 0)

    a0, b1, a1, b0, lse = lax.optimization_barrier((a0, b1, a1, b0, lse))
    near = with_siblings((a0, b1, a1, b0))
    lanes = min(LANES, half)
    acc, cnt = call(
        functools.partial(own_kernel, cores),
        (f32(share, width), f32(share, lanes)),
        [VMEM] * 4,
        (points, twice, norm, lse),
        "own",
        flops=4 * share * width * rows,
    )
    lse, acc, cnt, near = lax.optimization_barrier((lse, acc, cnt, near))
    lse_d = lax.ppermute(lse, "dp", [(i, i ^ 3) for i in range(n)])
    near, d0, d1, acc, cnt, lse_d = lax.optimization_barrier((near, d0, d1, acc, cnt, lse_d))
    lead = call(
        functools.partial(lead_kernel, cores, order, half),
        (f32(size, width), f32(size, lanes)),
        [SMEM] + [VMEM] * (6 + 4 * cores),
        (where, twice, norm, acc, cnt, *near, d0, d1),
        "lead",
        flops=4 * size * width * 2 * rows,
    )
    given = (where, twice, norm, acc, cnt, lse_d)
    far = with_siblings((d0, d1))
    rows_given = (*near, *far)
    block_sum = f32(size + 8, width)
    turn = lines // 2
    forward = list(range(turn - 1, 0, -1))
    backward = [lines - s for s in range(turn - 1, 0, -1)]
    first = call(
        functools.partial(first_kernel, cores, order, half),
        block_sum,
        [SMEM] + [VMEM] * (5 + 2 * cores),
        (where, twice, norm, lse_d, *lead, *far),
        "first",
        flops=4 * size * width * 2 * rows,
    )

    def sums_of(steps):
        made = call(
            functools.partial(rest_kernel, cores, order, half, steps),
            [block_sum] * len(steps),
            [SMEM] + [VMEM] * (5 + 6 * cores),
            (*given, *rows_given),
            "rest",
            flops=4 * size * width * 3 * rows * len(steps),
        )
        return dict(zip(steps, made))

    def plus(a, b):
        return call(add_kernel, block_sum, [VMEM] * 2, (a, b), "add")

    sums = {**sums_of(backward), **sums_of(forward + [0])}
    from_ahead = ring(sums[backward[0]], -1)
    for s in backward[1:]:
        from_ahead = ring(plus(sums[s], from_ahead), -1)
    from_behind = ring(first, 1)
    for s in forward:
        from_behind = ring(plus(sums[s], from_behind), 1)
    done = call(
        finish_kernel,
        block_sum,
        [SMEM] + [VMEM] * 4,
        (where, twice, sums[0], from_behind, from_ahead),
        "finish",
    )

    steps = [-s for s in range(1, lines // 2 + 1)] + list(range(1, lines // 2))
    got = {(0, 0): done}

    def after(x, *names):
        return lax.optimization_barrier((x, *(got[k] for k in names)))[0]

    def plane(s, *names):
        x = after(got[0, s], *names) if names else got[0, s]
        got[1, s], got[2, s] = exchange(x, 0), exchange(x, 1)

    got[0, -1] = ring(done, 1)
    plane(0)
    for s in steps[1:]:
        if s < 0:
            got[0, s] = ring(got[0, s + 1], 1)
        elif s == 1:
            got[0, s] = ring(after(done, (0, -1), (1, 0), (2, 0)), -1)
        else:
            got[0, s] = ring(got[0, s - 1], -1)
    plane(-1, (1, 0), (2, 0))
    got[3, 0] = exchange(got[1, 0], 1)
    before = [(1, -1), (2, -1)]
    for s in steps[1:]:
        plane(s, *before)
        before = [(3, 0)] if s == steps[-2] else [(2, s)]
    got[3, 1] = ring(after(got[3, 0], (0, 1)), -1)
    got[3, -1] = ring(after(got[3, 0], (0, 1)), 1)
    for s in steps:
        if abs(s) > 1:
            got[3, s] = exchange(got[1, s], 1)
    late = [(3, -1), (2, 1)]
    middle = [(1, 1), (3, 1), (3, -lines // 2)]
    groups = ([k for k in got if k not in middle + late], middle, late)
    new = counts = None
    for later, names in enumerate(groups):
        args = [where] + [got[k] for k in names]
        if later:
            args += [counts, new]
        new, counts = call(
            functools.partial(place_kernel, names, order, later),
            (f32(local_cent, width), f32(local_cent // LANES, LANES)),
            [SMEM] + [VMEM] * len(names) + ([VMEM, ANY] if later else []),
            args,
            ("place_early", "place_middle", "place_late")[later],
            out_specs=(ANY, ANY),
            scratch=[
                pltpu.VMEM((local_cent // LANES, LANES), jnp.float32),
                pltpu.SemaphoreType.DMA((len(names) + 1,)),
            ],
            aliases={len(args) - 1: 0} if later else {},
        )
    return new, counts.reshape(-1), log_evidence.reshape(-1)


def solution(mesh):
    n, cores = mesh.shape["dp"], mesh.shape["cent"]
    return jax.shard_map(
        functools.partial(body, n, cores),
        mesh=mesh,
        in_specs=(P("dp", None), P("cent", None)),
        out_specs=(P("cent", None), P("cent"), P("dp")),
        check_vma=False,
    )
```

```python
import functools
import math

import jax
import jax.numpy as jnp
from jax import lax
from jax.experimental import pallas as pl
from jax.experimental.pallas import tpu as pltpu
from jax.sharding import PartitionSpec as P

prior_mass = 0.5
VMEM_LIMIT = 24 * 1024 * 1024
LANES = 128
NT = (((1,), (1,)), ((), ()))
NN = (((1,), (0,)), ((), ()))
VMEM = pl.BlockSpec(memory_space=pltpu.VMEM)
SMEM = pl.BlockSpec(memory_space=pltpu.SMEM)
ANY = pl.BlockSpec(memory_space=pl.ANY)
HBM = pl.BlockSpec(memory_space=pltpu.HBM)


def f32(*shape):
    return jax.ShapeDtypeStruct(shape, jnp.float32)


def call(kernel, out_shape, in_specs, args, name, out_specs=None, scratch=(), flops=0, aliases={}):
    return pl.pallas_call(
        kernel,
        out_shape=out_shape,
        in_specs=in_specs,
        out_specs=jax.tree.map(lambda _: VMEM, out_shape) if out_specs is None else out_specs,
        scratch_shapes=list(scratch),
        input_output_aliases=aliases,
        compiler_params=pltpu.CompilerParams(vmem_limit_bytes=VMEM_LIMIT),
        cost_estimate=pl.CostEstimate(
            flops=flops,
            bytes_accessed=sum(a.size * a.dtype.itemsize for a in args),
            transcendentals=0,
        ),
        name=name,
    )(*args)


def open_kernel(where_ref, points_ref, out_ref):
    block = out_ref.shape[0]
    start = pl.multiple_of(where_ref[1] * block, block)
    out_ref[...] = points_ref[pl.ds(start, block), :].astype(jnp.float32)


def widen(norm, width):
    if width <= norm.shape[1]:
        return norm[:, :width]
    return jnp.concatenate([norm] * (width // norm.shape[1]), axis=1)


def norms(c):
    c = c.astype(jnp.float32)
    return jnp.broadcast_to(jnp.sum(c * c, axis=1, keepdims=True), (c.shape[0], LANES))


def stats_kernel(lines, where_ref, points_ref, c_ref, out_ref, twice_ref, norm_ref, all_norm_ref):
    rows, local = points_ref.shape[0], c_ref.shape[0]
    chunk = local // lines
    tile, size = min(256, rows), chunk // 4
    kept = pl.multiple_of(lax.rem(where_ref[0], 4) * size, size)
    for l in range(lines):
        c = c_ref[l * chunk : (l + 1) * chunk, :]
        all_norm_ref[...] = norms(c)
        twice = c + c
        for start in range(0, rows, tile):
            at = slice(start, start + tile)
            dots = lax.dot_general(twice, points_ref[at, :], NT, preferred_element_type=jnp.float32)
            score = dots - widen(all_norm_ref[...], tile)
            top = jnp.max(score, axis=0, keepdims=True)
            total = jnp.sum(jnp.exp(score - top), axis=0, keepdims=True)
            if l:
                old_top, old_total = out_ref[0:1, at], out_ref[1:2, at]
                new_top = jnp.maximum(old_top, top)
                total = old_total * jnp.exp(old_top - new_top) + total * jnp.exp(top - new_top)
                top = new_top
            out_ref[0:1, at] = top
            out_ref[1:2, at] = total
        mine = c_ref[pl.ds(pl.multiple_of(l * chunk + kept, size), size), :]
        twice_ref[l * size : (l + 1) * size, :] = mine + mine
        norm_ref[l * size : (l + 1) * size, :] = all_norm_ref[pl.ds(kept, size), :]


def stats(where, points, centroids, lines):
    rows, width = points.shape
    local = centroids.shape[0]
    return call(
        functools.partial(stats_kernel, lines),
        (
            f32(2, rows),
            jax.ShapeDtypeStruct((local // 4, width), jnp.bfloat16),
            f32(local // 4, LANES),
        ),
        [SMEM, VMEM, VMEM],
        (where, points, centroids),
        "stats",
        scratch=[pltpu.VMEM((local // lines, LANES), jnp.float32)],
        flops=4 * rows * local * width,
    )


def lse_kernel(cores, every, a_ref, b_ref, *refs):
    pair_refs = refs[:cores]
    lse_ref, evidence_ref, pack_a_ref, pack_b_ref = refs[cores:]
    half = lse_ref.shape[1]
    top = functools.reduce(jnp.maximum, [p[0:1, :] for p in pair_refs])
    total = functools.reduce(jnp.add, [p[1:2, :] * jnp.exp(p[0:1, :] - top) for p in pair_refs])
    lse = top + jnp.log(total)
    evidence = lse - math.log(every)
    for k in range(evidence_ref.shape[0]):
        evidence_ref[k : k + 1, :] = evidence[:, k * LANES : (k + 1) * LANES]
    for i in range(2 * cores):
        lse_ref[i : i + 1, :] = lse[:, i * half : (i + 1) * half]
    for piece, pack_ref in ((a_ref[0:half, :], pack_a_ref), (b_ref[half:, :], pack_b_ref)):
        pack_ref[0:half, :] = piece
        pack_ref[half:, :] = jnp.zeros_like(pack_ref[half:, :])
        pack_ref[half : half + 2 * cores, 0:half] = lse_ref[...]


def weigh(twice, norm, x, lse, lanes):
    dots = lax.dot_general(twice, x, NT, preferred_element_type=jnp.float32)
    score = dots - widen(norm, x.shape[0])
    resp = jnp.exp(score - lse).astype(jnp.bfloat16)
    part = lax.dot_general(resp, x, NN, preferred_element_type=jnp.float32)
    wide = resp.astype(jnp.float32)
    counted = functools.reduce(
        jnp.add, [wide[:, k : k + lanes] for k in range(0, x.shape[0], lanes)]
    )
    return part, counted


def two_rows(ref, at, half):
    return jnp.concatenate([ref[pl.ds(at, 1), :][:, 0:half], ref[pl.ds(at + 1, 1), :][:, 0:half]], axis=1)


def own_kernel(cores, points_ref, twice_ref, norm_ref, lse_ref, acc_ref, cnt_ref):
    half = points_ref.shape[0] // (2 * cores)
    for i in range(cores):
        x = points_ref[2 * i * half : 2 * (i + 1) * half, :]
        lse = two_rows(lse_ref, 2 * i, half)
        part, counted = weigh(twice_ref[...], norm_ref[...], x, lse, cnt_ref.shape[1])
        if i == 0:
            acc_ref[...] = part
            cnt_ref[...] = counted
        else:
            acc_ref[...] += part
            cnt_ref[...] += counted


def near_rows(cores, half, core, refs, d0_ref, d1_ref):
    for kind in range(2):
        for rc in range(cores):
            tail_ref = d1_ref if (kind + rc) % 2 == 0 else d0_ref
            at = half + 2 * (core ^ rc)
            yield (lambda ref=refs[kind * cores + rc]: ref[...]), (
                lambda at=at, tail_ref=tail_ref: two_rows(tail_ref, at, half)
            )


def far_rows(cores, half, core, refs, lse_ref):
    for rc in range(cores):
        yield (
            lambda rc=rc: jnp.concatenate([refs[rc][0:half, :], refs[cores + rc][0:half, :]], axis=0)
        ), (lambda at=2 * (core ^ rc): two_rows(lse_ref, at, half))


def add_rows(rows, half, twice, norm, acc, cnt):
    for x, lse in rows:
        part, counted = weigh(twice, norm, x().astype(jnp.bfloat16), lse(), cnt.shape[1])
        acc, cnt = acc + part, cnt + counted
    return acc, cnt


def store_sums(out_ref, acc, cnt):
    size, width = acc.shape
    turned = jnp.sum(cnt.T, axis=0, keepdims=True)
    if size < width:
        turned = jnp.concatenate([turned, jnp.zeros((1, width - size), jnp.float32)], axis=1)
    out_ref[0:size, :] = acc
    out_ref[size : size + 8, :] = jnp.broadcast_to(turned, (8, width))


def lead_kernel(cores, order, half, where_ref, twice_ref, norm_ref, acc_ref, cnt_ref, *refs):
    out_acc_ref, out_cnt_ref = refs[-2:]
    near, (d0_ref, d1_ref) = refs[: 2 * cores], refs[2 * cores : 2 * cores + 2]
    size = out_acc_ref.shape[0]
    place = ahead(order, lax.div(where_ref[0], 4), len(order) // 2)
    at = pl.ds(pl.multiple_of(place * size, size), size)
    out_acc_ref[...], out_cnt_ref[...] = add_rows(
        near_rows(cores, half, where_ref[1], near, d0_ref, d1_ref),
        half,
        twice_ref[at, :],
        norm_ref[at, :],
        acc_ref[at, :],
        cnt_ref[at, :],
    )


def block_sums(cores, order, half, steps, where_ref, twice_ref, norm_ref, acc_ref, cnt_ref, lse_ref, near, far, out_ref):
    size = out_ref.shape[0] - 8
    place = ahead(order, lax.div(where_ref[0], 4), steps)
    at = pl.ds(pl.multiple_of(place * size, size), size)
    twice, norm = twice_ref[at, :], norm_ref[at, :]
    acc, cnt = add_rows(
        near_rows(cores, half, where_ref[1], near, far[0], far[cores]),
        half,
        twice,
        norm,
        acc_ref[at, :],
        cnt_ref[at, :],
    )
    acc, cnt = add_rows(far_rows(cores, half, where_ref[1], far, lse_ref), half, twice, norm, acc, cnt)
    store_sums(out_ref, acc, cnt)


def first_kernel(cores, order, half, where_ref, twice_ref, norm_ref, lse_ref, lead_acc_ref, lead_cnt_ref, *refs):
    far, out_ref = refs[: 2 * cores], refs[2 * cores]
    size = lead_acc_ref.shape[0]
    place = ahead(order, lax.div(where_ref[0], 4), len(order) // 2)
    at = pl.ds(pl.multiple_of(place * size, size), size)
    acc, cnt = add_rows(
        far_rows(cores, half, where_ref[1], far, lse_ref),
        half,
        twice_ref[at, :],
        norm_ref[at, :],
        lead_acc_ref[...],
        lead_cnt_ref[...],
    )
    store_sums(out_ref, acc, cnt)


def rest_kernel(cores, order, half, steps, where_ref, twice_ref, norm_ref, acc_ref, cnt_ref, lse_ref, *refs):
    near, far = refs[: 2 * cores], refs[2 * cores : 4 * cores]
    for s, out_ref in zip(steps, refs[4 * cores :]):
        block_sums(
            cores, order, half, s, where_ref, twice_ref, norm_ref, acc_ref, cnt_ref, lse_ref, near, far, out_ref
        )


def ahead(order, line, steps):
    n = len(order)
    return functools.reduce(
        jnp.add,
        [jnp.where(line == order[p], order[(p + steps) % n], 0) for p in range(n)],
    )


def add_kernel(a_ref, b_ref, out_ref):
    out_ref[...] = a_ref[...] + b_ref[...]


def finish_kernel(where_ref, twice_ref, mine_ref, first_ref, second_ref, out_ref):
    size, width = out_ref.shape[0] - 8, out_ref.shape[1]
    start = pl.multiple_of(lax.div(where_ref[0], 4) * size, size)
    c = 0.5 * twice_ref[pl.ds(start, size), :].astype(jnp.float32)
    total = mine_ref[...] + first_ref[...] + second_ref[...]
    counts = total[size:, :]
    column = counts.T[:size, 0:1]
    out_ref[0:size, :] = (total[:size, :] + prior_mass * c) / (column + prior_mass)
    row = lax.broadcasted_iota(jnp.int32, (8, LANES), 0)
    spread = jnp.zeros((8, LANES), jnp.float32)
    for k in range(size // LANES):
        spread = jnp.where(row == k, counts[:, k * LANES : (k + 1) * LANES], spread)
    out_ref[size:, :] = jnp.concatenate([spread] * (width // LANES), axis=1)


def place_kernel(names, order, later, where_ref, *refs):
    count, lines = len(names), len(order)
    block_refs = refs[:count]
    new_ref, counts_out_ref, counts_ref, sems = refs[-4:]
    size = block_refs[0].shape[0] - 8
    plane, line = lax.rem(where_ref[0], 4), lax.div(where_ref[0], 4)
    each = size // LANES
    odd = lax.rem(where_ref[1], 2)
    bits = (0, 1 + odd, 2 - odd, 3)
    places = [ahead(order, line, steps) * 4 + (plane ^ bits[way]) for way, steps in names]
    copies = []
    for i in range(count):
        at = pl.multiple_of(places[i] * size, size)
        copies.append(
            pltpu.make_async_copy(block_refs[i].at[0:size, :], new_ref.at[pl.ds(at, size), :], sems.at[i])
        )
        copies[-1].start()
    if later:
        counts_ref[...] = refs[count][...]
    for i in range(count):
        for k in range(each):
            counts_ref[pl.ds(places[i] * each + k, 1), :] = block_refs[i][size + k : size + k + 1, 0:LANES]
    copies.append(pltpu.make_async_copy(counts_ref, counts_out_ref, sems.at[count]))
    copies[-1].start()
    for copy in copies:
        copy.wait()


def body(n, cores, points, centroids):
    rows, width = points.shape
    local_cent = centroids.shape[0]
    lines = n // 4
    half = rows // (2 * cores)
    share = local_cent // 4
    size = share // lines
    order = tuple(range(0, lines, 2)) + tuple(range(1, lines, 2))[::-1]
    where = jnp.stack([lax.axis_index("dp"), lax.axis_index("cent")]).astype(jnp.int32)

    def exchange(x, kind):
        pairs = [
            (i * cores + c, (i ^ (1 if (kind + c) % 2 == 0 else 2)) * cores + c)
            for i in range(n)
            for c in range(cores)
        ]
        return lax.ppermute(x, ("dp", "cent"), pairs)

    def flip_core(x, bits):
        return lax.ppermute(x, "cent", [(i, i ^ bits) for i in range(cores)])

    def ring(x, way):
        pairs = [(order[p], order[(p + way) % lines]) for p in range(lines)]
        return lax.ppermute(x, "dp", [(4 * a + i, 4 * b + i) for a, b in pairs for i in range(4)])

    def with_siblings(pieces):
        return [a if rc == 0 else flip_core(a, rc) for a in pieces for rc in range(cores)]

    mine = call(open_kernel, f32(2 * half, width), [SMEM, VMEM], (where, points), "open")
    by_a, by_b = exchange(mine, 0), exchange(mine, 1)

    pair, twice, norm = stats(where, points, centroids, lines)
    pairs = [pair] + [flip_core(pair, rc) for rc in range(1, cores)]
    tail = max(8, 2 * cores)
    lse, log_evidence, pack_a, pack_b = call(
        functools.partial(lse_kernel, cores, local_cent * cores),
        (f32(2 * cores, half), f32(rows // LANES, LANES), f32(half + tail, width), f32(half + tail, width)),
        [VMEM] * (2 + cores),
        (by_a, by_b, *pairs),
        "lse",
    )
    d0, d1 = exchange(pack_a, 1), exchange(pack_b, 0)

    by_a, by_b, lse = lax.optimization_barrier((by_a, by_b, lse))
    near = with_siblings((by_a, by_b))
    lanes = min(LANES, half)
    acc, cnt = call(
        functools.partial(own_kernel, cores),
        (f32(share, width), f32(share, lanes)),
        [VMEM] * 4,
        (points, twice, norm, lse),
        "own",
        flops=4 * share * width * rows,
    )
    lse, acc, cnt, near = lax.optimization_barrier((lse, acc, cnt, near))
    lse_d = lax.ppermute(lse, "dp", [(i, i ^ 3) for i in range(n)])
    near, d0, d1, acc, cnt, lse_d = lax.optimization_barrier((near, d0, d1, acc, cnt, lse_d))
    lead = call(
        functools.partial(lead_kernel, cores, order, half),
        (f32(size, width), f32(size, lanes)),
        [SMEM] + [VMEM] * (6 + 2 * cores),
        (where, twice, norm, acc, cnt, *near, d0, d1),
        "lead",
        flops=4 * size * width * 2 * rows,
    )
    given = (where, twice, norm, acc, cnt, lse_d)
    far = with_siblings((d0, d1))
    rows_given = (*near, *far)
    block_sum = f32(size + 8, width)
    turn = lines // 2
    forward = list(range(turn - 1, 0, -1))
    backward = [lines - s for s in range(turn - 1, 0, -1)]
    first = call(
        functools.partial(first_kernel, cores, order, half),
        block_sum,
        [SMEM] + [VMEM] * (5 + 2 * cores),
        (where, twice, norm, lse_d, *lead, *far),
        "first",
        flops=4 * size * width * 2 * rows,
    )

    def sums_of(steps):
        made = call(
            functools.partial(rest_kernel, cores, order, half, steps),
            [block_sum] * len(steps),
            [SMEM] + [VMEM] * (5 + 4 * cores),
            (*given, *rows_given),
            "rest",
            flops=4 * size * width * 3 * rows * len(steps),
        )
        return dict(zip(steps, made))

    def plus(a, b):
        return call(add_kernel, block_sum, [VMEM] * 2, (a, b), "add")

    sums = {**sums_of(backward), **sums_of(forward + [0])}
    from_ahead = ring(sums[backward[0]], -1)
    for s in backward[1:]:
        from_ahead = ring(plus(sums[s], from_ahead), -1)
    from_behind = ring(first, 1)
    for s in forward:
        from_behind = ring(plus(sums[s], from_behind), 1)
    done = call(
        finish_kernel,
        block_sum,
        [SMEM] + [VMEM] * 4,
        (where, twice, sums[0], from_behind, from_ahead),
        "finish",
    )

    steps = [-s for s in range(1, lines // 2 + 1)] + list(range(1, lines // 2))
    got = {(0, 0): done}
    previous, older, plane_b = (), (done, done), [done]
    for s in [0] + steps:
        x = got[0, s]
        if previous:
            x = lax.optimization_barrier((x, *previous))[0]
        got[1, s], got[2, s] = exchange(x, 0), exchange(x, 1)
        if s == steps[-1]:
            break
        got[3, s] = exchange(got[1, s], 1)
        plane_b.append(got[2, s])
        previous, older = (plane_b[-2 if s == steps[-2] else -1], *older[:1]), (*older[1:], got[3, s])
        ahead_of = steps[([0] + steps).index(s)]
        x = got[0, ahead_of + (1 if ahead_of < 0 else -1)]
        if ahead_of > 0:
            x = lax.optimization_barrier((x, got[0, s]))[0]
        got[0, ahead_of] = ring(x, 1 if ahead_of < 0 else -1)
    before = got[3, steps[-1] - 1] if steps[-1] > 0 else got[3, steps[-1] + 1]
    before = lax.optimization_barrier((before, got[0, steps[-1]]))[0]
    got[3, steps[-1]] = ring(before, -1 if steps[-1] > 0 else 1)
    late = [(1, steps[-1]), (2, steps[-1])]
    middle = [(w, steps[-2]) for w in (1, 2, 3)] + [(3, steps[-1])]
    groups = ([k for k in got if k not in middle + late], middle, late)
    new = counts = None
    for later, names in enumerate(groups):
        args = [where] + [got[k] for k in names]
        if later:
            args += [counts, new]
        new, counts = call(
            functools.partial(place_kernel, names, order, later),
            (f32(local_cent, width), f32(local_cent // LANES, LANES)),
            [SMEM] + [VMEM] * len(names) + ([VMEM, ANY] if later else []),
            args,
            ("place_early", "place_middle", "place_late")[later],
            out_specs=(ANY, ANY),
            scratch=[
                pltpu.VMEM((local_cent // LANES, LANES), jnp.float32),
                pltpu.SemaphoreType.DMA((len(names) + 1,)),
            ],
            aliases={len(args) - 1: 0} if later else {},
        )
    return new, counts.reshape(-1), log_evidence.reshape(-1)


def solution(mesh):
    n, cores = mesh.shape["dp"], mesh.shape["cent"]
    return jax.shard_map(
        functools.partial(body, n, cores),
        mesh=mesh,
        in_specs=(P("dp", None), P("cent", None)),
        out_specs=(P("cent", None), P("cent"), P("dp")),
        check_vma=False,
    )
```

```python
import functools
import math

import jax
import jax.numpy as jnp
from jax import lax
from jax.experimental import pallas as pl
from jax.experimental.pallas import tpu as pltpu
from jax.sharding import PartitionSpec as P

prior_mass = 0.5
VMEM_LIMIT = 24 * 1024 * 1024
LANES = 128
NT = (((1,), (1,)), ((), ()))
NN = (((1,), (0,)), ((), ()))
VMEM = pl.BlockSpec(memory_space=pltpu.VMEM)
SMEM = pl.BlockSpec(memory_space=pltpu.SMEM)
ANY = pl.BlockSpec(memory_space=pl.ANY)
HBM = pl.BlockSpec(memory_space=pltpu.HBM)


def f32(*shape):
    return jax.ShapeDtypeStruct(shape, jnp.float32)


def call(kernel, out_shape, in_specs, args, name, out_specs=None, scratch=(), flops=0, aliases={}):
    return pl.pallas_call(
        kernel,
        out_shape=out_shape,
        in_specs=in_specs,
        out_specs=jax.tree.map(lambda _: VMEM, out_shape) if out_specs is None else out_specs,
        scratch_shapes=list(scratch),
        input_output_aliases=aliases,
        compiler_params=pltpu.CompilerParams(vmem_limit_bytes=VMEM_LIMIT),
        cost_estimate=pl.CostEstimate(
            flops=flops,
            bytes_accessed=sum(a.size * a.dtype.itemsize for a in args),
            transcendentals=0,
        ),
        name=name,
    )(*args)


def open_kernel(where_ref, points_ref, out_ref):
    block = out_ref.shape[0]
    start = pl.multiple_of(where_ref[1] * block, block)
    out_ref[...] = points_ref[pl.ds(start, block), :].astype(jnp.float32)


def widen(norm, width):
    if width <= norm.shape[1]:
        return norm[:, :width]
    return jnp.concatenate([norm] * (width // norm.shape[1]), axis=1)


def norms(c):
    c = c.astype(jnp.float32)
    return jnp.broadcast_to(jnp.sum(c * c, axis=1, keepdims=True), (c.shape[0], LANES))


def stats_kernel(lines, where_ref, points_ref, c_ref, out_ref, twice_ref, norm_ref, all_norm_ref):
    rows, local = points_ref.shape[0], c_ref.shape[0]
    chunk = local // lines
    tile, size = min(256, rows), chunk // 4
    kept = pl.multiple_of(lax.rem(where_ref[0], 4) * size, size)
    for l in range(lines):
        c = c_ref[l * chunk : (l + 1) * chunk, :]
        all_norm_ref[...] = norms(c)
        twice = c + c
        for start in range(0, rows, tile):
            at = slice(start, start + tile)
            dots = lax.dot_general(twice, points_ref[at, :], NT, preferred_element_type=jnp.float32)
            score = dots - widen(all_norm_ref[...], tile)
            top = jnp.max(score, axis=0, keepdims=True)
            total = jnp.sum(jnp.exp(score - top), axis=0, keepdims=True)
            if l:
                old_top, old_total = out_ref[0:1, at], out_ref[1:2, at]
                new_top = jnp.maximum(old_top, top)
                total = old_total * jnp.exp(old_top - new_top) + total * jnp.exp(top - new_top)
                top = new_top
            out_ref[0:1, at] = top
            out_ref[1:2, at] = total
        mine = c_ref[pl.ds(pl.multiple_of(l * chunk + kept, size), size), :]
        twice_ref[l * size : (l + 1) * size, :] = mine + mine
        norm_ref[l * size : (l + 1) * size, :] = all_norm_ref[pl.ds(kept, size), :]


def stats(where, points, centroids, lines):
    rows, width = points.shape
    local = centroids.shape[0]
    return call(
        functools.partial(stats_kernel, lines),
        (
            f32(2, rows),
            jax.ShapeDtypeStruct((local // 4, width), jnp.bfloat16),
            f32(local // 4, LANES),
        ),
        [SMEM, VMEM, VMEM],
        (where, points, centroids),
        "stats",
        scratch=[pltpu.VMEM((local // lines, LANES), jnp.float32)],
        flops=4 * rows * local * width,
    )


def lse_kernel(cores, every, *refs):
    pair_refs = refs[:cores]
    lse_ref, evidence_ref = refs[cores:]
    half = lse_ref.shape[1]
    top = functools.reduce(jnp.maximum, [p[0:1, :] for p in pair_refs])
    total = functools.reduce(jnp.add, [p[1:2, :] * jnp.exp(p[0:1, :] - top) for p in pair_refs])
    lse = top + jnp.log(total)
    evidence = lse - math.log(every)
    for k in range(evidence_ref.shape[0]):
        evidence_ref[k : k + 1, :] = evidence[:, k * LANES : (k + 1) * LANES]
    for i in range(2 * cores):
        lse_ref[i : i + 1, :] = lse[:, i * half : (i + 1) * half]


def halves_kernel(a_ref, b_ref, first_ref, second_ref):
    half = first_ref.shape[0]
    first_ref[...] = a_ref[0:half, :]
    second_ref[...] = b_ref[half:, :]


def weigh(twice, norm, x, lse, lanes):
    dots = lax.dot_general(twice, x, NT, preferred_element_type=jnp.float32)
    score = dots - widen(norm, x.shape[0])
    resp = jnp.exp(score - lse).astype(jnp.bfloat16)
    part = lax.dot_general(resp, x, NN, preferred_element_type=jnp.float32)
    wide = resp.astype(jnp.float32)
    counted = functools.reduce(
        jnp.add, [wide[:, k : k + lanes] for k in range(0, x.shape[0], lanes)]
    )
    return part, counted


def two_rows(ref, at, half):
    return jnp.concatenate([ref[pl.ds(at, 1), :][:, 0:half], ref[pl.ds(at + 1, 1), :][:, 0:half]], axis=1)


def own_kernel(cores, points_ref, twice_ref, norm_ref, lse_ref, acc_ref, cnt_ref):
    half = points_ref.shape[0] // (2 * cores)
    for i in range(cores):
        x = points_ref[2 * i * half : 2 * (i + 1) * half, :]
        lse = two_rows(lse_ref, 2 * i, half)
        part, counted = weigh(twice_ref[...], norm_ref[...], x, lse, cnt_ref.shape[1])
        if i == 0:
            acc_ref[...] = part
            cnt_ref[...] = counted
        else:
            acc_ref[...] += part
            cnt_ref[...] += counted


def far_rows(cores, half, core, refs, lse_ref):
    for rc in range(cores):
        yield (
            lambda rc=rc: jnp.concatenate([refs[rc][...], refs[cores + rc][...]], axis=0)
        ), (lambda at=2 * (core ^ rc): two_rows(lse_ref, at, half))


def add_rows(rows, half, twice, norm, acc, cnt):
    for x, lse in rows:
        part, counted = weigh(twice, norm, x().astype(jnp.bfloat16), lse(), cnt.shape[1])
        acc, cnt = acc + part, cnt + counted
    return acc, cnt


def store_sums(out_ref, acc, cnt):
    size, width = acc.shape
    turned = jnp.sum(cnt.T, axis=0, keepdims=True)
    if size < width:
        turned = jnp.concatenate([turned, jnp.zeros((1, width - size), jnp.float32)], axis=1)
    out_ref[0:size, :] = acc
    out_ref[size : size + 8, :] = jnp.broadcast_to(turned, (8, width))


def near_kernel(cores, half, where_ref, twice_ref, norm_ref, acc_in_ref, cnt_in_ref, lse_a_ref, lse_b_ref, *refs):
    acc_ref, cnt_ref = refs[2 * cores :]
    acc_ref[...] = acc_in_ref[...]
    cnt_ref[...] = cnt_in_ref[...]
    for kind in range(2):
        for rc in range(cores):
            lse_ref = lse_a_ref if (kind + rc) % 2 == 0 else lse_b_ref
            lse = two_rows(lse_ref, 2 * (where_ref[1] ^ rc), half)
            x = refs[kind * cores + rc][...].astype(jnp.bfloat16)
            part, counted = weigh(twice_ref[...], norm_ref[...], x, lse, cnt_ref.shape[1])
            acc_ref[...] += part
            cnt_ref[...] += counted


def far_kernel(cores, order, half, steps, where_ref, twice_ref, norm_ref, acc_ref, cnt_ref, lse_ref, *refs):
    far, out_refs = refs[: 2 * cores], refs[2 * cores :]
    line = lax.div(where_ref[0], 4)
    for s, out_ref in zip(steps, out_refs):
        size = out_ref.shape[0] - 8
        at = pl.ds(pl.multiple_of(ahead(order, line, s) * size, size), size)
        acc, cnt = add_rows(
            far_rows(cores, half, where_ref[1], far, lse_ref),
            half,
            twice_ref[at, :],
            norm_ref[at, :],
            acc_ref[at, :],
            cnt_ref[at, :],
        )
        store_sums(out_ref, acc, cnt)


def ahead(order, line, steps):
    n = len(order)
    return functools.reduce(
        jnp.add,
        [jnp.where(line == order[p], order[(p + steps) % n], 0) for p in range(n)],
    )


def add_kernel(a_ref, b_ref, out_ref):
    out_ref[...] = a_ref[...] + b_ref[...]


def finish_kernel(where_ref, twice_ref, mine_ref, first_ref, second_ref, out_ref):
    size, width = out_ref.shape[0] - 8, out_ref.shape[1]
    start = pl.multiple_of(lax.div(where_ref[0], 4) * size, size)
    c = 0.5 * twice_ref[pl.ds(start, size), :].astype(jnp.float32)
    total = mine_ref[...] + first_ref[...] + second_ref[...]
    counts = total[size:, :]
    column = counts.T[:size, 0:1]
    out_ref[0:size, :] = (total[:size, :] + prior_mass * c) / (column + prior_mass)
    row = lax.broadcasted_iota(jnp.int32, (8, LANES), 0)
    spread = jnp.zeros((8, LANES), jnp.float32)
    for k in range(size // LANES):
        spread = jnp.where(row == k, counts[:, k * LANES : (k + 1) * LANES], spread)
    out_ref[size:, :] = jnp.concatenate([spread] * (width // LANES), axis=1)


def place_kernel(names, order, later, where_ref, *refs):
    count, lines = len(names), len(order)
    block_refs = refs[:count]
    new_ref, counts_out_ref, counts_ref, sems = refs[-4:]
    size = block_refs[0].shape[0] - 8
    plane, line = lax.rem(where_ref[0], 4), lax.div(where_ref[0], 4)
    each = size // LANES
    odd = lax.rem(where_ref[1], 2)
    bits = (0, 1 + odd, 2 - odd, 3)
    places = [ahead(order, line, steps) * 4 + (plane ^ bits[way]) for way, steps in names]
    copies = []
    for i in range(count):
        at = pl.multiple_of(places[i] * size, size)
        copies.append(
            pltpu.make_async_copy(block_refs[i].at[0:size, :], new_ref.at[pl.ds(at, size), :], sems.at[i])
        )
        copies[-1].start()
    if later:
        counts_ref[...] = refs[count][...]
    for i in range(count):
        for k in range(each):
            counts_ref[pl.ds(places[i] * each + k, 1), :] = block_refs[i][size + k : size + k + 1, 0:LANES]
    copies.append(pltpu.make_async_copy(counts_ref, counts_out_ref, sems.at[count]))
    copies[-1].start()
    for copy in copies:
        copy.wait()


def body(n, cores, points, centroids):
    rows, width = points.shape
    local_cent = centroids.shape[0]
    lines = n // 4
    half = rows // (2 * cores)
    share = local_cent // 4
    size = share // lines
    order = tuple(range(0, lines, 2)) + tuple(range(1, lines, 2))[::-1]
    where = jnp.stack([lax.axis_index("dp"), lax.axis_index("cent")]).astype(jnp.int32)

    def exchange(x, kind):
        pairs = [
            (i * cores + c, (i ^ (1 if (kind + c) % 2 == 0 else 2)) * cores + c)
            for i in range(n)
            for c in range(cores)
        ]
        return lax.ppermute(x, ("dp", "cent"), pairs)

    def flip_core(x, bits):
        return lax.ppermute(x, "cent", [(i, i ^ bits) for i in range(cores)])

    def ring(x, way):
        pairs = [(order[p], order[(p + way) % lines]) for p in range(lines)]
        return lax.ppermute(x, "dp", [(4 * a + i, 4 * b + i) for a, b in pairs for i in range(4)])

    def with_siblings(pieces):
        return [a if rc == 0 else flip_core(a, rc) for a in pieces for rc in range(cores)]

    mine = call(open_kernel, f32(2 * half, width), [SMEM, VMEM], (where, points), "open")
    by_a, by_b = exchange(mine, 0), exchange(mine, 1)

    pair, twice, norm = stats(where, points, centroids, lines)
    pairs = [pair] + [flip_core(pair, rc) for rc in range(1, cores)]
    lse, log_evidence = call(
        functools.partial(lse_kernel, cores, local_cent * cores),
        (f32(2 * cores, half), f32(rows // LANES, LANES)),
        [VMEM] * cores,
        pairs,
        "lse",
    )
    lse_a, lse_b = exchange(lse, 0), exchange(lse, 1)
    first_a, second_b = call(
        halves_kernel, (f32(half, width), f32(half, width)), [VMEM] * 2, (by_a, by_b), "halves"
    )
    d0, d1 = exchange(first_a, 1), exchange(second_b, 0)

    lanes = min(LANES, half)
    acc_shape, cnt_shape = f32(share, width), f32(share, lanes)
    acc, cnt = call(
        functools.partial(own_kernel, cores),
        (acc_shape, cnt_shape),
        [VMEM] * 4,
        (points, twice, norm, lse),
        "own",
        flops=4 * share * width * rows,
    )
    lse_d = lax.ppermute(lse, "dp", [(i, i ^ 3) for i in range(n)])
    by_a, by_b, lse_a, lse_b, lse_d = lax.optimization_barrier((by_a, by_b, lse_a, lse_b, lse_d))
    near = with_siblings((by_a, by_b))
    acc, cnt = call(
        functools.partial(near_kernel, cores, half),
        (acc_shape, cnt_shape),
        [SMEM] + [VMEM] * (6 + 2 * cores),
        (where, twice, norm, acc, cnt, lse_a, lse_b, *near),
        "near",
        flops=4 * share * width * 2 * rows,
        aliases={3: 0, 4: 1},
    )
    d0, d1, acc, cnt = lax.optimization_barrier((d0, d1, acc, cnt))
    far = with_siblings((d0, d1))
    block_sum = f32(size + 8, width)
    turn = lines // 2
    forward = list(range(turn - 1, 0, -1))
    backward = [lines - s for s in range(turn - 1, 0, -1)]

    def sums_of(steps, name):
        made = call(
            functools.partial(far_kernel, cores, order, half, steps),
            [block_sum] * len(steps),
            [SMEM] + [VMEM] * (5 + 2 * cores),
            (where, twice, norm, acc, cnt, lse_d, *far),
            name,
            flops=4 * size * width * rows * len(steps),
        )
        return dict(zip(steps, made))

    def plus(a, b):
        return call(add_kernel, block_sum, [VMEM] * 2, (a, b), "add")

    first = sums_of([turn], "first")[turn]
    sums = {**sums_of(backward, "second"), **sums_of(forward + [0], "rest")}
    from_ahead = ring(sums[backward[0]], -1)
    for s in backward[1:]:
        from_ahead = ring(plus(sums[s], from_ahead), -1)
    from_behind = ring(first, 1)
    for s in forward:
        from_behind = ring(plus(sums[s], from_behind), 1)
    done = call(
        finish_kernel,
        block_sum,
        [SMEM] + [VMEM] * 4,
        (where, twice, sums[0], from_behind, from_ahead),
        "finish",
    )

    steps = [-s for s in range(1, lines // 2 + 1)] + list(range(1, lines // 2))
    got = {(0, 0): done}
    previous, older, plane_b = (), (done, done), [done]
    for s in [0] + steps:
        x = got[0, s]
        if previous:
            x = lax.optimization_barrier((x, *previous))[0]
        got[1, s], got[2, s] = exchange(x, 0), exchange(x, 1)
        if s == steps[-1]:
            break
        got[3, s] = exchange(got[1, s], 1)
        plane_b.append(got[2, s])
        previous, older = (plane_b[-2 if s == steps[-2] else -1], *older[:1]), (*older[1:], got[3, s])
        ahead_of = steps[([0] + steps).index(s)]
        x = got[0, ahead_of + (1 if ahead_of < 0 else -1)]
        if ahead_of > 0:
            x = lax.optimization_barrier((x, got[0, s]))[0]
        got[0, ahead_of] = ring(x, 1 if ahead_of < 0 else -1)
    before = got[3, steps[-1] - 1] if steps[-1] > 0 else got[3, steps[-1] + 1]
    before = lax.optimization_barrier((before, got[0, steps[-1]]))[0]
    got[3, steps[-1]] = ring(before, -1 if steps[-1] > 0 else 1)
    late = [(1, steps[-1]), (2, steps[-1])]
    middle = [(w, steps[-2]) for w in (1, 2, 3)] + [(3, steps[-1])]
    groups = ([k for k in got if k not in middle + late], middle, late)
    new = counts = None
    for later, names in enumerate(groups):
        args = [where] + [got[k] for k in names]
        if later:
            args += [counts, new]
        new, counts = call(
            functools.partial(place_kernel, names, order, later),
            (f32(local_cent, width), f32(local_cent // LANES, LANES)),
            [SMEM] + [VMEM] * len(names) + ([VMEM, ANY] if later else []),
            args,
            ("place_early", "place_middle", "place_late")[later],
            out_specs=(ANY, ANY),
            scratch=[
                pltpu.VMEM((local_cent // LANES, LANES), jnp.float32),
                pltpu.SemaphoreType.DMA((len(names) + 1,)),
            ],
            aliases={len(args) - 1: 0} if later else {},
        )
    return new, counts.reshape(-1), log_evidence.reshape(-1)


def solution(mesh):
    n, cores = mesh.shape["dp"], mesh.shape["cent"]
    return jax.shard_map(
        functools.partial(body, n, cores),
        mesh=mesh,
        in_specs=(P("dp", None), P("cent", None)),
        out_specs=(P("cent", None), P("cent"), P("dp")),
        check_vma=False,
    )
```

```python
import functools
import math

import jax
import jax.numpy as jnp
from jax import lax
from jax.experimental import pallas as pl
from jax.experimental.pallas import tpu as pltpu
from jax.sharding import PartitionSpec as P

prior_mass = 0.5
VMEM_LIMIT = 24 * 1024 * 1024
LANES = 128
NT = (((1,), (1,)), ((), ()))
NN = (((1,), (0,)), ((), ()))
VMEM = pl.BlockSpec(memory_space=pltpu.VMEM)
SMEM = pl.BlockSpec(memory_space=pltpu.SMEM)
ANY = pl.BlockSpec(memory_space=pl.ANY)
HBM = pl.BlockSpec(memory_space=pltpu.HBM)


def f32(*shape):
    return jax.ShapeDtypeStruct(shape, jnp.float32)


def call(kernel, out_shape, in_specs, args, name, out_specs=None, scratch=(), flops=0, aliases={}):
    return pl.pallas_call(
        kernel,
        out_shape=out_shape,
        in_specs=in_specs,
        out_specs=jax.tree.map(lambda _: VMEM, out_shape) if out_specs is None else out_specs,
        scratch_shapes=list(scratch),
        input_output_aliases=aliases,
        compiler_params=pltpu.CompilerParams(vmem_limit_bytes=VMEM_LIMIT),
        cost_estimate=pl.CostEstimate(
            flops=flops,
            bytes_accessed=sum(a.size * a.dtype.itemsize for a in args),
            transcendentals=0,
        ),
        name=name,
    )(*args)


def open_kernel(where_ref, points_ref, out_ref):
    block = out_ref.shape[0]
    start = pl.multiple_of(where_ref[1] * block, block)
    out_ref[...] = points_ref[pl.ds(start, block), :].astype(jnp.float32)


def widen(norm, width):
    if width <= norm.shape[1]:
        return norm[:, :width]
    return jnp.concatenate([norm] * (width // norm.shape[1]), axis=1)


def norms(c):
    c = c.astype(jnp.float32)
    return jnp.broadcast_to(jnp.sum(c * c, axis=1, keepdims=True), (c.shape[0], LANES))


def stats_kernel(lines, where_ref, points_ref, c_ref, out_ref, twice_ref, norm_ref, all_norm_ref):
    rows, local = points_ref.shape[0], c_ref.shape[0]
    chunk = local // lines
    tile, size = min(256, rows), chunk // 4
    kept = pl.multiple_of(lax.rem(where_ref[0], 4) * size, size)
    for l in range(lines):
        c = c_ref[l * chunk : (l + 1) * chunk, :]
        all_norm_ref[...] = norms(c)
        twice = c + c
        for start in range(0, rows, tile):
            at = slice(start, start + tile)
            dots = lax.dot_general(twice, points_ref[at, :], NT, preferred_element_type=jnp.float32)
            score = dots - widen(all_norm_ref[...], tile)
            top = jnp.max(score, axis=0, keepdims=True)
            total = jnp.sum(jnp.exp(score - top), axis=0, keepdims=True)
            if l:
                old_top, old_total = out_ref[0:1, at], out_ref[1:2, at]
                new_top = jnp.maximum(old_top, top)
                total = old_total * jnp.exp(old_top - new_top) + total * jnp.exp(top - new_top)
                top = new_top
            out_ref[0:1, at] = top
            out_ref[1:2, at] = total
        mine = c_ref[pl.ds(pl.multiple_of(l * chunk + kept, size), size), :]
        twice_ref[l * size : (l + 1) * size, :] = mine + mine
        norm_ref[l * size : (l + 1) * size, :] = all_norm_ref[pl.ds(kept, size), :]


def stats(where, points, centroids, lines):
    rows, width = points.shape
    local = centroids.shape[0]
    return call(
        functools.partial(stats_kernel, lines),
        (
            f32(2, rows),
            jax.ShapeDtypeStruct((local // 4, width), jnp.bfloat16),
            f32(local // 4, LANES),
        ),
        [SMEM, VMEM, VMEM],
        (where, points, centroids),
        "stats",
        scratch=[pltpu.VMEM((local // lines, LANES), jnp.float32)],
        flops=4 * rows * local * width,
    )


def lse_kernel(cores, every, a_ref, b_ref, *refs):
    pair_refs = refs[:cores]
    lse_ref, evidence_ref, pack_a_ref, pack_b_ref = refs[cores:]
    half = lse_ref.shape[1]
    top = functools.reduce(jnp.maximum, [p[0:1, :] for p in pair_refs])
    total = functools.reduce(jnp.add, [p[1:2, :] * jnp.exp(p[0:1, :] - top) for p in pair_refs])
    lse = top + jnp.log(total)
    evidence = lse - math.log(every)
    for k in range(evidence_ref.shape[0]):
        evidence_ref[k : k + 1, :] = evidence[:, k * LANES : (k + 1) * LANES]
    for i in range(2 * cores):
        lse_ref[i : i + 1, :] = lse[:, i * half : (i + 1) * half]
    for piece, pack_ref in ((a_ref[0:half, :], pack_a_ref), (b_ref[half:, :], pack_b_ref)):
        pack_ref[0:half, :] = piece
        pack_ref[half:, :] = jnp.zeros_like(pack_ref[half:, :])
        pack_ref[half : half + 2 * cores, 0:half] = lse_ref[...]


def weigh(twice, norm, x, lse, lanes):
    dots = lax.dot_general(twice, x, NT, preferred_element_type=jnp.float32)
    score = dots - widen(norm, x.shape[0])
    resp = jnp.exp(score - lse).astype(jnp.bfloat16)
    part = lax.dot_general(resp, x, NN, preferred_element_type=jnp.float32)
    wide = resp.astype(jnp.float32)
    counted = functools.reduce(
        jnp.add, [wide[:, k : k + lanes] for k in range(0, x.shape[0], lanes)]
    )
    return part, counted


def two_rows(ref, at, half):
    return jnp.concatenate([ref[pl.ds(at, 1), :][:, 0:half], ref[pl.ds(at + 1, 1), :][:, 0:half]], axis=1)


def own_kernel(cores, points_ref, twice_ref, norm_ref, lse_ref, acc_ref, cnt_ref):
    half = points_ref.shape[0] // (2 * cores)
    for i in range(cores):
        x = points_ref[2 * i * half : 2 * (i + 1) * half, :]
        lse = two_rows(lse_ref, 2 * i, half)
        part, counted = weigh(twice_ref[...], norm_ref[...], x, lse, cnt_ref.shape[1])
        if i == 0:
            acc_ref[...] = part
            cnt_ref[...] = counted
        else:
            acc_ref[...] += part
            cnt_ref[...] += counted


def near_rows(cores, half, core, refs, d0_ref, d1_ref):
    for kind in range(2):
        for rc in range(cores):
            tail_ref = d1_ref if (kind + rc) % 2 == 0 else d0_ref
            at = half + 2 * (core ^ rc)
            yield (lambda ref=refs[kind * cores + rc]: ref[...]), (
                lambda at=at, tail_ref=tail_ref: two_rows(tail_ref, at, half)
            )


def far_rows(cores, half, core, refs, lse_ref):
    for rc in range(cores):
        yield (
            lambda rc=rc: jnp.concatenate([refs[rc][0:half, :], refs[cores + rc][0:half, :]], axis=0)
        ), (lambda at=2 * (core ^ rc): two_rows(lse_ref, at, half))


def add_rows(rows, half, twice, norm, acc, cnt):
    for x, lse in rows:
        part, counted = weigh(twice, norm, x().astype(jnp.bfloat16), lse(), cnt.shape[1])
        acc, cnt = acc + part, cnt + counted
    return acc, cnt


def store_sums(out_ref, acc, cnt):
    size, width = acc.shape
    turned = jnp.sum(cnt.T, axis=0, keepdims=True)
    if size < width:
        turned = jnp.concatenate([turned, jnp.zeros((1, width - size), jnp.float32)], axis=1)
    out_ref[0:size, :] = acc
    out_ref[size : size + 8, :] = jnp.broadcast_to(turned, (8, width))


def lead_kernel(cores, order, half, where_ref, twice_ref, norm_ref, acc_ref, cnt_ref, *refs):
    out_acc_ref, out_cnt_ref = refs[-2:]
    near, (d0_ref, d1_ref) = refs[: 2 * cores], refs[2 * cores : 2 * cores + 2]
    size = out_acc_ref.shape[0]
    place = ahead(order, lax.div(where_ref[0], 4), len(order) // 2)
    at = pl.ds(pl.multiple_of(place * size, size), size)
    out_acc_ref[...], out_cnt_ref[...] = add_rows(
        near_rows(cores, half, where_ref[1], near, d0_ref, d1_ref),
        half,
        twice_ref[at, :],
        norm_ref[at, :],
        acc_ref[at, :],
        cnt_ref[at, :],
    )


def block_sums(cores, order, half, steps, where_ref, twice_ref, norm_ref, acc_ref, cnt_ref, lse_ref, near, far, out_ref):
    size = out_ref.shape[0] - 8
    place = ahead(order, lax.div(where_ref[0], 4), steps)
    at = pl.ds(pl.multiple_of(place * size, size), size)
    twice, norm = twice_ref[at, :], norm_ref[at, :]
    acc, cnt = add_rows(
        near_rows(cores, half, where_ref[1], near, far[0], far[cores]),
        half,
        twice,
        norm,
        acc_ref[at, :],
        cnt_ref[at, :],
    )
    acc, cnt = add_rows(far_rows(cores, half, where_ref[1], far, lse_ref), half, twice, norm, acc, cnt)
    store_sums(out_ref, acc, cnt)


def first_kernel(cores, order, half, where_ref, twice_ref, norm_ref, lse_ref, lead_acc_ref, lead_cnt_ref, *refs):
    far, out_ref = refs[: 2 * cores], refs[2 * cores]
    size = lead_acc_ref.shape[0]
    place = ahead(order, lax.div(where_ref[0], 4), len(order) // 2)
    at = pl.ds(pl.multiple_of(place * size, size), size)
    acc, cnt = add_rows(
        far_rows(cores, half, where_ref[1], far, lse_ref),
        half,
        twice_ref[at, :],
        norm_ref[at, :],
        lead_acc_ref[...],
        lead_cnt_ref[...],
    )
    store_sums(out_ref, acc, cnt)


def rest_kernel(cores, order, half, steps, where_ref, twice_ref, norm_ref, acc_ref, cnt_ref, lse_ref, *refs):
    near, far = refs[: 2 * cores], refs[2 * cores : 4 * cores]
    for s, out_ref in zip(steps, refs[4 * cores :]):
        block_sums(
            cores, order, half, s, where_ref, twice_ref, norm_ref, acc_ref, cnt_ref, lse_ref, near, far, out_ref
        )


def ahead(order, line, steps):
    n = len(order)
    return functools.reduce(
        jnp.add,
        [jnp.where(line == order[p], order[(p + steps) % n], 0) for p in range(n)],
    )


def add_kernel(a_ref, b_ref, out_ref):
    out_ref[...] = a_ref[...] + b_ref[...]


def finish_kernel(where_ref, twice_ref, mine_ref, first_ref, second_ref, out_ref):
    size, width = out_ref.shape[0] - 8, out_ref.shape[1]
    start = pl.multiple_of(lax.div(where_ref[0], 4) * size, size)
    c = 0.5 * twice_ref[pl.ds(start, size), :].astype(jnp.float32)
    total = mine_ref[...] + first_ref[...] + second_ref[...]
    counts = total[size:, :]
    column = counts.T[:size, 0:1]
    out_ref[0:size, :] = (total[:size, :] + prior_mass * c) / (column + prior_mass)
    row = lax.broadcasted_iota(jnp.int32, (8, LANES), 0)
    spread = jnp.zeros((8, LANES), jnp.float32)
    for k in range(size // LANES):
        spread = jnp.where(row == k, counts[:, k * LANES : (k + 1) * LANES], spread)
    out_ref[size:, :] = jnp.concatenate([spread] * (width // LANES), axis=1)


def sort_kernel(where_ref, first_ref, second_ref, along_ref, over_ref):
    odd = lax.rem(where_ref[1], 2) == 1

    @pl.when(odd)
    def _():
        along_ref[...] = second_ref[...]
        over_ref[...] = first_ref[...]

    @pl.when(jnp.logical_not(odd))
    def _():
        along_ref[...] = first_ref[...]
        over_ref[...] = second_ref[...]


def place_kernel(names, order, later, where_ref, *refs):
    count, lines = len(names), len(order)
    block_refs = refs[:count]
    new_ref, counts_out_ref, counts_ref, sems = refs[-4:]
    size = block_refs[0].shape[0] - 8
    plane, line = lax.rem(where_ref[0], 4), lax.div(where_ref[0], 4)
    each = size // LANES
    odd = lax.rem(where_ref[1], 2)
    bits = (0, 1 + odd, 2 - odd, 3)
    places = [ahead(order, line, steps) * 4 + (plane ^ bits[way]) for way, steps in names]
    copies = []
    for i in range(count):
        at = pl.multiple_of(places[i] * size, size)
        copies.append(
            pltpu.make_async_copy(block_refs[i].at[0:size, :], new_ref.at[pl.ds(at, size), :], sems.at[i])
        )
        copies[-1].start()
    if later:
        counts_ref[...] = refs[count][...]
    for i in range(count):
        for k in range(each):
            counts_ref[pl.ds(places[i] * each + k, 1), :] = block_refs[i][size + k : size + k + 1, 0:LANES]
    copies.append(pltpu.make_async_copy(counts_ref, counts_out_ref, sems.at[count]))
    copies[-1].start()
    for copy in copies:
        copy.wait()


def body(n, cores, points, centroids):
    rows, width = points.shape
    local_cent = centroids.shape[0]
    lines = n // 4
    half = rows // (2 * cores)
    share = local_cent // 4
    size = share // lines
    order = tuple(range(0, lines, 2)) + tuple(range(1, lines, 2))[::-1]
    where = jnp.stack([lax.axis_index("dp"), lax.axis_index("cent")]).astype(jnp.int32)

    def exchange(x, kind):
        pairs = [
            (i * cores + c, (i ^ (1 if (kind + c) % 2 == 0 else 2)) * cores + c)
            for i in range(n)
            for c in range(cores)
        ]
        return lax.ppermute(x, ("dp", "cent"), pairs)

    def flip_core(x, bits):
        return lax.ppermute(x, "cent", [(i, i ^ bits) for i in range(cores)])

    def ring(x, way):
        pairs = [(order[p], order[(p + way) % lines]) for p in range(lines)]
        return lax.ppermute(x, "dp", [(4 * a + i, 4 * b + i) for a, b in pairs for i in range(4)])

    def with_siblings(pieces):
        return [a if rc == 0 else flip_core(a, rc) for a in pieces for rc in range(cores)]

    mine = call(open_kernel, f32(2 * half, width), [SMEM, VMEM], (where, points), "open")
    by_a, by_b = exchange(mine, 0), exchange(mine, 1)

    pair, twice, norm = stats(where, points, centroids, lines)
    pairs = [pair] + [flip_core(pair, rc) for rc in range(1, cores)]
    tail = max(8, 2 * cores)
    lse, log_evidence, pack_a, pack_b = call(
        functools.partial(lse_kernel, cores, local_cent * cores),
        (f32(2 * cores, half), f32(rows // LANES, LANES), f32(half + tail, width), f32(half + tail, width)),
        [VMEM] * (2 + cores),
        (by_a, by_b, *pairs),
        "lse",
    )
    d0, d1 = exchange(pack_a, 1), exchange(pack_b, 0)

    by_a, by_b, lse = lax.optimization_barrier((by_a, by_b, lse))
    near = with_siblings((by_a, by_b))
    lanes = min(LANES, half)
    acc, cnt = call(
        functools.partial(own_kernel, cores),
        (f32(share, width), f32(share, lanes)),
        [VMEM] * 4,
        (points, twice, norm, lse),
        "own",
        flops=4 * share * width * rows,
    )
    lse, acc, cnt, near = lax.optimization_barrier((lse, acc, cnt, near))
    lse_d = lax.ppermute(lse, "dp", [(i, i ^ 3) for i in range(n)])
    near, d0, d1, acc, cnt, lse_d = lax.optimization_barrier((near, d0, d1, acc, cnt, lse_d))
    lead = call(
        functools.partial(lead_kernel, cores, order, half),
        (f32(size, width), f32(size, lanes)),
        [SMEM] + [VMEM] * (6 + 2 * cores),
        (where, twice, norm, acc, cnt, *near, d0, d1),
        "lead",
        flops=4 * size * width * 2 * rows,
    )
    given = (where, twice, norm, acc, cnt, lse_d)
    far = with_siblings((d0, d1))
    rows_given = (*near, *far)
    block_sum = f32(size + 8, width)
    turn = lines // 2
    forward = list(range(turn - 1, 0, -1))
    backward = [lines - s for s in range(turn - 1, 0, -1)]
    first = call(
        functools.partial(first_kernel, cores, order, half),
        block_sum,
        [SMEM] + [VMEM] * (5 + 2 * cores),
        (where, twice, norm, lse_d, *lead, *far),
        "first",
        flops=4 * size * width * 2 * rows,
    )

    def sums_of(steps):
        made = call(
            functools.partial(rest_kernel, cores, order, half, steps),
            [block_sum] * len(steps),
            [SMEM] + [VMEM] * (5 + 4 * cores),
            (*given, *rows_given),
            "rest",
            flops=4 * size * width * 3 * rows * len(steps),
        )
        return dict(zip(steps, made))

    def plus(a, b):
        return call(add_kernel, block_sum, [VMEM] * 2, (a, b), "add")

    sums = {**sums_of(backward), **sums_of(forward + [0])}
    from_ahead = ring(sums[backward[0]], -1)
    for s in backward[1:]:
        from_ahead = ring(plus(sums[s], from_ahead), -1)
    from_behind = ring(first, 1)
    for s in forward:
        from_behind = ring(plus(sums[s], from_behind), 1)
    done = call(
        finish_kernel,
        block_sum,
        [SMEM] + [VMEM] * 4,
        (where, twice, sums[0], from_behind, from_ahead),
        "finish",
    )

    def either(x, even_first):
        following = {order[p]: order[(p + 1) % lines] for p in range(lines)}
        pairs = []
        for i in range(n):
            for c in range(cores):
                if (c % 2 == 0) == even_first:
                    to = 4 * following[i // 4] + i % 4
                else:
                    to = i ^ (1 if c % 2 == 0 else 2)
                pairs.append((i * cores + c, to * cores + c))
        return lax.ppermute(x, ("dp", "cent"), pairs)

    got = {(0, 0): done}
    waits = {}
    for k in range(lines - 1):
        x = got[0, -k]
        if k:
            x = lax.optimization_barrier((x, *(got[w] for w in waits[k])))[0]
        first, second = either(x, True), either(x, False)
        got[2, -k] = exchange(x, 1)
        got[0, -k - 1], got[1, -k] = call(
            sort_kernel, (block_sum, block_sum), [SMEM] + [VMEM] * 2, (where, first, second), "sort"
        )
        got[3, -k] = exchange(got[1, -k], 1)
        waits[k + 1] = [(2, -k)] + ([(3, 1 - k)] if k else [])
    end = 1 - lines
    x = lax.optimization_barrier((got[0, end], *(got[w] for w in waits.get(lines - 1, []))))[0]
    got[1, end], got[2, end] = exchange(x, 0), exchange(x, 1)
    got[3, end] = ring(lax.optimization_barrier((got[3, 0], got[0, end]))[0], -1)
    late = [(1, end), (2, end)]
    middle = [(1, end + 1), (2, end + 1), (3, end + 1), (3, end)]
    groups = ([k for k in got if k not in middle + late], middle, late)
    new = counts = None
    for later, names in enumerate(groups):
        args = [where] + [got[k] for k in names]
        if later:
            args += [counts, new]
        new, counts = call(
            functools.partial(place_kernel, names, order, later),
            (f32(local_cent, width), f32(local_cent // LANES, LANES)),
            [SMEM] + [VMEM] * len(names) + ([VMEM, ANY] if later else []),
            args,
            ("place_early", "place_middle", "place_late")[later],
            out_specs=(ANY, ANY),
            scratch=[
                pltpu.VMEM((local_cent // LANES, LANES), jnp.float32),
                pltpu.SemaphoreType.DMA((len(names) + 1,)),
            ],
            aliases={len(args) - 1: 0} if later else {},
        )
    return new, counts.reshape(-1), log_evidence.reshape(-1)


def solution(mesh):
    n, cores = mesh.shape["dp"], mesh.shape["cent"]
    return jax.shard_map(
        functools.partial(body, n, cores),
        mesh=mesh,
        in_specs=(P("dp", None), P("cent", None)),
        out_specs=(P("cent", None), P("cent"), P("dp")),
        check_vma=False,
    )
```

```python
import functools
import math

import jax
import jax.numpy as jnp
from jax import lax
from jax.experimental import pallas as pl
from jax.experimental.pallas import tpu as pltpu
from jax.sharding import PartitionSpec as P

prior_mass = 0.5
VMEM_LIMIT = 24 * 1024 * 1024
LANES = 128
NT = (((1,), (1,)), ((), ()))
NN = (((1,), (0,)), ((), ()))
VMEM = pl.BlockSpec(memory_space=pltpu.VMEM)
SMEM = pl.BlockSpec(memory_space=pltpu.SMEM)
ANY = pl.BlockSpec(memory_space=pl.ANY)
HBM = pl.BlockSpec(memory_space=pltpu.HBM)


def f32(*shape):
    return jax.ShapeDtypeStruct(shape, jnp.float32)


def call(kernel, out_shape, in_specs, args, name, out_specs=None, scratch=(), flops=0, aliases={}):
    return pl.pallas_call(
        kernel,
        out_shape=out_shape,
        in_specs=in_specs,
        out_specs=jax.tree.map(lambda _: VMEM, out_shape) if out_specs is None else out_specs,
        scratch_shapes=list(scratch),
        input_output_aliases=aliases,
        compiler_params=pltpu.CompilerParams(vmem_limit_bytes=VMEM_LIMIT),
        cost_estimate=pl.CostEstimate(
            flops=flops,
            bytes_accessed=sum(a.size * a.dtype.itemsize for a in args),
            transcendentals=0,
        ),
        name=name,
    )(*args)


def open_kernel(where_ref, points_ref, out_ref):
    block = out_ref.shape[0]
    start = pl.multiple_of(where_ref[1] * block, block)
    out_ref[...] = points_ref[pl.ds(start, block), :].astype(jnp.float32)


def widen(norm, width):
    if width <= norm.shape[1]:
        return norm[:, :width]
    return jnp.concatenate([norm] * (width // norm.shape[1]), axis=1)


def norms(c):
    c = c.astype(jnp.float32)
    return jnp.broadcast_to(jnp.sum(c * c, axis=1, keepdims=True), (c.shape[0], LANES))


def stats_kernel(lines, where_ref, points_ref, c_ref, out_ref, twice_ref, norm_ref, all_norm_ref):
    rows, local = points_ref.shape[0], c_ref.shape[0]
    chunk = local // lines
    tile, size = min(256, rows), chunk // 4
    kept = pl.multiple_of(lax.rem(where_ref[0], 4) * size, size)
    for l in range(lines):
        c = c_ref[l * chunk : (l + 1) * chunk, :]
        all_norm_ref[...] = norms(c)
        twice = c + c
        for start in range(0, rows, tile):
            at = slice(start, start + tile)
            dots = lax.dot_general(twice, points_ref[at, :], NT, preferred_element_type=jnp.float32)
            score = dots - widen(all_norm_ref[...], tile)
            top = jnp.max(score, axis=0, keepdims=True)
            total = jnp.sum(jnp.exp(score - top), axis=0, keepdims=True)
            if l:
                old_top, old_total = out_ref[0:1, at], out_ref[1:2, at]
                new_top = jnp.maximum(old_top, top)
                total = old_total * jnp.exp(old_top - new_top) + total * jnp.exp(top - new_top)
                top = new_top
            out_ref[0:1, at] = top
            out_ref[1:2, at] = total
        mine = c_ref[pl.ds(pl.multiple_of(l * chunk + kept, size), size), :]
        twice_ref[l * size : (l + 1) * size, :] = mine + mine
        norm_ref[l * size : (l + 1) * size, :] = all_norm_ref[pl.ds(kept, size), :]


def stats(where, points, centroids, lines):
    rows, width = points.shape
    local = centroids.shape[0]
    return call(
        functools.partial(stats_kernel, lines),
        (
            f32(2, rows),
            jax.ShapeDtypeStruct((local // 4, width), jnp.bfloat16),
            f32(local // 4, LANES),
        ),
        [SMEM, VMEM, VMEM],
        (where, points, centroids),
        "stats",
        scratch=[pltpu.VMEM((local // lines, LANES), jnp.float32)],
        flops=4 * rows * local * width,
    )


def lse_kernel(cores, every, a_ref, b_ref, *refs):
    pair_refs = refs[:cores]
    lse_ref, evidence_ref, pack_a_ref, pack_b_ref = refs[cores:]
    half = lse_ref.shape[1]
    top = functools.reduce(jnp.maximum, [p[0:1, :] for p in pair_refs])
    total = functools.reduce(jnp.add, [p[1:2, :] * jnp.exp(p[0:1, :] - top) for p in pair_refs])
    lse = top + jnp.log(total)
    evidence = lse - math.log(every)
    for k in range(evidence_ref.shape[0]):
        evidence_ref[k : k + 1, :] = evidence[:, k * LANES : (k + 1) * LANES]
    for i in range(2 * cores):
        lse_ref[i : i + 1, :] = lse[:, i * half : (i + 1) * half]
    for piece, pack_ref in ((a_ref[0:half, :], pack_a_ref), (b_ref[half:, :], pack_b_ref)):
        pack_ref[0:half, :] = piece
        pack_ref[half:, :] = jnp.zeros_like(pack_ref[half:, :])
        pack_ref[half : half + 2 * cores, 0:half] = lse_ref[...]


def weigh(twice, norm, x, lse, lanes):
    dots = lax.dot_general(twice, x, NT, preferred_element_type=jnp.float32)
    score = dots - widen(norm, x.shape[0])
    resp = jnp.exp(score - lse).astype(jnp.bfloat16)
    part = lax.dot_general(resp, x, NN, preferred_element_type=jnp.float32)
    wide = resp.astype(jnp.float32)
    counted = functools.reduce(
        jnp.add, [wide[:, k : k + lanes] for k in range(0, x.shape[0], lanes)]
    )
    return part, counted


def two_rows(ref, at, half):
    return jnp.concatenate([ref[pl.ds(at, 1), :][:, 0:half], ref[pl.ds(at + 1, 1), :][:, 0:half]], axis=1)


def own_kernel(cores, points_ref, twice_ref, norm_ref, lse_ref, acc_ref, cnt_ref):
    half = points_ref.shape[0] // (2 * cores)
    for i in range(cores):
        x = points_ref[2 * i * half : 2 * (i + 1) * half, :]
        lse = two_rows(lse_ref, 2 * i, half)
        part, counted = weigh(twice_ref[...], norm_ref[...], x, lse, cnt_ref.shape[1])
        if i == 0:
            acc_ref[...] = part
            cnt_ref[...] = counted
        else:
            acc_ref[...] += part
            cnt_ref[...] += counted


def near_rows(cores, half, core, refs, d0_ref, d1_ref):
    for kind in range(2):
        for rc in range(cores):
            tail_ref = d1_ref if (kind + rc) % 2 == 0 else d0_ref
            at = half + 2 * (core ^ rc)
            yield (lambda ref=refs[kind * cores + rc]: ref[...]), (
                lambda at=at, tail_ref=tail_ref: two_rows(tail_ref, at, half)
            )


def far_rows(cores, half, core, refs, lse_ref):
    for rc in range(cores):
        yield (
            lambda rc=rc: jnp.concatenate([refs[rc][0:half, :], refs[cores + rc][0:half, :]], axis=0)
        ), (lambda at=2 * (core ^ rc): two_rows(lse_ref, at, half))


def add_rows(rows, half, twice, norm, acc, cnt):
    for x, lse in rows:
        part, counted = weigh(twice, norm, x().astype(jnp.bfloat16), lse(), cnt.shape[1])
        acc, cnt = acc + part, cnt + counted
    return acc, cnt


def store_sums(out_ref, acc, cnt):
    size, width = acc.shape
    turned = jnp.sum(cnt.T, axis=0, keepdims=True)
    if size < width:
        turned = jnp.concatenate([turned, jnp.zeros((1, width - size), jnp.float32)], axis=1)
    out_ref[0:size, :] = acc
    out_ref[size : size + 8, :] = jnp.broadcast_to(turned, (8, width))


def lead_kernel(cores, order, half, where_ref, twice_ref, norm_ref, acc_ref, cnt_ref, *refs):
    out_acc_ref, out_cnt_ref = refs[-2:]
    near, (d0_ref, d1_ref) = refs[: 2 * cores], refs[2 * cores : 2 * cores + 2]
    size = out_acc_ref.shape[0]
    place = ahead(order, lax.div(where_ref[0], 4), len(order) // 2)
    at = pl.ds(pl.multiple_of(place * size, size), size)
    out_acc_ref[...], out_cnt_ref[...] = add_rows(
        near_rows(cores, half, where_ref[1], near, d0_ref, d1_ref),
        half,
        twice_ref[at, :],
        norm_ref[at, :],
        acc_ref[at, :],
        cnt_ref[at, :],
    )


def block_sums(cores, order, half, steps, where_ref, twice_ref, norm_ref, acc_ref, cnt_ref, lse_ref, near, far, out_ref):
    size = out_ref.shape[0] - 8
    place = ahead(order, lax.div(where_ref[0], 4), steps)
    at = pl.ds(pl.multiple_of(place * size, size), size)
    twice, norm = twice_ref[at, :], norm_ref[at, :]
    acc, cnt = add_rows(
        near_rows(cores, half, where_ref[1], near, far[0], far[cores]),
        half,
        twice,
        norm,
        acc_ref[at, :],
        cnt_ref[at, :],
    )
    acc, cnt = add_rows(far_rows(cores, half, where_ref[1], far, lse_ref), half, twice, norm, acc, cnt)
    store_sums(out_ref, acc, cnt)


def first_kernel(cores, order, half, where_ref, twice_ref, norm_ref, lse_ref, lead_acc_ref, lead_cnt_ref, *refs):
    far, out_ref = refs[: 2 * cores], refs[2 * cores]
    size = lead_acc_ref.shape[0]
    place = ahead(order, lax.div(where_ref[0], 4), len(order) // 2)
    at = pl.ds(pl.multiple_of(place * size, size), size)
    acc, cnt = add_rows(
        far_rows(cores, half, where_ref[1], far, lse_ref),
        half,
        twice_ref[at, :],
        norm_ref[at, :],
        lead_acc_ref[...],
        lead_cnt_ref[...],
    )
    store_sums(out_ref, acc, cnt)


def rest_kernel(cores, order, half, steps, where_ref, twice_ref, norm_ref, acc_ref, cnt_ref, lse_ref, *refs):
    near, far = refs[: 2 * cores], refs[2 * cores : 4 * cores]
    for s, out_ref in zip(steps, refs[4 * cores :]):
        block_sums(
            cores, order, half, s, where_ref, twice_ref, norm_ref, acc_ref, cnt_ref, lse_ref, near, far, out_ref
        )


def ahead(order, line, steps):
    n = len(order)
    return functools.reduce(
        jnp.add,
        [jnp.where(line == order[p], order[(p + steps) % n], 0) for p in range(n)],
    )


def add_kernel(a_ref, b_ref, out_ref):
    out_ref[...] = a_ref[...] + b_ref[...]


def finish_kernel(where_ref, twice_ref, mine_ref, first_ref, second_ref, out_ref):
    size, width = out_ref.shape[0] - 8, out_ref.shape[1]
    start = pl.multiple_of(lax.div(where_ref[0], 4) * size, size)
    c = 0.5 * twice_ref[pl.ds(start, size), :].astype(jnp.float32)
    total = mine_ref[...] + first_ref[...] + second_ref[...]
    counts = total[size:, :]
    column = counts.T[:size, 0:1]
    out_ref[0:size, :] = (total[:size, :] + prior_mass * c) / (column + prior_mass)
    row = lax.broadcasted_iota(jnp.int32, (8, LANES), 0)
    spread = jnp.zeros((8, LANES), jnp.float32)
    for k in range(size // LANES):
        spread = jnp.where(row == k, counts[:, k * LANES : (k + 1) * LANES], spread)
    out_ref[size:, :] = jnp.concatenate([spread] * (width // LANES), axis=1)


def place_kernel(names, order, later, where_ref, *refs):
    count, lines = len(names), len(order)
    block_refs = refs[:count]
    new_ref, counts_out_ref, counts_ref, sems = refs[-4:]
    size = block_refs[0].shape[0] - 8
    plane, line = lax.rem(where_ref[0], 4), lax.div(where_ref[0], 4)
    each = size // LANES
    odd = lax.rem(where_ref[1], 2)
    bits = (0, 1 + odd, 2 - odd, 3)
    places = [ahead(order, line, steps) * 4 + (plane ^ bits[way]) for way, steps in names]
    copies = []
    for i in range(count):
        at = pl.multiple_of(places[i] * size, size)
        copies.append(
            pltpu.make_async_copy(block_refs[i].at[0:size, :], new_ref.at[pl.ds(at, size), :], sems.at[i])
        )
        copies[-1].start()
    if later:
        counts_ref[...] = refs[count][...]
    for i in range(count):
        for k in range(each):
            counts_ref[pl.ds(places[i] * each + k, 1), :] = block_refs[i][size + k : size + k + 1, 0:LANES]
    copies.append(pltpu.make_async_copy(counts_ref, counts_out_ref, sems.at[count]))
    copies[-1].start()
    for copy in copies:
        copy.wait()


def body(n, cores, points, centroids):
    rows, width = points.shape
    local_cent = centroids.shape[0]
    lines = n // 4
    half = rows // (2 * cores)
    share = local_cent // 4
    size = share // lines
    order = tuple(range(0, lines, 2)) + tuple(range(1, lines, 2))[::-1]
    where = jnp.stack([lax.axis_index("dp"), lax.axis_index("cent")]).astype(jnp.int32)

    def exchange(x, kind):
        pairs = [
            (i * cores + c, (i ^ (1 if (kind + c) % 2 == 0 else 2)) * cores + c)
            for i in range(n)
            for c in range(cores)
        ]
        return lax.ppermute(x, ("dp", "cent"), pairs)

    def flip_core(x, bits):
        return lax.ppermute(x, "cent", [(i, i ^ bits) for i in range(cores)])

    def ring(x, way):
        pairs = [(order[p], order[(p + way) % lines]) for p in range(lines)]
        return lax.ppermute(x, "dp", [(4 * a + i, 4 * b + i) for a, b in pairs for i in range(4)])

    def with_siblings(pieces):
        return [a if rc == 0 else flip_core(a, rc) for a in pieces for rc in range(cores)]

    mine = call(open_kernel, f32(2 * half, width), [SMEM, VMEM], (where, points), "open")
    by_a, by_b = exchange(mine, 0), exchange(mine, 1)

    pair, twice, norm = stats(where, points, centroids, lines)
    pairs = [pair] + [flip_core(pair, rc) for rc in range(1, cores)]
    tail = max(8, 2 * cores)
    lse, log_evidence, pack_a, pack_b = call(
        functools.partial(lse_kernel, cores, local_cent * cores),
        (f32(2 * cores, half), f32(rows // LANES, LANES), f32(half + tail, width), f32(half + tail, width)),
        [VMEM] * (2 + cores),
        (by_a, by_b, *pairs),
        "lse",
    )
    d0, d1 = exchange(pack_a, 1), exchange(pack_b, 0)

    by_a, by_b, lse = lax.optimization_barrier((by_a, by_b, lse))
    near = with_siblings((by_a, by_b))
    lanes = min(LANES, half)
    acc, cnt = call(
        functools.partial(own_kernel, cores),
        (f32(share, width), f32(share, lanes)),
        [VMEM] * 4,
        (points, twice, norm, lse),
        "own",
        flops=4 * share * width * rows,
    )
    lse, acc, cnt, near = lax.optimization_barrier((lse, acc, cnt, near))
    lse_d = lax.ppermute(lse, "dp", [(i, i ^ 3) for i in range(n)])
    near, d0, d1, acc, cnt, lse_d = lax.optimization_barrier((near, d0, d1, acc, cnt, lse_d))
    lead = call(
        functools.partial(lead_kernel, cores, order, half),
        (f32(size, width), f32(size, lanes)),
        [SMEM] + [VMEM] * (6 + 2 * cores),
        (where, twice, norm, acc, cnt, *near, d0, d1),
        "lead",
        flops=4 * size * width * 2 * rows,
    )
    given = (where, twice, norm, acc, cnt, lse_d)
    far = with_siblings((d0, d1))
    rows_given = (*near, *far)
    block_sum = f32(size + 8, width)
    turn = lines // 2
    forward = list(range(turn - 1, 0, -1))
    backward = [lines - s for s in range(turn - 1, 0, -1)]
    first = call(
        functools.partial(first_kernel, cores, order, half),
        block_sum,
        [SMEM] + [VMEM] * (5 + 2 * cores),
        (where, twice, norm, lse_d, *lead, *far),
        "first",
        flops=4 * size * width * 2 * rows,
    )

    def sums_of(steps):
        made = call(
            functools.partial(rest_kernel, cores, order, half, steps),
            [block_sum] * len(steps),
            [SMEM] + [VMEM] * (5 + 4 * cores),
            (*given, *rows_given),
            "rest",
            flops=4 * size * width * 3 * rows * len(steps),
        )
        return dict(zip(steps, made))

    def plus(a, b):
        return call(add_kernel, block_sum, [VMEM] * 2, (a, b), "add")

    sums = {**sums_of(backward), **sums_of(forward + [0])}
    from_ahead = ring(sums[backward[0]], -1)
    for s in backward[1:]:
        from_ahead = ring(plus(sums[s], from_ahead), -1)
    from_behind = ring(first, 1)
    for s in forward:
        from_behind = ring(plus(sums[s], from_behind), 1)
    done = call(
        finish_kernel,
        block_sum,
        [SMEM] + [VMEM] * 4,
        (where, twice, sums[0], from_behind, from_ahead),
        "finish",
    )

    steps = [-s for s in range(1, lines // 2 + 1)] + list(range(1, lines // 2))
    got = {(0, 0): done}
    previous, older, plane_b = (), (done, done), [done]
    for s in [0] + steps:
        x = got[0, s]
        if previous:
            x = lax.optimization_barrier((x, *previous))[0]
        got[1, s], got[2, s] = exchange(x, 0), exchange(x, 1)
        if s == steps[-1]:
            break
        got[3, s] = exchange(got[2, s], 0) if s == -1 else exchange(got[1, s], 1)
        plane_b.append(got[2, s])
        previous, older = (plane_b[-2 if s == steps[-2] else -1], *older[:1]), (*older[1:], got[3, s])
        if s == -1:
            previous += (got[1, s],)
        ahead_of = steps[([0] + steps).index(s)]
        x = got[0, ahead_of + (1 if ahead_of < 0 else -1)]
        if ahead_of > 0:
            x = lax.optimization_barrier((x, got[0, s]))[0]
        got[0, ahead_of] = ring(x, 1 if ahead_of < 0 else -1)
    before = got[3, steps[-1] - 1] if steps[-1] > 0 else got[3, steps[-1] + 1]
    before = lax.optimization_barrier((before, got[0, steps[-1]]))[0]
    got[3, steps[-1]] = ring(before, -1 if steps[-1] > 0 else 1)
    late = [(1, steps[-1]), (2, steps[-1])]
    middle = [(w, steps[-2]) for w in (1, 2, 3)] + [(3, steps[-1])]
    groups = ([k for k in got if k not in middle + late], middle, late)
    new = counts = None
    for later, names in enumerate(groups):
        args = [where] + [got[k] for k in names]
        if later:
            args += [counts, new]
        new, counts = call(
            functools.partial(place_kernel, names, order, later),
            (f32(local_cent, width), f32(local_cent // LANES, LANES)),
            [SMEM] + [VMEM] * len(names) + ([VMEM, ANY] if later else []),
            args,
            ("place_early", "place_middle", "place_late")[later],
            out_specs=(ANY, ANY),
            scratch=[
                pltpu.VMEM((local_cent // LANES, LANES), jnp.float32),
                pltpu.SemaphoreType.DMA((len(names) + 1,)),
            ],
            aliases={len(args) - 1: 0} if later else {},
        )
    return new, counts.reshape(-1), log_evidence.reshape(-1)


def solution(mesh):
    n, cores = mesh.shape["dp"], mesh.shape["cent"]
    return jax.shard_map(
        functools.partial(body, n, cores),
        mesh=mesh,
        in_specs=(P("dp", None), P("cent", None)),
        out_specs=(P("cent", None), P("cent"), P("dp")),
        check_vma=False,
    )
```

```python
import functools
import math

import jax
import jax.numpy as jnp
from jax import lax
from jax.experimental import pallas as pl
from jax.experimental.pallas import tpu as pltpu
from jax.sharding import PartitionSpec as P

prior_mass = 0.5
VMEM_LIMIT = 24 * 1024 * 1024
LANES = 128
NT = (((1,), (1,)), ((), ()))
NN = (((1,), (0,)), ((), ()))
VMEM = pl.BlockSpec(memory_space=pltpu.VMEM)
HERE = "here"
ANY = pl.BlockSpec(memory_space=pl.ANY)
HBM = pl.BlockSpec(memory_space=pltpu.HBM)


def f32(*shape):
    return jax.ShapeDtypeStruct(shape, jnp.float32)


def call(kernel, out_shape, in_specs, args, name, out_specs=None, scratch=(), flops=0, aliases={}):
    if in_specs[0] is HERE:
        placed = kernel

        def kernel(*refs):
            placed((lax.axis_index("dp"), lax.axis_index("cent")), *refs)

        in_specs = in_specs[1:]
    return pl.pallas_call(
        kernel,
        out_shape=out_shape,
        in_specs=in_specs,
        out_specs=jax.tree.map(lambda _: VMEM, out_shape) if out_specs is None else out_specs,
        scratch_shapes=list(scratch),
        input_output_aliases=aliases,
        compiler_params=pltpu.CompilerParams(vmem_limit_bytes=VMEM_LIMIT),
        cost_estimate=pl.CostEstimate(
            flops=flops,
            bytes_accessed=sum(a.size * a.dtype.itemsize for a in args),
            transcendentals=0,
        ),
        name=name,
    )(*args)


def open_kernel(here, points_ref, out_ref):
    block = out_ref.shape[0]
    start = pl.multiple_of(here[1] * block, block)
    out_ref[...] = points_ref[pl.ds(start, block), :].astype(jnp.float32)


def widen(norm, width):
    if width <= norm.shape[1]:
        return norm[:, :width]
    return jnp.concatenate([norm] * (width // norm.shape[1]), axis=1)


def norms(c):
    c = c.astype(jnp.float32)
    return jnp.broadcast_to(jnp.sum(c * c, axis=1, keepdims=True), (c.shape[0], LANES))


def stats_kernel(lines, here, points_ref, c_ref, out_ref, twice_ref, norm_ref, all_norm_ref):
    rows, local = points_ref.shape[0], c_ref.shape[0]
    chunk = local // lines
    tile, size = min(256, rows), chunk // 4
    kept = pl.multiple_of(lax.rem(here[0], 4) * size, size)
    for l in range(lines):
        c = c_ref[l * chunk : (l + 1) * chunk, :]
        all_norm_ref[...] = norms(c)
        twice = c + c
        for start in range(0, rows, tile):
            at = slice(start, start + tile)
            dots = lax.dot_general(twice, points_ref[at, :], NT, preferred_element_type=jnp.float32)
            score = dots - widen(all_norm_ref[...], tile)
            top = jnp.max(score, axis=0, keepdims=True)
            total = jnp.sum(jnp.exp(score - top), axis=0, keepdims=True)
            if l:
                old_top, old_total = out_ref[0:1, at], out_ref[1:2, at]
                new_top = jnp.maximum(old_top, top)
                total = old_total * jnp.exp(old_top - new_top) + total * jnp.exp(top - new_top)
                top = new_top
            out_ref[0:1, at] = top
            out_ref[1:2, at] = total
        mine = c_ref[pl.ds(pl.multiple_of(l * chunk + kept, size), size), :]
        twice_ref[l * size : (l + 1) * size, :] = mine + mine
        norm_ref[l * size : (l + 1) * size, :] = all_norm_ref[pl.ds(kept, size), :]


def stats(points, centroids, lines):
    rows, width = points.shape
    local = centroids.shape[0]
    return call(
        functools.partial(stats_kernel, lines),
        (
            f32(2, rows),
            jax.ShapeDtypeStruct((local // 4, width), jnp.bfloat16),
            f32(local // 4, LANES),
        ),
        [HERE, VMEM, VMEM],
        (points, centroids),
        "stats",
        scratch=[pltpu.VMEM((local // lines, LANES), jnp.float32)],
        flops=4 * rows * local * width,
    )


def lse_kernel(cores, every, a_ref, b_ref, *refs):
    pair_refs = refs[:cores]
    lse_ref, evidence_ref, pack_a_ref, pack_b_ref = refs[cores:]
    half = lse_ref.shape[1]
    top = functools.reduce(jnp.maximum, [p[0:1, :] for p in pair_refs])
    total = functools.reduce(jnp.add, [p[1:2, :] * jnp.exp(p[0:1, :] - top) for p in pair_refs])
    lse = top + jnp.log(total)
    evidence = lse - math.log(every)
    for k in range(evidence_ref.shape[0]):
        evidence_ref[k : k + 1, :] = evidence[:, k * LANES : (k + 1) * LANES]
    for i in range(2 * cores):
        lse_ref[i : i + 1, :] = lse[:, i * half : (i + 1) * half]
    for piece, pack_ref in ((a_ref[0:half, :], pack_a_ref), (b_ref[half:, :], pack_b_ref)):
        pack_ref[0:half, :] = piece
        pack_ref[half:, :] = jnp.zeros_like(pack_ref[half:, :])
        pack_ref[half : half + 2 * cores, 0:half] = lse_ref[...]


def weigh(twice, norm, x, lse, lanes):
    dots = lax.dot_general(twice, x, NT, preferred_element_type=jnp.float32)
    score = dots - widen(norm, x.shape[0])
    resp = jnp.exp(score - lse).astype(jnp.bfloat16)
    part = lax.dot_general(resp, x, NN, preferred_element_type=jnp.float32)
    wide = resp.astype(jnp.float32)
    counted = functools.reduce(
        jnp.add, [wide[:, k : k + lanes] for k in range(0, x.shape[0], lanes)]
    )
    return part, counted


def two_rows(ref, at, half):
    return jnp.concatenate([ref[pl.ds(at, 1), :][:, 0:half], ref[pl.ds(at + 1, 1), :][:, 0:half]], axis=1)


def own_kernel(cores, points_ref, twice_ref, norm_ref, lse_ref, acc_ref, cnt_ref):
    half = points_ref.shape[0] // (2 * cores)
    for i in range(cores):
        x = points_ref[2 * i * half : 2 * (i + 1) * half, :]
        lse = two_rows(lse_ref, 2 * i, half)
        part, counted = weigh(twice_ref[...], norm_ref[...], x, lse, cnt_ref.shape[1])
        if i == 0:
            acc_ref[...] = part
            cnt_ref[...] = counted
        else:
            acc_ref[...] += part
            cnt_ref[...] += counted


def near_rows(cores, half, core, refs, d0_ref, d1_ref):
    for kind in range(2):
        for rc in range(cores):
            tail_ref = d1_ref if (kind + rc) % 2 == 0 else d0_ref
            at = half + 2 * (core ^ rc)
            yield (lambda ref=refs[kind * cores + rc]: ref[...]), (
                lambda at=at, tail_ref=tail_ref: two_rows(tail_ref, at, half)
            )


def far_rows(cores, half, core, refs, lse_ref):
    for rc in range(cores):
        yield (
            lambda rc=rc: jnp.concatenate([refs[rc][0:half, :], refs[cores + rc][0:half, :]], axis=0)
        ), (lambda at=2 * (core ^ rc): two_rows(lse_ref, at, half))


def add_rows(rows, half, twice, norm, acc, cnt):
    for x, lse in rows:
        part, counted = weigh(twice, norm, x().astype(jnp.bfloat16), lse(), cnt.shape[1])
        acc, cnt = acc + part, cnt + counted
    return acc, cnt


def store_sums(out_ref, acc, cnt):
    size, width = acc.shape
    turned = jnp.sum(cnt.T, axis=0, keepdims=True)
    if size < width:
        turned = jnp.concatenate([turned, jnp.zeros((1, width - size), jnp.float32)], axis=1)
    out_ref[0:size, :] = acc
    out_ref[size : size + 8, :] = jnp.broadcast_to(turned, (8, width))


def lead_kernel(cores, order, half, here, twice_ref, norm_ref, acc_ref, cnt_ref, *refs):
    out_acc_ref, out_cnt_ref = refs[-2:]
    near, (d0_ref, d1_ref) = refs[: 2 * cores], refs[2 * cores : 2 * cores + 2]
    size = out_acc_ref.shape[0]
    place = ahead(order, lax.div(here[0], 4), len(order) // 2)
    at = pl.ds(pl.multiple_of(place * size, size), size)
    out_acc_ref[...], out_cnt_ref[...] = add_rows(
        near_rows(cores, half, here[1], near, d0_ref, d1_ref),
        half,
        twice_ref[at, :],
        norm_ref[at, :],
        acc_ref[at, :],
        cnt_ref[at, :],
    )


def block_sums(cores, order, half, steps, here, twice_ref, norm_ref, acc_ref, cnt_ref, lse_ref, near, far, out_ref):
    size = out_ref.shape[0] - 8
    place = ahead(order, lax.div(here[0], 4), steps)
    at = pl.ds(pl.multiple_of(place * size, size), size)
    twice, norm = twice_ref[at, :], norm_ref[at, :]
    acc, cnt = add_rows(
        near_rows(cores, half, here[1], near, far[0], far[cores]),
        half,
        twice,
        norm,
        acc_ref[at, :],
        cnt_ref[at, :],
    )
    acc, cnt = add_rows(far_rows(cores, half, here[1], far, lse_ref), half, twice, norm, acc, cnt)
    store_sums(out_ref, acc, cnt)


def first_kernel(cores, order, half, here, twice_ref, norm_ref, lse_ref, lead_acc_ref, lead_cnt_ref, *refs):
    far, out_ref = refs[: 2 * cores], refs[2 * cores]
    size = lead_acc_ref.shape[0]
    place = ahead(order, lax.div(here[0], 4), len(order) // 2)
    at = pl.ds(pl.multiple_of(place * size, size), size)
    acc, cnt = add_rows(
        far_rows(cores, half, here[1], far, lse_ref),
        half,
        twice_ref[at, :],
        norm_ref[at, :],
        lead_acc_ref[...],
        lead_cnt_ref[...],
    )
    store_sums(out_ref, acc, cnt)


def rest_kernel(cores, order, half, steps, here, twice_ref, norm_ref, acc_ref, cnt_ref, lse_ref, *refs):
    near, far = refs[: 2 * cores], refs[2 * cores : 4 * cores]
    for s, out_ref in zip(steps, refs[4 * cores :]):
        block_sums(
            cores, order, half, s, here, twice_ref, norm_ref, acc_ref, cnt_ref, lse_ref, near, far, out_ref
        )


def ahead(order, line, steps):
    n = len(order)
    return functools.reduce(
        jnp.add,
        [jnp.where(line == order[p], order[(p + steps) % n], 0) for p in range(n)],
    )


def add_kernel(a_ref, b_ref, out_ref):
    out_ref[...] = a_ref[...] + b_ref[...]


def finish_kernel(here, twice_ref, mine_ref, first_ref, second_ref, out_ref):
    size, width = out_ref.shape[0] - 8, out_ref.shape[1]
    start = pl.multiple_of(lax.div(here[0], 4) * size, size)
    c = 0.5 * twice_ref[pl.ds(start, size), :].astype(jnp.float32)
    total = mine_ref[...] + first_ref[...] + second_ref[...]
    counts = total[size:, :]
    column = counts.T[:size, 0:1]
    out_ref[0:size, :] = (total[:size, :] + prior_mass * c) / (column + prior_mass)
    row = lax.broadcasted_iota(jnp.int32, (8, LANES), 0)
    spread = jnp.zeros((8, LANES), jnp.float32)
    for k in range(size // LANES):
        spread = jnp.where(row == k, counts[:, k * LANES : (k + 1) * LANES], spread)
    out_ref[size:, :] = jnp.concatenate([spread] * (width // LANES), axis=1)


def place_kernel(names, order, later, here, *refs):
    count, lines = len(names), len(order)
    block_refs = refs[:count]
    new_ref, counts_out_ref, counts_ref, sems = refs[-4:]
    size = block_refs[0].shape[0] - 8
    plane, line = lax.rem(here[0], 4), lax.div(here[0], 4)
    each = size // LANES
    odd = lax.rem(here[1], 2)
    bits = (0, 1 + odd, 2 - odd, 3)
    places = [ahead(order, line, steps) * 4 + (plane ^ bits[way]) for way, steps in names]
    copies = []
    for i in range(count):
        at = pl.multiple_of(places[i] * size, size)
        copies.append(
            pltpu.make_async_copy(block_refs[i].at[0:size, :], new_ref.at[pl.ds(at, size), :], sems.at[i])
        )
        copies[-1].start()
    if later:
        counts_ref[...] = refs[count][...]
    for i in range(count):
        for k in range(each):
            counts_ref[pl.ds(places[i] * each + k, 1), :] = block_refs[i][size + k : size + k + 1, 0:LANES]
    copies.append(pltpu.make_async_copy(counts_ref, counts_out_ref, sems.at[count]))
    copies[-1].start()
    for copy in copies:
        copy.wait()


def body(n, cores, points, centroids):
    rows, width = points.shape
    local_cent = centroids.shape[0]
    lines = n // 4
    half = rows // (2 * cores)
    share = local_cent // 4
    size = share // lines
    order = tuple(range(0, lines, 2)) + tuple(range(1, lines, 2))[::-1]

    def exchange(x, kind):
        pairs = [
            (i * cores + c, (i ^ (1 if (kind + c) % 2 == 0 else 2)) * cores + c)
            for i in range(n)
            for c in range(cores)
        ]
        return lax.ppermute(x, ("dp", "cent"), pairs)

    def flip_core(x, bits):
        return lax.ppermute(x, "cent", [(i, i ^ bits) for i in range(cores)])

    def ring(x, way):
        pairs = [(order[p], order[(p + way) % lines]) for p in range(lines)]
        return lax.ppermute(x, "dp", [(4 * a + i, 4 * b + i) for a, b in pairs for i in range(4)])

    def with_siblings(pieces):
        return [a if rc == 0 else flip_core(a, rc) for a in pieces for rc in range(cores)]

    mine = call(open_kernel, f32(2 * half, width), [HERE, VMEM], (points,), "open")
    by_a, by_b = exchange(mine, 0), exchange(mine, 1)

    pair, twice, norm = stats(points, centroids, lines)
    pairs = [pair] + [flip_core(pair, rc) for rc in range(1, cores)]
    tail = max(8, 2 * cores)
    lse, log_evidence, pack_a, pack_b = call(
        functools.partial(lse_kernel, cores, local_cent * cores),
        (f32(2 * cores, half), f32(rows // LANES, LANES), f32(half + tail, width), f32(half + tail, width)),
        [VMEM] * (2 + cores),
        (by_a, by_b, *pairs),
        "lse",
    )
    d0, d1 = exchange(pack_a, 1), exchange(pack_b, 0)

    by_a, by_b, lse = lax.optimization_barrier((by_a, by_b, lse))
    near = with_siblings((by_a, by_b))
    lanes = min(LANES, half)
    acc, cnt = call(
        functools.partial(own_kernel, cores),
        (f32(share, width), f32(share, lanes)),
        [VMEM] * 4,
        (points, twice, norm, lse),
        "own",
        flops=4 * share * width * rows,
    )
    lse, acc, cnt, near = lax.optimization_barrier((lse, acc, cnt, near))
    lse_d = lax.ppermute(lse, "dp", [(i, i ^ 3) for i in range(n)])
    near, d0, d1, acc, cnt, lse_d = lax.optimization_barrier((near, d0, d1, acc, cnt, lse_d))
    lead = call(
        functools.partial(lead_kernel, cores, order, half),
        (f32(size, width), f32(size, lanes)),
        [HERE] + [VMEM] * (6 + 2 * cores),
        (twice, norm, acc, cnt, *near, d0, d1),
        "lead",
        flops=4 * size * width * 2 * rows,
    )
    given = (twice, norm, acc, cnt, lse_d)
    far = with_siblings((d0, d1))
    rows_given = (*near, *far)
    block_sum = f32(size + 8, width)
    turn = lines // 2
    forward = list(range(turn - 1, 0, -1))
    backward = [lines - s for s in range(turn - 1, 0, -1)]
    first = call(
        functools.partial(first_kernel, cores, order, half),
        block_sum,
        [HERE] + [VMEM] * (5 + 2 * cores),
        (twice, norm, lse_d, *lead, *far),
        "first",
        flops=4 * size * width * 2 * rows,
    )

    def sums_of(steps):
        made = call(
            functools.partial(rest_kernel, cores, order, half, steps),
            [block_sum] * len(steps),
            [HERE] + [VMEM] * (5 + 4 * cores),
            (*given, *rows_given),
            "rest",
            flops=4 * size * width * 3 * rows * len(steps),
        )
        return dict(zip(steps, made))

    def plus(a, b):
        return call(add_kernel, block_sum, [VMEM] * 2, (a, b), "add")

    sums = {**sums_of(backward), **sums_of(forward + [0])}
    from_ahead = ring(sums[backward[0]], -1)
    for s in backward[1:]:
        from_ahead = ring(plus(sums[s], from_ahead), -1)
    from_behind = ring(first, 1)
    for s in forward:
        from_behind = ring(plus(sums[s], from_behind), 1)
    done = call(
        finish_kernel,
        block_sum,
        [HERE] + [VMEM] * 4,
        (twice, sums[0], from_behind, from_ahead),
        "finish",
    )

    steps = [-s for s in range(1, lines // 2 + 1)] + list(range(1, lines // 2))
    got = {(0, 0): done}
    previous, older, plane_b = (), (done, done), [done]
    for s in [0] + steps:
        x = got[0, s]
        if previous:
            x = lax.optimization_barrier((x, *previous))[0]
        got[1, s], got[2, s] = exchange(x, 0), exchange(x, 1)
        if s == steps[-1]:
            break
        got[3, s] = exchange(got[1, s], 1)
        plane_b.append(got[2, s])
        previous, older = (plane_b[-2 if s == steps[-2] else -1], *older[:1]), (*older[1:], got[3, s])
        ahead_of = steps[([0] + steps).index(s)]
        x = got[0, ahead_of + (1 if ahead_of < 0 else -1)]
        if ahead_of > 0:
            x = lax.optimization_barrier((x, got[0, s]))[0]
        got[0, ahead_of] = ring(x, 1 if ahead_of < 0 else -1)
    before = got[3, steps[-1] - 1] if steps[-1] > 0 else got[3, steps[-1] + 1]
    before = lax.optimization_barrier((before, got[0, steps[-1]]))[0]
    got[3, steps[-1]] = ring(before, -1 if steps[-1] > 0 else 1)
    late = [(1, steps[-1]), (2, steps[-1])]
    middle = [(w, steps[-2]) for w in (1, 2, 3)] + [(3, steps[-1])]
    groups = ([k for k in got if k not in middle + late], middle, late)
    new = counts = None
    for later, names in enumerate(groups):
        args = [got[k] for k in names]
        if later:
            args += [counts, new]
        new, counts = call(
            functools.partial(place_kernel, names, order, later),
            (f32(local_cent, width), f32(local_cent // LANES, LANES)),
            [HERE] + [VMEM] * len(names) + ([VMEM, ANY] if later else []),
            args,
            ("place_early", "place_middle", "place_late")[later],
            out_specs=(ANY, ANY),
            scratch=[
                pltpu.VMEM((local_cent // LANES, LANES), jnp.float32),
                pltpu.SemaphoreType.DMA((len(names) + 1,)),
            ],
            aliases={len(args) - 1: 0} if later else {},
        )
    return new, counts.reshape(-1), log_evidence.reshape(-1)


def solution(mesh):
    n, cores = mesh.shape["dp"], mesh.shape["cent"]
    return jax.shard_map(
        functools.partial(body, n, cores),
        mesh=mesh,
        in_specs=(P("dp", None), P("cent", None)),
        out_specs=(P("cent", None), P("cent"), P("dp")),
        check_vma=False,
    )
```

```python
import functools
import math

import jax
import jax.numpy as jnp
from jax import lax
from jax.experimental import pallas as pl
from jax.experimental.pallas import tpu as pltpu
from jax.sharding import PartitionSpec as P

prior_mass = 0.5
VMEM_LIMIT = 24 * 1024 * 1024
LANES = 128
NT = (((1,), (1,)), ((), ()))
NN = (((1,), (0,)), ((), ()))
VMEM = pl.BlockSpec(memory_space=pltpu.VMEM)
HERE = "here"
ANY = pl.BlockSpec(memory_space=pl.ANY)
HBM = pl.BlockSpec(memory_space=pltpu.HBM)


def f32(*shape):
    return jax.ShapeDtypeStruct(shape, jnp.float32)


def call(kernel, out_shape, in_specs, args, name, out_specs=None, scratch=(), flops=0, aliases={}):
    if in_specs[0] is HERE:
        placed = kernel

        def kernel(*refs):
            placed((lax.axis_index("dp"), lax.axis_index("cent")), *refs)

        in_specs = in_specs[1:]
    return pl.pallas_call(
        kernel,
        out_shape=out_shape,
        in_specs=in_specs,
        out_specs=jax.tree.map(lambda _: VMEM, out_shape) if out_specs is None else out_specs,
        scratch_shapes=list(scratch),
        input_output_aliases=aliases,
        compiler_params=pltpu.CompilerParams(vmem_limit_bytes=VMEM_LIMIT),
        cost_estimate=pl.CostEstimate(
            flops=flops,
            bytes_accessed=sum(a.size * a.dtype.itemsize for a in args),
            transcendentals=0,
        ),
        name=name,
    )(*args)


def open_kernel(here, points_ref, out_ref):
    block = out_ref.shape[0]
    start = pl.multiple_of(here[1] * block, block)
    out_ref[...] = points_ref[pl.ds(start, block), :].astype(jnp.float32)


def widen(norm, width):
    if width <= norm.shape[1]:
        return norm[:, :width]
    return jnp.concatenate([norm] * (width // norm.shape[1]), axis=1)


def norms(c):
    c = c.astype(jnp.float32)
    return jnp.broadcast_to(jnp.sum(c * c, axis=1, keepdims=True), (c.shape[0], LANES))


def stats_kernel(lines, here, points_ref, c_ref, out_ref, twice_ref, norm_ref, all_norm_ref):
    rows, local = points_ref.shape[0], c_ref.shape[0]
    chunk = local // lines
    tile, size = min(256, rows), chunk // 4
    kept = pl.multiple_of(lax.rem(here[0], 4) * size, size)
    for l in range(lines):
        c = c_ref[l * chunk : (l + 1) * chunk, :]
        all_norm_ref[...] = norms(c)
        twice = c + c
        for start in range(0, rows, tile):
            at = slice(start, start + tile)
            dots = lax.dot_general(twice, points_ref[at, :], NT, preferred_element_type=jnp.float32)
            score = dots - widen(all_norm_ref[...], tile)
            top = jnp.max(score, axis=0, keepdims=True)
            total = jnp.sum(jnp.exp(score - top), axis=0, keepdims=True)
            if l:
                old_top, old_total = out_ref[0:1, at], out_ref[1:2, at]
                new_top = jnp.maximum(old_top, top)
                total = old_total * jnp.exp(old_top - new_top) + total * jnp.exp(top - new_top)
                top = new_top
            out_ref[0:1, at] = top
            out_ref[1:2, at] = total
        mine = c_ref[pl.ds(pl.multiple_of(l * chunk + kept, size), size), :]
        twice_ref[l * size : (l + 1) * size, :] = mine + mine
        norm_ref[l * size : (l + 1) * size, :] = all_norm_ref[pl.ds(kept, size), :]


def stats(points, centroids, lines):
    rows, width = points.shape
    local = centroids.shape[0]
    return call(
        functools.partial(stats_kernel, lines),
        (
            f32(2, rows),
            jax.ShapeDtypeStruct((local // 4, width), jnp.bfloat16),
            f32(local // 4, LANES),
        ),
        [HERE, VMEM, VMEM],
        (points, centroids),
        "stats",
        scratch=[pltpu.VMEM((local // lines, LANES), jnp.float32)],
        flops=4 * rows * local * width,
    )


def lse_kernel(cores, every, *refs):
    pair_refs = refs[:cores]
    lse_ref, evidence_ref = refs[cores:]
    half = lse_ref.shape[1]
    top = functools.reduce(jnp.maximum, [p[0:1, :] for p in pair_refs])
    total = functools.reduce(jnp.add, [p[1:2, :] * jnp.exp(p[0:1, :] - top) for p in pair_refs])
    lse = top + jnp.log(total)
    evidence = lse - math.log(every)
    for k in range(evidence_ref.shape[0]):
        evidence_ref[k : k + 1, :] = evidence[:, k * LANES : (k + 1) * LANES]
    for i in range(2 * cores):
        lse_ref[i : i + 1, :] = lse[:, i * half : (i + 1) * half]


def pack_kernel(lse_ref, a_ref, b_ref, pack_a_ref, pack_b_ref):
    count, half = lse_ref.shape
    for piece, pack_ref in ((a_ref[0:half, :], pack_a_ref), (b_ref[half:, :], pack_b_ref)):
        pack_ref[0:half, :] = piece
        pack_ref[half:, :] = jnp.zeros_like(pack_ref[half:, :])
        pack_ref[half : half + count, 0:half] = lse_ref[...]


def weigh(twice, norm, x, lse, lanes):
    dots = lax.dot_general(twice, x, NT, preferred_element_type=jnp.float32)
    score = dots - widen(norm, x.shape[0])
    resp = jnp.exp(score - lse).astype(jnp.bfloat16)
    part = lax.dot_general(resp, x, NN, preferred_element_type=jnp.float32)
    wide = resp.astype(jnp.float32)
    counted = functools.reduce(
        jnp.add, [wide[:, k : k + lanes] for k in range(0, x.shape[0], lanes)]
    )
    return part, counted


def two_rows(ref, at, half):
    return jnp.concatenate([ref[pl.ds(at, 1), :][:, 0:half], ref[pl.ds(at + 1, 1), :][:, 0:half]], axis=1)


def own_kernel(cores, points_ref, twice_ref, norm_ref, lse_ref, acc_ref, cnt_ref):
    half = points_ref.shape[0] // (2 * cores)
    for i in range(cores):
        x = points_ref[2 * i * half : 2 * (i + 1) * half, :]
        lse = two_rows(lse_ref, 2 * i, half)
        part, counted = weigh(twice_ref[...], norm_ref[...], x, lse, cnt_ref.shape[1])
        if i == 0:
            acc_ref[...] = part
            cnt_ref[...] = counted
        else:
            acc_ref[...] += part
            cnt_ref[...] += counted


def near_rows(cores, half, core, refs, d0_ref, d1_ref):
    for kind in range(2):
        for rc in range(cores):
            tail_ref = d1_ref if (kind + rc) % 2 == 0 else d0_ref
            at = half + 2 * (core ^ rc)
            yield (lambda ref=refs[kind * cores + rc]: ref[...]), (
                lambda at=at, tail_ref=tail_ref: two_rows(tail_ref, at, half)
            )


def far_rows(cores, half, core, refs, lse_ref):
    for rc in range(cores):
        yield (
            lambda rc=rc: jnp.concatenate([refs[rc][0:half, :], refs[cores + rc][0:half, :]], axis=0)
        ), (lambda at=2 * (core ^ rc): two_rows(lse_ref, at, half))


def add_rows(rows, half, twice, norm, acc, cnt):
    for x, lse in rows:
        part, counted = weigh(twice, norm, x().astype(jnp.bfloat16), lse(), cnt.shape[1])
        acc, cnt = acc + part, cnt + counted
    return acc, cnt


def store_sums(out_ref, acc, cnt):
    size, width = acc.shape
    turned = jnp.sum(cnt.T, axis=0, keepdims=True)
    if size < width:
        turned = jnp.concatenate([turned, jnp.zeros((1, width - size), jnp.float32)], axis=1)
    out_ref[0:size, :] = acc
    out_ref[size : size + 8, :] = jnp.broadcast_to(turned, (8, width))


def lead_kernel(cores, order, half, here, twice_ref, norm_ref, acc_ref, cnt_ref, *refs):
    out_acc_ref, out_cnt_ref = refs[-2:]
    near, (d0_ref, d1_ref) = refs[: 2 * cores], refs[2 * cores : 2 * cores + 2]
    size = out_acc_ref.shape[0]
    place = ahead(order, lax.div(here[0], 4), len(order) // 2)
    at = pl.ds(pl.multiple_of(place * size, size), size)
    out_acc_ref[...], out_cnt_ref[...] = add_rows(
        near_rows(cores, half, here[1], near, d0_ref, d1_ref),
        half,
        twice_ref[at, :],
        norm_ref[at, :],
        acc_ref[at, :],
        cnt_ref[at, :],
    )


def block_sums(cores, order, half, steps, here, twice_ref, norm_ref, acc_ref, cnt_ref, lse_ref, near, far, out_ref):
    size = out_ref.shape[0] - 8
    place = ahead(order, lax.div(here[0], 4), steps)
    at = pl.ds(pl.multiple_of(place * size, size), size)
    twice, norm = twice_ref[at, :], norm_ref[at, :]
    acc, cnt = add_rows(
        near_rows(cores, half, here[1], near, far[0], far[cores]),
        half,
        twice,
        norm,
        acc_ref[at, :],
        cnt_ref[at, :],
    )
    acc, cnt = add_rows(far_rows(cores, half, here[1], far, lse_ref), half, twice, norm, acc, cnt)
    store_sums(out_ref, acc, cnt)


def first_kernel(cores, order, half, here, twice_ref, norm_ref, lse_ref, lead_acc_ref, lead_cnt_ref, *refs):
    far, out_ref = refs[: 2 * cores], refs[2 * cores]
    size = lead_acc_ref.shape[0]
    place = ahead(order, lax.div(here[0], 4), len(order) // 2)
    at = pl.ds(pl.multiple_of(place * size, size), size)
    acc, cnt = add_rows(
        far_rows(cores, half, here[1], far, lse_ref),
        half,
        twice_ref[at, :],
        norm_ref[at, :],
        lead_acc_ref[...],
        lead_cnt_ref[...],
    )
    store_sums(out_ref, acc, cnt)


def rest_kernel(cores, order, half, steps, here, twice_ref, norm_ref, acc_ref, cnt_ref, lse_ref, *refs):
    near, far = refs[: 2 * cores], refs[2 * cores : 4 * cores]
    for s, out_ref in zip(steps, refs[4 * cores :]):
        block_sums(
            cores, order, half, s, here, twice_ref, norm_ref, acc_ref, cnt_ref, lse_ref, near, far, out_ref
        )


def ahead(order, line, steps):
    n = len(order)
    return functools.reduce(
        jnp.add,
        [jnp.where(line == order[p], order[(p + steps) % n], 0) for p in range(n)],
    )


def add_kernel(a_ref, b_ref, out_ref):
    out_ref[...] = a_ref[...] + b_ref[...]


def finish_kernel(here, twice_ref, mine_ref, first_ref, second_ref, out_ref):
    size, width = out_ref.shape[0] - 8, out_ref.shape[1]
    start = pl.multiple_of(lax.div(here[0], 4) * size, size)
    c = 0.5 * twice_ref[pl.ds(start, size), :].astype(jnp.float32)
    total = mine_ref[...] + first_ref[...] + second_ref[...]
    counts = total[size:, :]
    column = counts.T[:size, 0:1]
    out_ref[0:size, :] = (total[:size, :] + prior_mass * c) / (column + prior_mass)
    row = lax.broadcasted_iota(jnp.int32, (8, LANES), 0)
    spread = jnp.zeros((8, LANES), jnp.float32)
    for k in range(size // LANES):
        spread = jnp.where(row == k, counts[:, k * LANES : (k + 1) * LANES], spread)
    out_ref[size:, :] = jnp.concatenate([spread] * (width // LANES), axis=1)


def place_kernel(names, order, later, here, *refs):
    count, lines = len(names), len(order)
    block_refs = refs[:count]
    new_ref, counts_out_ref, counts_ref, sems = refs[-4:]
    size = block_refs[0].shape[0] - 8
    plane, line = lax.rem(here[0], 4), lax.div(here[0], 4)
    each = size // LANES
    odd = lax.rem(here[1], 2)
    bits = (0, 1 + odd, 2 - odd, 3)
    places = [ahead(order, line, steps) * 4 + (plane ^ bits[way]) for way, steps in names]
    copies = []
    for i in range(count):
        at = pl.multiple_of(places[i] * size, size)
        copies.append(
            pltpu.make_async_copy(block_refs[i].at[0:size, :], new_ref.at[pl.ds(at, size), :], sems.at[i])
        )
        copies[-1].start()
    if later:
        counts_ref[...] = refs[count][...]
    for i in range(count):
        for k in range(each):
            counts_ref[pl.ds(places[i] * each + k, 1), :] = block_refs[i][size + k : size + k + 1, 0:LANES]
    copies.append(pltpu.make_async_copy(counts_ref, counts_out_ref, sems.at[count]))
    copies[-1].start()
    for copy in copies:
        copy.wait()


def body(n, cores, points, centroids):
    rows, width = points.shape
    local_cent = centroids.shape[0]
    lines = n // 4
    half = rows // (2 * cores)
    share = local_cent // 4
    size = share // lines
    order = tuple(range(0, lines, 2)) + tuple(range(1, lines, 2))[::-1]

    def exchange(x, kind):
        pairs = [
            (i * cores + c, (i ^ (1 if (kind + c) % 2 == 0 else 2)) * cores + c)
            for i in range(n)
            for c in range(cores)
        ]
        return lax.ppermute(x, ("dp", "cent"), pairs)

    def flip_core(x, bits):
        return lax.ppermute(x, "cent", [(i, i ^ bits) for i in range(cores)])

    def ring(x, way):
        pairs = [(order[p], order[(p + way) % lines]) for p in range(lines)]
        return lax.ppermute(x, "dp", [(4 * a + i, 4 * b + i) for a, b in pairs for i in range(4)])

    def with_siblings(pieces):
        return [a if rc == 0 else flip_core(a, rc) for a in pieces for rc in range(cores)]

    mine = call(open_kernel, f32(2 * half, width), [HERE, VMEM], (points,), "open")
    by_a, by_b = exchange(mine, 0), exchange(mine, 1)

    pair, twice, norm = stats(points, centroids, lines)
    pairs = [pair] + [flip_core(pair, rc) for rc in range(1, cores)]
    lse, log_evidence = call(
        functools.partial(lse_kernel, cores, local_cent * cores),
        (f32(2 * cores, half), f32(rows // LANES, LANES)),
        [VMEM] * cores,
        pairs,
        "lse",
    )
    lanes = min(LANES, half)
    acc, cnt = call(
        functools.partial(own_kernel, cores),
        (f32(share, width), f32(share, lanes)),
        [VMEM] * 4,
        (points, twice, norm, lse),
        "own",
        flops=4 * share * width * rows,
    )
    lse, acc, cnt, by_a, by_b = lax.optimization_barrier((lse, acc, cnt, by_a, by_b))
    piece = f32(half + max(8, 2 * cores), width)
    pack_a, pack_b = call(pack_kernel, (piece, piece), [VMEM] * 3, (lse, by_a, by_b), "pack")
    d0, d1 = exchange(pack_a, 1), exchange(pack_b, 0)
    lse_d = lax.ppermute(lse, "dp", [(i, i ^ 3) for i in range(n)])
    by_a, by_b, _ = lax.optimization_barrier((by_a, by_b, pack_a))
    near = with_siblings((by_a, by_b))
    near, d0, d1, acc, cnt, lse_d = lax.optimization_barrier((near, d0, d1, acc, cnt, lse_d))
    lead = call(
        functools.partial(lead_kernel, cores, order, half),
        (f32(size, width), f32(size, lanes)),
        [HERE] + [VMEM] * (6 + 2 * cores),
        (twice, norm, acc, cnt, *near, d0, d1),
        "lead",
        flops=4 * size * width * 2 * rows,
    )
    given = (twice, norm, acc, cnt, lse_d)
    far = with_siblings((d0, d1))
    rows_given = (*near, *far)
    block_sum = f32(size + 8, width)
    turn = lines // 2
    forward = list(range(turn - 1, 0, -1))
    backward = [lines - s for s in range(turn - 1, 0, -1)]
    first = call(
        functools.partial(first_kernel, cores, order, half),
        block_sum,
        [HERE] + [VMEM] * (5 + 2 * cores),
        (twice, norm, lse_d, *lead, *far),
        "first",
        flops=4 * size * width * 2 * rows,
    )

    def sums_of(steps):
        made = call(
            functools.partial(rest_kernel, cores, order, half, steps),
            [block_sum] * len(steps),
            [HERE] + [VMEM] * (5 + 4 * cores),
            (*given, *rows_given),
            "rest",
            flops=4 * size * width * 3 * rows * len(steps),
        )
        return dict(zip(steps, made))

    def plus(a, b):
        return call(add_kernel, block_sum, [VMEM] * 2, (a, b), "add")

    sums = {**sums_of(backward), **sums_of(forward + [0])}
    from_ahead = ring(sums[backward[0]], -1)
    for s in backward[1:]:
        from_ahead = ring(plus(sums[s], from_ahead), -1)
    from_behind = ring(first, 1)
    for s in forward:
        from_behind = ring(plus(sums[s], from_behind), 1)
    done = call(
        finish_kernel,
        block_sum,
        [HERE] + [VMEM] * 4,
        (twice, sums[0], from_behind, from_ahead),
        "finish",
    )

    steps = [-s for s in range(1, lines // 2 + 1)] + list(range(1, lines // 2))
    got = {(0, 0): done}
    previous, older, plane_b = (), (done, done), [done]
    for s in [0] + steps:
        x = got[0, s]
        if previous:
            x = lax.optimization_barrier((x, *previous))[0]
        got[1, s], got[2, s] = exchange(x, 0), exchange(x, 1)
        if s == steps[-1]:
            break
        got[3, s] = exchange(got[1, s], 1)
        plane_b.append(got[2, s])
        previous, older = (plane_b[-2 if s == steps[-2] else -1], *older[:1]), (*older[1:], got[3, s])
        ahead_of = steps[([0] + steps).index(s)]
        x = got[0, ahead_of + (1 if ahead_of < 0 else -1)]
        if ahead_of > 0:
            x = lax.optimization_barrier((x, got[0, s]))[0]
        got[0, ahead_of] = ring(x, 1 if ahead_of < 0 else -1)
    before = got[3, steps[-1] - 1] if steps[-1] > 0 else got[3, steps[-1] + 1]
    before = lax.optimization_barrier((before, got[0, steps[-1]]))[0]
    got[3, steps[-1]] = ring(before, -1 if steps[-1] > 0 else 1)
    late = [(1, steps[-1]), (2, steps[-1])]
    middle = [(w, steps[-2]) for w in (1, 2, 3)] + [(3, steps[-1])]
    groups = ([k for k in got if k not in middle + late], middle, late)
    new = counts = None
    for later, names in enumerate(groups):
        args = [got[k] for k in names]
        if later:
            args += [counts, new]
        new, counts = call(
            functools.partial(place_kernel, names, order, later),
            (f32(local_cent, width), f32(local_cent // LANES, LANES)),
            [HERE] + [VMEM] * len(names) + ([VMEM, ANY] if later else []),
            args,
            ("place_early", "place_middle", "place_late")[later],
            out_specs=(ANY, ANY),
            scratch=[
                pltpu.VMEM((local_cent // LANES, LANES), jnp.float32),
                pltpu.SemaphoreType.DMA((len(names) + 1,)),
            ],
            aliases={len(args) - 1: 0} if later else {},
        )
    return new, counts.reshape(-1), log_evidence.reshape(-1)


def solution(mesh):
    n, cores = mesh.shape["dp"], mesh.shape["cent"]
    return jax.shard_map(
        functools.partial(body, n, cores),
        mesh=mesh,
        in_specs=(P("dp", None), P("cent", None)),
        out_specs=(P("cent", None), P("cent"), P("dp")),
        check_vma=False,
    )
```

```python
import functools
import math

import jax
import jax.numpy as jnp
from jax import lax
from jax.experimental import pallas as pl
from jax.experimental.pallas import tpu as pltpu
from jax.sharding import PartitionSpec as P

prior_mass = 0.5
VMEM_LIMIT = 24 * 1024 * 1024
LANES = 128
NT = (((1,), (1,)), ((), ()))
NN = (((1,), (0,)), ((), ()))
VMEM = pl.BlockSpec(memory_space=pltpu.VMEM)
HERE = "here"
ANY = pl.BlockSpec(memory_space=pl.ANY)
HBM = pl.BlockSpec(memory_space=pltpu.HBM)


def f32(*shape):
    return jax.ShapeDtypeStruct(shape, jnp.float32)


def call(kernel, out_shape, in_specs, args, name, out_specs=None, scratch=(), flops=0, aliases={}):
    if in_specs[0] is HERE:
        placed = kernel

        def kernel(*refs):
            placed((lax.axis_index("dp"), lax.axis_index("cent")), *refs)

        in_specs = in_specs[1:]
    return pl.pallas_call(
        kernel,
        out_shape=out_shape,
        in_specs=in_specs,
        out_specs=jax.tree.map(lambda _: VMEM, out_shape) if out_specs is None else out_specs,
        scratch_shapes=list(scratch),
        input_output_aliases=aliases,
        compiler_params=pltpu.CompilerParams(vmem_limit_bytes=VMEM_LIMIT),
        cost_estimate=pl.CostEstimate(
            flops=flops,
            bytes_accessed=sum(a.size * a.dtype.itemsize for a in args),
            transcendentals=0,
        ),
        name=name,
    )(*args)


def open_kernel(here, points_ref, out_ref):
    block = out_ref.shape[0]
    start = pl.multiple_of(here[1] * block, block)
    out_ref[...] = points_ref[pl.ds(start, block), :].astype(jnp.float32)


def widen(norm, width):
    if width <= norm.shape[1]:
        return norm[:, :width]
    return jnp.concatenate([norm] * (width // norm.shape[1]), axis=1)


def norms(c):
    c = c.astype(jnp.float32)
    return jnp.broadcast_to(jnp.sum(c * c, axis=1, keepdims=True), (c.shape[0], LANES))


def stats_kernel(lines, here, points_ref, c_ref, out_ref, twice_ref, norm_ref, all_norm_ref):
    rows, local = points_ref.shape[0], c_ref.shape[0]
    chunk = local // lines
    tile, size = min(256, rows), chunk // 4
    kept = pl.multiple_of(lax.rem(here[0], 4) * size, size)
    for l in range(lines):
        c = c_ref[l * chunk : (l + 1) * chunk, :]
        all_norm_ref[...] = norms(c)
        twice = c + c
        for start in range(0, rows, tile):
            at = slice(start, start + tile)
            dots = lax.dot_general(twice, points_ref[at, :], NT, preferred_element_type=jnp.float32)
            score = dots - widen(all_norm_ref[...], tile)
            top = jnp.max(score, axis=0, keepdims=True)
            total = jnp.sum(jnp.exp(score - top), axis=0, keepdims=True)
            if l:
                old_top, old_total = out_ref[0:1, at], out_ref[1:2, at]
                new_top = jnp.maximum(old_top, top)
                total = old_total * jnp.exp(old_top - new_top) + total * jnp.exp(top - new_top)
                top = new_top
            out_ref[0:1, at] = top
            out_ref[1:2, at] = total
        mine = c_ref[pl.ds(pl.multiple_of(l * chunk + kept, size), size), :]
        twice_ref[l * size : (l + 1) * size, :] = mine + mine
        norm_ref[l * size : (l + 1) * size, :] = all_norm_ref[pl.ds(kept, size), :]


def stats(points, centroids, lines):
    rows, width = points.shape
    local = centroids.shape[0]
    return call(
        functools.partial(stats_kernel, lines),
        (
            f32(2, rows),
            jax.ShapeDtypeStruct((local // 4, width), jnp.bfloat16),
            f32(local // 4, LANES),
        ),
        [HERE, VMEM, VMEM],
        (points, centroids),
        "stats",
        scratch=[pltpu.VMEM((local // lines, LANES), jnp.float32)],
        flops=4 * rows * local * width,
    )


def lse_kernel(cores, every, *refs):
    pair_refs = refs[:cores]
    lse_ref, evidence_ref = refs[cores:]
    half = lse_ref.shape[1]
    top = functools.reduce(jnp.maximum, [p[0:1, :] for p in pair_refs])
    total = functools.reduce(jnp.add, [p[1:2, :] * jnp.exp(p[0:1, :] - top) for p in pair_refs])
    lse = top + jnp.log(total)
    evidence = lse - math.log(every)
    for k in range(evidence_ref.shape[0]):
        evidence_ref[k : k + 1, :] = evidence[:, k * LANES : (k + 1) * LANES]
    for i in range(2 * cores):
        lse_ref[i : i + 1, :] = lse[:, i * half : (i + 1) * half]


def pack_kernel(lse_ref, a_ref, b_ref, pack_a_ref, pack_b_ref):
    count, half = lse_ref.shape
    for piece, pack_ref in ((a_ref[0:half, :], pack_a_ref), (b_ref[half:, :], pack_b_ref)):
        pack_ref[0:half, :] = piece
        pack_ref[half:, :] = jnp.zeros_like(pack_ref[half:, :])
        pack_ref[half : half + count, 0:half] = lse_ref[...]


def weigh(twice, norm, x, lse, lanes):
    dots = lax.dot_general(twice, x, NT, preferred_element_type=jnp.float32)
    score = dots - widen(norm, x.shape[0])
    resp = jnp.exp(score - lse).astype(jnp.bfloat16)
    part = lax.dot_general(resp, x, NN, preferred_element_type=jnp.float32)
    wide = resp.astype(jnp.float32)
    counted = functools.reduce(
        jnp.add, [wide[:, k : k + lanes] for k in range(0, x.shape[0], lanes)]
    )
    return part, counted


def two_rows(ref, at, half):
    return jnp.concatenate([ref[pl.ds(at, 1), :][:, 0:half], ref[pl.ds(at + 1, 1), :][:, 0:half]], axis=1)


def own_kernel(cores, points_ref, twice_ref, norm_ref, lse_ref, acc_ref, cnt_ref):
    half = points_ref.shape[0] // (2 * cores)
    for i in range(cores):
        x = points_ref[2 * i * half : 2 * (i + 1) * half, :]
        lse = two_rows(lse_ref, 2 * i, half)
        part, counted = weigh(twice_ref[...], norm_ref[...], x, lse, cnt_ref.shape[1])
        if i == 0:
            acc_ref[...] = part
            cnt_ref[...] = counted
        else:
            acc_ref[...] += part
            cnt_ref[...] += counted


def near_rows(cores, half, core, refs, d0_ref, d1_ref):
    for kind in range(2):
        for rc in range(cores):
            tail_ref = d1_ref if (kind + rc) % 2 == 0 else d0_ref
            at = half + 2 * (core ^ rc)
            yield (lambda ref=refs[kind * cores + rc]: ref[...]), (
                lambda at=at, tail_ref=tail_ref: two_rows(tail_ref, at, half)
            )


def far_rows(cores, half, core, refs, lse_ref):
    for rc in range(cores):
        yield (
            lambda rc=rc: jnp.concatenate([refs[rc][0:half, :], refs[cores + rc][0:half, :]], axis=0)
        ), (lambda at=2 * (core ^ rc): two_rows(lse_ref, at, half))


def add_rows(rows, half, twice, norm, acc, cnt):
    for x, lse in rows:
        part, counted = weigh(twice, norm, x().astype(jnp.bfloat16), lse(), cnt.shape[1])
        acc, cnt = acc + part, cnt + counted
    return acc, cnt


def store_sums(out_ref, acc, cnt):
    size, width = acc.shape
    turned = jnp.sum(cnt.T, axis=0, keepdims=True)
    if size < width:
        turned = jnp.concatenate([turned, jnp.zeros((1, width - size), jnp.float32)], axis=1)
    out_ref[0:size, :] = acc
    out_ref[size : size + 8, :] = jnp.broadcast_to(turned, (8, width))


def lead_kernel(cores, order, half, here, twice_ref, norm_ref, acc_ref, cnt_ref, *refs):
    out_acc_ref, out_cnt_ref = refs[-2:]
    near, (d0_ref, d1_ref) = refs[: 2 * cores], refs[2 * cores : 2 * cores + 2]
    size = out_acc_ref.shape[0]
    place = ahead(order, lax.div(here[0], 4), len(order) // 2)
    at = pl.ds(pl.multiple_of(place * size, size), size)
    out_acc_ref[...], out_cnt_ref[...] = add_rows(
        near_rows(cores, half, here[1], near, d0_ref, d1_ref),
        half,
        twice_ref[at, :],
        norm_ref[at, :],
        acc_ref[at, :],
        cnt_ref[at, :],
    )


def block_sums(cores, order, half, steps, here, twice_ref, norm_ref, acc_ref, cnt_ref, lse_ref, near, far, out_ref):
    size = out_ref.shape[0] - 8
    place = ahead(order, lax.div(here[0], 4), steps)
    at = pl.ds(pl.multiple_of(place * size, size), size)
    twice, norm = twice_ref[at, :], norm_ref[at, :]
    acc, cnt = add_rows(
        near_rows(cores, half, here[1], near, far[0], far[cores]),
        half,
        twice,
        norm,
        acc_ref[at, :],
        cnt_ref[at, :],
    )
    acc, cnt = add_rows(far_rows(cores, half, here[1], far, lse_ref), half, twice, norm, acc, cnt)
    store_sums(out_ref, acc, cnt)


def first_kernel(cores, order, half, here, twice_ref, norm_ref, lse_ref, lead_acc_ref, lead_cnt_ref, *refs):
    far, out_ref = refs[: 2 * cores], refs[2 * cores]
    size = lead_acc_ref.shape[0]
    place = ahead(order, lax.div(here[0], 4), len(order) // 2)
    at = pl.ds(pl.multiple_of(place * size, size), size)
    acc, cnt = add_rows(
        far_rows(cores, half, here[1], far, lse_ref),
        half,
        twice_ref[at, :],
        norm_ref[at, :],
        lead_acc_ref[...],
        lead_cnt_ref[...],
    )
    store_sums(out_ref, acc, cnt)


def rest_kernel(cores, order, half, steps, here, twice_ref, norm_ref, acc_ref, cnt_ref, lse_ref, *refs):
    near, far = refs[: 2 * cores], refs[2 * cores : 4 * cores]
    for s, out_ref in zip(steps, refs[4 * cores :]):
        block_sums(
            cores, order, half, s, here, twice_ref, norm_ref, acc_ref, cnt_ref, lse_ref, near, far, out_ref
        )


def ahead(order, line, steps):
    n = len(order)
    return functools.reduce(
        jnp.add,
        [jnp.where(line == order[p], order[(p + steps) % n], 0) for p in range(n)],
    )


def add_kernel(a_ref, b_ref, out_ref):
    out_ref[...] = a_ref[...] + b_ref[...]


def finish_kernel(here, twice_ref, mine_ref, first_ref, second_ref, out_ref):
    size, width = out_ref.shape[0] - 8, out_ref.shape[1]
    start = pl.multiple_of(lax.div(here[0], 4) * size, size)
    c = 0.5 * twice_ref[pl.ds(start, size), :].astype(jnp.float32)
    total = mine_ref[...] + first_ref[...] + second_ref[...]
    counts = total[size:, :]
    column = counts.T[:size, 0:1]
    out_ref[0:size, :] = (total[:size, :] + prior_mass * c) / (column + prior_mass)
    row = lax.broadcasted_iota(jnp.int32, (8, LANES), 0)
    spread = jnp.zeros((8, LANES), jnp.float32)
    for k in range(size // LANES):
        spread = jnp.where(row == k, counts[:, k * LANES : (k + 1) * LANES], spread)
    out_ref[size:, :] = jnp.concatenate([spread] * (width // LANES), axis=1)


def place_kernel(names, order, later, here, *refs):
    count, lines = len(names), len(order)
    block_refs = refs[:count]
    new_ref, counts_out_ref, counts_ref, sems = refs[-4:]
    size = block_refs[0].shape[0] - 8
    plane, line = lax.rem(here[0], 4), lax.div(here[0], 4)
    each = size // LANES
    odd = lax.rem(here[1], 2)
    bits = (0, 1 + odd, 2 - odd, 3)
    places = [ahead(order, line, steps) * 4 + (plane ^ bits[way]) for way, steps in names]
    copies = []
    for i in range(count):
        at = pl.multiple_of(places[i] * size, size)
        copies.append(
            pltpu.make_async_copy(block_refs[i].at[0:size, :], new_ref.at[pl.ds(at, size), :], sems.at[i])
        )
        copies[-1].start()
    if later:
        counts_ref[...] = refs[count][...]
    for i in range(count):
        for k in range(each):
            counts_ref[pl.ds(places[i] * each + k, 1), :] = block_refs[i][size + k : size + k + 1, 0:LANES]
    copies.append(pltpu.make_async_copy(counts_ref, counts_out_ref, sems.at[count]))
    copies[-1].start()
    for copy in copies:
        copy.wait()


def body(n, cores, points, centroids):
    rows, width = points.shape
    local_cent = centroids.shape[0]
    lines = n // 4
    half = rows // (2 * cores)
    share = local_cent // 4
    size = share // lines
    order = tuple(range(0, lines, 2)) + tuple(range(1, lines, 2))[::-1]

    def exchange(x, kind):
        pairs = [
            (i * cores + c, (i ^ (1 if (kind + c) % 2 == 0 else 2)) * cores + c)
            for i in range(n)
            for c in range(cores)
        ]
        return lax.ppermute(x, ("dp", "cent"), pairs)

    def flip_core(x, bits):
        return lax.ppermute(x, "cent", [(i, i ^ bits) for i in range(cores)])

    def ring(x, way):
        pairs = [(order[p], order[(p + way) % lines]) for p in range(lines)]
        return lax.ppermute(x, "dp", [(4 * a + i, 4 * b + i) for a, b in pairs for i in range(4)])

    def with_siblings(pieces):
        return [a if rc == 0 else flip_core(a, rc) for a in pieces for rc in range(cores)]

    mine = call(open_kernel, f32(2 * half, width), [HERE, VMEM], (points,), "open")
    by_a, by_b = exchange(mine, 0), exchange(mine, 1)

    pair, twice, norm = stats(points, centroids, lines)
    pairs = [pair] + [flip_core(pair, rc) for rc in range(1, cores)]
    lse, log_evidence = call(
        functools.partial(lse_kernel, cores, local_cent * cores),
        (f32(2 * cores, half), f32(rows // LANES, LANES)),
        [VMEM] * cores,
        pairs,
        "lse",
    )
    lanes = min(LANES, half)
    acc, cnt = call(
        functools.partial(own_kernel, cores),
        (f32(share, width), f32(share, lanes)),
        [VMEM] * 4,
        (points, twice, norm, lse),
        "own",
        flops=4 * share * width * rows,
    )
    lse, acc, cnt, by_a, by_b = lax.optimization_barrier((lse, acc, cnt, by_a, by_b))
    piece = f32(half + max(8, 2 * cores), width)
    pack_a, pack_b = call(pack_kernel, (piece, piece), [VMEM] * 3, (lse, by_a, by_b), "pack")
    d0, d1 = exchange(pack_a, 1), exchange(pack_b, 0)
    lse_d = lax.ppermute(lse, "dp", [(i, i ^ 3) for i in range(n)])
    by_a, by_b, _ = lax.optimization_barrier((by_a, by_b, pack_a))
    near = with_siblings((by_a, by_b))
    near, d0, d1, acc, cnt, lse_d = lax.optimization_barrier((near, d0, d1, acc, cnt, lse_d))
    lead = call(
        functools.partial(lead_kernel, cores, order, half),
        (f32(size, width), f32(size, lanes)),
        [HERE] + [VMEM] * (6 + 2 * cores),
        (twice, norm, acc, cnt, *near, d0, d1),
        "lead",
        flops=4 * size * width * 2 * rows,
    )
    given = (twice, norm, acc, cnt, lse_d)
    far = with_siblings((d0, d1))
    rows_given = (*near, *far)
    block_sum = f32(size + 8, width)
    turn = lines // 2
    forward = list(range(turn - 1, 0, -1))
    backward = [lines - s for s in range(turn - 1, 0, -1)]
    first = call(
        functools.partial(first_kernel, cores, order, half),
        block_sum,
        [HERE] + [VMEM] * (5 + 2 * cores),
        (twice, norm, lse_d, *lead, *far),
        "first",
        flops=4 * size * width * 2 * rows,
    )

    def sums_of(steps):
        made = call(
            functools.partial(rest_kernel, cores, order, half, steps),
            [block_sum] * len(steps),
            [HERE] + [VMEM] * (5 + 4 * cores),
            (*given, *rows_given),
            "rest",
            flops=4 * size * width * 3 * rows * len(steps),
        )
        return dict(zip(steps, made))

    def plus(a, b):
        return call(add_kernel, block_sum, [VMEM] * 2, (a, b), "add")

    sums = {**sums_of(backward), **sums_of(forward + [0])}
    from_ahead = ring(sums[backward[0]], -1)
    for s in backward[1:]:
        from_ahead = ring(plus(sums[s], from_ahead), -1)
    from_behind = ring(first, 1)
    for s in forward:
        from_behind = ring(plus(sums[s], from_behind), 1)
    done = call(
        finish_kernel,
        block_sum,
        [HERE] + [VMEM] * 4,
        (twice, sums[0], from_behind, from_ahead),
        "finish",
    )

    steps = [-s for s in range(1, lines // 2 + 1)] + list(range(1, lines // 2))
    got = {(0, 0): done}
    previous, older, plane_b = (), (done, done), [done]
    for s in [0] + steps:
        x = got[0, s]
        if previous:
            x = lax.optimization_barrier((x, *previous))[0]
        got[1, s], got[2, s] = exchange(x, 0), exchange(x, 1)
        if s == steps[-1]:
            break
        got[3, s] = exchange(got[1, s], 1)
        plane_b.append(got[2, s])
        previous, older = (plane_b[-2 if s == steps[-2] else -1], *older[:1]), (*older[1:], got[3, s])
        ahead_of = steps[([0] + steps).index(s)]
        x = got[0, ahead_of + (1 if ahead_of < 0 else -1)]
        if ahead_of > 0:
            x = lax.optimization_barrier((x, got[0, s]))[0]
        got[0, ahead_of] = ring(x, 1 if ahead_of < 0 else -1)
    before = got[3, steps[-1] - 1] if steps[-1] > 0 else got[3, steps[-1] + 1]
    before = lax.optimization_barrier((before, got[0, steps[-2]]))[0]
    got[3, steps[-1]] = ring(before, -1 if steps[-1] > 0 else 1)
    late = [(1, steps[-1]), (2, steps[-1])]
    middle = [(w, steps[-2]) for w in (1, 2, 3)]
    groups = ([k for k in got if k not in middle + late], middle, late)
    new = counts = None
    for later, names in enumerate(groups):
        args = [got[k] for k in names]
        if later:
            args += [counts, new]
        new, counts = call(
            functools.partial(place_kernel, names, order, later),
            (f32(local_cent, width), f32(local_cent // LANES, LANES)),
            [HERE] + [VMEM] * len(names) + ([VMEM, ANY] if later else []),
            args,
            ("place_early", "place_middle", "place_late")[later],
            out_specs=(ANY, ANY),
            scratch=[
                pltpu.VMEM((local_cent // LANES, LANES), jnp.float32),
                pltpu.SemaphoreType.DMA((len(names) + 1,)),
            ],
            aliases={len(args) - 1: 0} if later else {},
        )
    return new, counts.reshape(-1), log_evidence.reshape(-1)


def solution(mesh):
    n, cores = mesh.shape["dp"], mesh.shape["cent"]
    return jax.shard_map(
        functools.partial(body, n, cores),
        mesh=mesh,
        in_specs=(P("dp", None), P("cent", None)),
        out_specs=(P("cent", None), P("cent"), P("dp")),
        check_vma=False,
    )
```
